32 devices in a mesh: fibre: 8 (over z, x), tm: 4 (over y, core).
Axes of the slice: x: 2, y: 2, z: 4, core: 2. Of those that a mesh axis runs over, the one named last changes fastest.
Arguments:
- record: bfloat16 [128, 131072], P('fibre', 'tm'), may hold values from -6 to 6
- offsets: int32 [128], P('tm'), may hold values from 0 to 1023
- src_idx: int32 [32], P('fibre'), may hold values from 0 to 127, as said below
Outputs:
- correlation: float32 [32, 128, 256], P('tm', 'fibre')
The draws below stay inside these ranges and needn't reach their ends.
Inputs may be any that keep to these rules, and one draw needn't show every extreme that they name: `src_idx`: the 4 entries at positions b * 4 .. (b + 1) * 4 - 1 are distinct channels among b * 16 .. (b + 1) * 16 - 1.
All inputs are finite; a program needn't handle non-finite values.
Results may differ from the reference program's by a relative error of at most 0.012.
Values may be sent and summed in bfloat16 or wider, within the bound.
No kernel may reach another device: no remote copies, remote signals or barrier semaphores. Data moves between devices by JAX's collectives and lax.ppermute only.
A program may use at most 128 MiB of HBM per device.

```python
import math
import jax
import jax.numpy as jnp
from jax import lax

W = 2048
HOP = 1024
NB = 384
B0 = 20
SMOOTH = 64
LAGS = 256
SRC_DEV = 4
C_DEV = 16
NWIN = 32
SRC = 32
CH = 128
TWIN = 128
TSAMP = 131072
N_FIBRE = 8
N_TM = 4


def draw_src_idx(key, part):
    block_keys = jax.random.split(jax.random.fold_in(key, 17), N_FIBRE)

    def pick_block(block_key):
        return jax.random.permutation(block_key, C_DEV)[:SRC_DEV]
    picked = jax.vmap(pick_block)(block_keys).astype(jnp.int32)
    base = (jnp.arange(N_FIBRE, dtype=jnp.int32) * C_DEV)[:, None]
    return (picked + base).reshape(SRC_DEV * N_FIBRE)


def set_ends(drawn, rng, smallest, largest):
    place = [jax.random.randint(jax.random.fold_in(rng, axis), (), 0, length) for axis, length in enumerate(drawn.shape)]
    longest = drawn.shape.index(max(drawn.shape))
    next_to = place[:longest] + [(place[longest] + 1) % drawn.shape[longest]] + place[longest + 1:]
    return drawn.at[tuple(place)].set(smallest).at[tuple(next_to)].set(largest)


def shard_levels(key, extent, cuts, smallest, largest):
    def one(axis_at, shards_of):
        draws = jax.random.uniform(jax.random.fold_in(jax.random.fold_in(key, 6), axis_at), (shards_of,), jnp.float32, smallest / len(cuts), largest / len(cuts))
        return jnp.repeat(jnp.exp(draws), extent[axis_at] // shards_of).reshape((-1,) + (1,) * (len(extent) - axis_at - 1))

    gain = one(*cuts[0])
    for cut in cuts[1:]:
        gain = gain * one(*cut)
    return gain


def scatter_about(key, extent, scale, reach, cuts=(), held_as=jnp.bfloat16):
    array = scale * jax.random.normal(key, extent, jnp.float32)
    if cuts:
        array = array * shard_levels(key, extent, cuts, -0.22, 0.18)
    return jnp.clip(array, -reach, reach).astype(held_as)


def setup_inputs(seed: int = 0) -> dict:
    keys = jax.random.split(jax.random.key(seed), 4)
    return {
        "record": scatter_about(keys[0], (CH, TSAMP), 1.0, 6.0, ((0, 8), (1, 4))),
        "offsets": set_ends(jax.random.randint(keys[1], (TWIN,), 0, HOP), jax.random.fold_in(keys[1], 1), 0, HOP - 1).astype(jnp.int32),
        "src_idx": draw_src_idx(jax.random.fold_in(keys[3], 71), 0),
    }


def forward_table():
    samples = jnp.arange(W, dtype=jnp.int32)
    freqs = B0 + jnp.arange(NB, dtype=jnp.int32)
    turns = (samples[:, None] * freqs[None, :] % W).astype(jnp.float32) * (2.0 * math.pi / W)
    taper = 0.5 - 0.5 * jnp.cos(samples.astype(jnp.float32) * (2.0 * math.pi / W))
    return jnp.concatenate([taper[:, None] * jnp.cos(turns), -taper[:, None] * jnp.sin(turns)], axis=1).astype(jnp.bfloat16)

def smoothing():
    rows = jnp.arange(NB, dtype=jnp.int32)[:, None]
    cols = jnp.arange(NB, dtype=jnp.int32)[None, :]
    first = jnp.clip(cols - SMOOTH // 2, 0, NB - SMOOTH)
    inside = (rows >= first) & (rows < first + SMOOTH)
    return jnp.where(inside, 1.0 / SMOOTH, 0.0).astype(jnp.float32)

def lag_table():
    freqs = B0 + jnp.arange(NB, dtype=jnp.int32)
    shifts = jnp.arange(LAGS, dtype=jnp.int32) - LAGS // 2
    turns = (freqs[:, None] * shifts[None, :] % W).astype(jnp.float32) * (2.0 * math.pi / W)
    return jnp.concatenate([jnp.cos(turns), -jnp.sin(turns)], axis=0).astype(jnp.bfloat16)

def whiten(spectra, smooth_mat):
    real = spectra[..., :NB]
    imag = spectra[..., NB:]
    power = real * real + imag * imag
    smoothed = jnp.dot(power.reshape(-1, NB), smooth_mat, precision=lax.Precision.HIGHEST).reshape(power.shape)
    factor = 1.0 / jnp.sqrt(smoothed + 1e-05)
    return jnp.concatenate([real * factor, imag * factor], axis=-1).astype(jnp.bfloat16)

def round_half(values):
    return lax.optimization_barrier(values.astype(jnp.bfloat16)).astype(jnp.float32)

def reference(record, offsets, src_idx):
    ftab = forward_table().astype(jnp.float32)
    smooth_mat = smoothing()
    ltab = lag_table().astype(jnp.float32)
    padded = jnp.concatenate([record, jnp.zeros((CH, W), jnp.bfloat16)], axis=1)
    starts = jnp.arange(TWIN, dtype=jnp.int32) * HOP + offsets
    factor = 1.0 / math.sqrt(TWIN * NB)
    block = math.gcd(SRC, 32)
    total = jnp.zeros((SRC, CH, LAGS), jnp.float32)

    def cut_window(first):
        return lax.dynamic_slice_in_dim(padded, first, W, 1)
    for group in range(N_TM):
        chosen = starts[group * NWIN:(group + 1) * NWIN]
        segments = jax.vmap(cut_window, out_axes=1)(chosen)
        spectra = jnp.dot(segments.reshape(-1, W).astype(jnp.float32), ftab, precision=lax.Precision.HIGHEST).reshape(CH, NWIN, 2 * NB)
        whitened = whiten(spectra, smooth_mat)
        sources = jnp.take(whitened, src_idx, axis=0)
        receivers = whitened.astype(jnp.float32)
        rec_real = receivers[..., :NB]
        rec_imag = receivers[..., NB:]

        def one_block(src_block):
            src_full = src_block.astype(jnp.float32)
            src_real = src_full[..., :NB]
            src_imag = src_full[..., NB:]
            hp = lax.Precision.HIGHEST
            real = jnp.einsum('swf,cwf->scf', src_real, rec_real, precision=hp) + jnp.einsum('swf,cwf->scf', src_imag, rec_imag, precision=hp)
            imag = jnp.einsum('swf,cwf->scf', src_real, rec_imag, precision=hp) - jnp.einsum('swf,cwf->scf', src_imag, rec_real, precision=hp)
            cross = round_half(jnp.concatenate([real, imag], axis=-1))
            lagged = jnp.dot(cross.reshape(-1, 2 * NB), ltab, precision=hp) * factor
            return round_half(lagged).reshape(block, CH, LAGS)
        part = lax.map(one_block, sources.reshape(SRC // block, block, NWIN, 2 * NB)).reshape(SRC, CH, LAGS)
        total = total + part
    return total
```

```python
import functools
import math

import jax
import jax.numpy as jnp
import numpy as np
from jax import lax
from jax.experimental import pallas as pl
from jax.experimental.pallas import tpu as pltpu
from jax.sharding import PartitionSpec as P

W = 2048
HOP = 1024
NB = 384
B0 = 20
SMOOTH = 64
LAGS = 256
LANE = 128
CUT = W + LANE


def forward_table():
    samples = np.arange(W, dtype=np.int64)
    freqs = B0 + np.arange(NB, dtype=np.int64)
    turns = (samples[:, None] * freqs[None, :] % W) * (2.0 * math.pi / W)
    taper = 0.5 - 0.5 * np.cos(samples * (2.0 * math.pi / W))
    table = np.concatenate([taper[:, None] * np.cos(turns), -taper[:, None] * np.sin(turns)], axis=1)
    return table.astype(np.float32).astype(jnp.bfloat16)


def smoothing():
    rows = np.arange(NB)[:, None]
    cols = np.arange(NB)[None, :]
    first = np.clip(cols - SMOOTH // 2, 0, NB - SMOOTH)
    return np.where((rows >= first) & (rows < first + SMOOTH), 1.0 / SMOOTH, 0.0).astype(jnp.bfloat16)


def lag_table():
    freqs = B0 + np.arange(NB, dtype=np.int64)
    shifts = np.arange(LAGS, dtype=np.int64) - LAGS // 2
    turns = (freqs[:, None] * shifts[None, :] % W) * (2.0 * math.pi / W)
    table = np.concatenate([np.cos(turns), -np.sin(turns)], axis=0)
    return table.astype(np.float32).astype(jnp.bfloat16)


def spectra_kernel(first, count, tail_at, n_src, offs, local, *refs):
    if tail_at is None:
        rec, ftab, smooth, out_r, out_s, seg = refs
    else:
        rec, halo, ftab, smooth, out_r, out_s, seg, tail = refs
        body_len = rec.shape[1] - tail_at * HOP
        tail[:, :body_len] = rec[:, tail_at * HOP :]
        tail[:, body_len:] = halo[...]
    c_dev = rec.shape[0]
    lanes = lax.broadcasted_iota(jnp.int32, (c_dev, LANE), 1)

    def cut(source, base, slot):
        start = base + offs[first + slot]
        begin = pl.multiple_of(start // LANE * LANE, LANE)
        rest = start % LANE
        keep = lanes < LANE - rest
        shift = (LANE - rest) % LANE
        chunk = source[:, pl.ds(begin, CUT)].astype(jnp.float32)
        turned = [
            pltpu.roll(chunk[:, i * LANE : (i + 1) * LANE], shift, 1) for i in range(CUT // LANE)
        ]
        row = pl.multiple_of(slot * c_dev, c_dev)
        for i in range(W // LANE):
            seg[pl.ds(row, c_dev), i * LANE : (i + 1) * LANE] = jnp.where(
                keep, turned[i], turned[i + 1]
            ).astype(jnp.bfloat16)

    plain = count if tail_at is None else tail_at - first

    @pl.loop(0, plain)
    def _(slot):
        cut(rec, (first + slot) * HOP, slot)

    for slot in range(plain, count):
        cut(tail, (first + slot - tail_at) * HOP, slot)

    spectra = jnp.dot(seg[...], ftab[...], preferred_element_type=jnp.float32)
    real = spectra[:, :NB]
    imag = spectra[:, NB:]
    power = (real * real + imag * imag).astype(jnp.bfloat16)
    smoothed = jnp.dot(power, smooth[...], preferred_element_type=jnp.float32)
    factor = lax.rsqrt(smoothed + 1e-05)
    out_r[:, :NB] = (real * factor).astype(jnp.bfloat16)
    out_r[:, NB:] = (imag * factor).astype(jnp.bfloat16)
    rows = lax.broadcasted_iota(jnp.int32, (n_src * count, count * c_dev), 0)
    cols = lax.broadcasted_iota(jnp.int32, (n_src * count, count * c_dev), 1)
    wanted = jnp.zeros_like(rows)
    for s in range(n_src):
        wanted = jnp.where(rows // count == s, local[s] + (rows % count) * c_dev, wanted)
    picker = jnp.where(cols == wanted, 1.0, 0.0).astype(jnp.bfloat16)
    out_s[...] = jnp.dot(picker, out_r[...], preferred_element_type=jnp.float32).astype(jnp.bfloat16)


def spectra_call(record, halo, offsets, local, ftab, smooth, first, count):
    c_dev = record.shape[0]
    n_src = local.shape[0]
    n_win = offsets.shape[0]
    tail_at = None if halo is None else n_win - 2
    vmem = pl.BlockSpec(memory_space=pltpu.VMEM)
    smem = pl.BlockSpec(memory_space=pltpu.SMEM)
    arrays = [record] + ([] if halo is None else [halo]) + [ftab, smooth]
    scratch = [pltpu.VMEM((count * c_dev, W), jnp.bfloat16)]
    if halo is not None:
        scratch.append(pltpu.VMEM((c_dev, 2 * HOP + W), jnp.bfloat16))
    return pl.pallas_call(
        functools.partial(spectra_kernel, first, count, tail_at, n_src),
        out_shape=(
            jax.ShapeDtypeStruct((count * c_dev, 2 * NB), jnp.bfloat16),
            jax.ShapeDtypeStruct((n_src * count, 2 * NB), jnp.bfloat16),
        ),
        in_specs=[smem, smem] + [vmem] * len(arrays),
        out_specs=(vmem, vmem),
        scratch_shapes=scratch,
        compiler_params=pltpu.CompilerParams(vmem_limit_bytes=48 << 20),
        cost_estimate=pl.CostEstimate(
            flops=2 * count * c_dev * W * 2 * NB, bytes_accessed=6 << 20, transcendentals=0
        ),
        name="spectra",
    )(offsets, local, *arrays)


def cross_kernel(n_list, n_rec, n_src, count, c_dev, final, scale, *refs):
    srcs, refs = refs[:n_list], refs[n_list:]
    recs, refs = refs[:n_rec], refs[n_rec:]
    if final:
        before, ltab, out, wide, cross = refs
    else:
        out, wide = refs
    for k in range(n_list):
        wide[k * n_src * count : (k + 1) * n_src * count, :] = srcs[k][0].astype(jnp.float32)
    block = 8 if n_list * n_src % 8 == 0 else n_src
    tiles = NB // LANE

    @pl.loop(0, n_list * n_src // block * tiles)
    def _(step):
        at = step // tiles * block
        lo = pl.ds(pl.multiple_of(step % tiles * LANE, LANE), LANE)
        hi = pl.ds(pl.multiple_of(step % tiles * LANE + NB, LANE), LANE)
        src_row = pl.multiple_of(at * count, block * count)
        src = wide.at[pl.ds(src_row, block * count)]
        for q in range(n_rec):
            rows = [
                pl.ds(pl.multiple_of(((at + s) * n_rec + q) * c_dev, c_dev), c_dev) for s in range(block)
            ]
            sums = []
            for s in range(block):
                if final:
                    sums.append([before[rows[s], lo], before[rows[s], hi]])
                else:
                    sums.append([0.0, 0.0])
            for w in range(count):
                row = slice(w * c_dev, (w + 1) * c_dev)
                rec_real = recs[q][row, lo].astype(jnp.float32)
                rec_imag = recs[q][row, hi].astype(jnp.float32)
                for s in range(block):
                    src_real = src[s * count + w : s * count + w + 1, lo]
                    src_imag = src[s * count + w : s * count + w + 1, hi]
                    sums[s][0] += src_real * rec_real + src_imag * rec_imag
                    sums[s][1] += src_real * rec_imag - src_imag * rec_real
            for s in range(block):
                if final:
                    cross[rows[s], lo] = sums[s][0].astype(jnp.bfloat16)
                    cross[rows[s], hi] = sums[s][1].astype(jnp.bfloat16)
                else:
                    out[rows[s], lo] = sums[s][0]
                    out[rows[s], hi] = sums[s][1]

    if final:
        lagged = jnp.dot(cross[...], ltab[...], preferred_element_type=jnp.float32)
        out[...] = (lagged * scale).astype(jnp.bfloat16)


def cross_call(srcs, recs, before, ltab, n_src, count, c_dev, scale):
    n_list, n_rec = len(srcs), len(recs)
    groups = srcs[0].shape[0]
    final = before is not None
    rows = n_list * n_src * n_rec * c_dev
    whole = pl.BlockSpec(memory_space=pltpu.VMEM)
    src_spec = pl.BlockSpec((1,) + srcs[0].shape[1:], lambda g: (g, 0, 0))
    scratch = [pltpu.VMEM((n_list * n_src * count, 2 * NB), jnp.float32)]
    if final:
        scratch.append(pltpu.VMEM((rows, 2 * NB), jnp.bfloat16))
        out_shape = jax.ShapeDtypeStruct((groups * rows, LAGS), jnp.bfloat16)
    else:
        out_shape = jax.ShapeDtypeStruct((groups * rows, 2 * NB), jnp.float32)
    row_block = lambda width: pl.BlockSpec((rows, width), lambda g: (g, 0))
    return pl.pallas_call(
        functools.partial(cross_kernel, n_list, n_rec, n_src, count, c_dev, final, scale),
        grid=(groups,),
        out_shape=out_shape,
        in_specs=[src_spec] * n_list + [whole] * n_rec + ([row_block(2 * NB), whole] if final else []),
        out_specs=row_block(out_shape.shape[1]),
        scratch_shapes=scratch,
        compiler_params=pltpu.CompilerParams(vmem_limit_bytes=48 << 20),
        cost_estimate=pl.CostEstimate(
            flops=groups * rows * count * NB * 40, bytes_accessed=4 << 20, transcendentals=0
        ),
        name="cross",
    )(*srcs, *recs, *([before, ltab] if final else []))


def body(record, offsets, src_idx):
    c_dev = record.shape[0]
    n_win = offsets.shape[0]
    n_src = src_idx.shape[0]
    n_tm = lax.axis_size("tm")
    n_fibre = lax.axis_size("fibre")
    n_group = n_fibre // 2
    fibre = lax.axis_index("fibre")
    tm = lax.axis_index("tm")
    half = n_win // 2
    scale = 1.0 / math.sqrt(n_win * n_tm * NB)
    ftab = jnp.asarray(forward_table())
    smooth = jnp.asarray(smoothing())
    ltab = jnp.asarray(lag_table())
    swap = [(i, i ^ 1) for i in range(n_fibre)]
    direct = n_group == 4 and n_tm == 4

    halo = lax.ppermute(record[:, :W], "tm", [(i, i - 1) for i in range(1, n_tm)])
    local = src_idx - fibre * c_dev
    parts = []
    for first, edge in ((0, None), (half, halo)):
        rec, src = spectra_call(record, edge, offsets, local, ftab, smooth, first, half)
        other = lax.ppermute(rec, "fibre", swap)
        if direct:
            srcs = [src[None]] + [
                lax.ppermute(src, "fibre", [(i, i ^ (2 * k)) for i in range(n_fibre)])[None]
                for k in range(1, n_group)
            ]
        else:
            ranks = [[2 * j + p for j in range(n_group)] for p in range(2)]
            srcs = [lax.all_gather(src, "fibre", axis=0, axis_index_groups=ranks)]
        parts.append((srcs, [rec, other]))
    before = cross_call(*parts[0], None, None, n_src, half, c_dev, scale)
    lagged = cross_call(*parts[1], before, ltab, n_src, half, c_dev, scale)
    lagged = lagged.reshape(n_group, n_src, 2, c_dev, LAGS)

    def piece(owner, side):
        if direct:
            return lax.dynamic_index_in_dim(lagged[:, :, side], (fibre // 2) ^ owner, 0, keepdims=True)
        share = n_group // n_tm
        return lax.dynamic_slice_in_dim(lagged[:, :, side], owner * share, share, 0)

    totals = []
    for side in range(2):
        total = None
        for k in range(n_tm):
            mine = piece(tm ^ k, side)
            if side or k:
                pairs = [
                    (i * n_tm + t, (i ^ side) * n_tm + (t ^ k)) for i in range(n_fibre) for t in range(n_tm)
                ]
                mine = lax.ppermute(mine, ("fibre", "tm"), pairs)
            mine = mine.astype(jnp.float32)
            total = mine if total is None else total + mine
        totals.append(total)
    even = fibre % 2 == 0
    near, far = totals
    out = jnp.stack([jnp.where(even, near, far), jnp.where(even, far, near)], axis=1)
    return out.reshape(-1, c_dev, LAGS)


def solution(mesh):
    return jax.shard_map(
        body,
        mesh=mesh,
        in_specs=(P("fibre", "tm"), P("tm"), P("fibre")),
        out_specs=P("tm", "fibre", None),
        check_vma=False,
    )
```

```python
import functools
import math

import jax
import jax.numpy as jnp
import numpy as np
from jax import lax
from jax.experimental import pallas as pl
from jax.experimental.pallas import tpu as pltpu
from jax.sharding import PartitionSpec as P

W = 2048
HOP = 1024
NB = 384
B0 = 20
SMOOTH = 64
LAGS = 256
LANE = 128
CUT = W + LANE
FOLD = W // 2
BINS = np.concatenate(
    [np.arange(0, 256, 2), np.arange(1, 256, 2), np.arange(256, NB, 2), np.arange(257, NB, 2)]
)


def taper_table():
    return (0.5 - 0.5 * np.cos(np.arange(W) * (2.0 * math.pi / W))).astype(np.float32)[None, :]


def half_tables():
    samples = np.arange(FOLD, dtype=np.int64)[:, None]

    def waves(bins):
        turns = (samples * (B0 + bins)[None, :] % W) * (2.0 * math.pi / W)
        return np.cos(turns), -np.sin(turns)

    even_cos, even_sin = waves(np.arange(0, NB, 2))
    odd_cos, odd_sin = waves(np.arange(1, NB, 2))
    cut = LANE
    columns = [
        even_cos[:, :cut], even_sin[:, :cut], even_cos[:, cut:], even_sin[:, cut:],
        odd_cos[:, :cut], odd_sin[:, :cut], odd_sin[:, cut:], odd_cos[:, cut:],
    ]
    return np.concatenate(columns, axis=1).astype(np.float32).astype(jnp.bfloat16)


def smoothing():
    rows = BINS[:, None]
    cols = BINS[None, :]
    first = np.clip(cols - SMOOTH // 2, 0, NB - SMOOTH)
    return np.where((rows >= first) & (rows < first + SMOOTH), 1.0 / SMOOTH, 0.0).astype(jnp.bfloat16)


def lag_table():
    shifts = np.arange(LAGS, dtype=np.int64) - LAGS // 2
    turns = ((B0 + BINS)[:, None] * shifts[None, :] % W) * (2.0 * math.pi / W)
    table = np.concatenate([np.cos(turns), -np.sin(turns)], axis=0)
    return table.astype(np.float32).astype(jnp.bfloat16)


def spectra_kernel(first, count, edge, c_dev, n_src, *refs):
    offs, sources, rec, *refs = refs
    if edge:
        halo, table, taper, smooth, out_r, out_s, *refs = refs
    else:
        table, taper, smooth, out_r, out_s, out_h, *refs = refs
    sums, diffs, held, table_v, taper_v, smooth_v, offs_v, sources_v, sems = refs
    begin = first * HOP
    width = (count + 2) * HOP
    copies = []

    def fetch(source, target):
        copy = pltpu.make_async_copy(source, target, sems.at[len(copies)])
        copy.start()
        copies.append(copy)

    fetch(offs, offs_v)
    fetch(sources, sources_v)
    fetch(taper, taper_v)
    inside = width - (W if edge else 0)
    step = inside // 2
    for at in range(0, inside, step):
        fetch(rec.at[:, pl.ds(begin + at, step)], held.at[:, pl.ds(at, step)])
    if edge:
        fetch(halo, held.at[:, pl.ds(inside, W)])
    else:
        fetch(rec.at[:, pl.ds(0, W)], out_h)
    ready = len(copies)
    rows = FOLD // 4
    for at in range(0, FOLD, rows):
        fetch(table.at[pl.ds(at, rows)], table_v.at[pl.ds(at, rows)])
    fetch(smooth, smooth_v)
    for copy in copies[:ready]:
        copy.wait()

    lanes = lax.broadcasted_iota(jnp.int32, (c_dev, LANE), 1)

    def cut(slot):
        start = slot * HOP + offs_v[first + slot]
        rest = start % LANE
        keep = lanes < LANE - rest
        shift = (LANE - rest) % LANE
        chunk = held[:, pl.ds(pl.multiple_of(start // LANE * LANE, LANE), CUT)].astype(jnp.float32)
        turned = [pltpu.roll(chunk[:, i * LANE : (i + 1) * LANE], shift, 1) for i in range(CUT // LANE)]
        row = pl.ds(pl.multiple_of(slot * c_dev, c_dev), c_dev)
        tiles = FOLD // LANE
        for i in range(tiles):
            lo = slice(i * LANE, (i + 1) * LANE)
            hi = slice(FOLD + i * LANE, FOLD + (i + 1) * LANE)
            near = jnp.where(keep, turned[i], turned[i + 1]) * taper_v[:, lo]
            far = jnp.where(keep, turned[tiles + i], turned[tiles + i + 1]) * taper_v[:, hi]
            sums[row, lo] = (near + far).astype(jnp.bfloat16)
            diffs[row, lo] = (near - far).astype(jnp.bfloat16)

    pl.loop(0, count, unroll=4)(cut)
    for copy in copies[ready:]:
        copy.wait()

    split = 3 * LANE
    even = jnp.dot(sums[...], table_v[:, :split], preferred_element_type=jnp.float32)
    odd = jnp.dot(diffs[...], table_v[:, split:], preferred_element_type=jnp.float32)
    left = lax.broadcasted_iota(jnp.int32, (1, LANE), 1) < LANE // 2
    mixed_even, mixed_odd = even[:, 2 * LANE :], odd[:, 2 * LANE :]
    real = [even[:, :LANE], odd[:, :LANE], jnp.where(left, mixed_even, mixed_odd)]
    swapped = pltpu.roll(jnp.where(left, mixed_odd, mixed_even), LANE // 2, 1)
    imag = [even[:, LANE : 2 * LANE], odd[:, LANE : 2 * LANE], swapped]
    power = jnp.concatenate([r * r + i * i for r, i in zip(real, imag)], axis=1).astype(jnp.bfloat16)
    smoothed = jnp.dot(power, smooth_v[...], preferred_element_type=jnp.float32)
    factor = lax.rsqrt(smoothed + 1e-05)
    for i in range(NB // LANE):
        lo = slice(i * LANE, (i + 1) * LANE)
        hi = slice(NB + i * LANE, NB + (i + 1) * LANE)
        out_r[:, lo] = (real[i] * factor[:, lo]).astype(jnp.bfloat16)
        out_r[:, hi] = (imag[i] * factor[:, lo]).astype(jnp.bfloat16)
    rows = lax.broadcasted_iota(jnp.int32, (n_src * count, 1), 0)
    cols = lax.broadcasted_iota(jnp.int32, (n_src * count, count * c_dev), 1)
    wanted = jnp.zeros_like(rows)
    for s in range(n_src):
        wanted = jnp.where(rows // count == s, sources_v[s] % c_dev + (rows % count) * c_dev, wanted)
    picker = jnp.where(cols == wanted, 1.0, 0.0).astype(jnp.bfloat16)
    out_s[...] = jnp.dot(picker, out_r[...], preferred_element_type=jnp.float32).astype(jnp.bfloat16)


def spectra_call(record, halo, offsets, src_idx, tables, first, count):
    c_dev = record.shape[0]
    n_src = src_idx.shape[0]
    edge = halo is not None
    vmem = pl.BlockSpec(memory_space=pltpu.VMEM)
    hbm = pl.BlockSpec(memory_space=pl.ANY)
    arrays = [offsets, src_idx, record] + ([halo] if edge else []) + list(tables)
    out_shape = [
        jax.ShapeDtypeStruct((count * c_dev, 2 * NB), jnp.bfloat16),
        jax.ShapeDtypeStruct((n_src * count, 2 * NB), jnp.bfloat16),
    ]
    if not edge:
        out_shape.append(jax.ShapeDtypeStruct((c_dev, W), jnp.bfloat16))
    return pl.pallas_call(
        functools.partial(spectra_kernel, first, count, edge, c_dev, n_src),
        out_shape=out_shape,
        in_specs=[hbm] * len(arrays),
        out_specs=[vmem] * len(out_shape),
        scratch_shapes=[
            pltpu.VMEM((count * c_dev, FOLD), jnp.bfloat16),
            pltpu.VMEM((count * c_dev, FOLD), jnp.bfloat16),
            pltpu.VMEM((c_dev, (count + 2) * HOP), jnp.bfloat16),
            pltpu.VMEM((FOLD, 2 * NB), jnp.bfloat16),
            pltpu.VMEM((1, W), jnp.float32),
            pltpu.VMEM((NB, NB), jnp.bfloat16),
            pltpu.SMEM(offsets.shape, jnp.int32),
            pltpu.SMEM(src_idx.shape, jnp.int32),
            pltpu.SemaphoreType.DMA((16,)),
        ],
        compiler_params=pltpu.CompilerParams(vmem_limit_bytes=32 << 20),
        cost_estimate=pl.CostEstimate(
            flops=2 * count * c_dev * W * 2 * NB, bytes_accessed=6 << 20, transcendentals=0
        ),
        name="spectra",
    )(*arrays)


def cross_kernel(n_list, n_rec, n_src, count, c_dev, final, scale, *refs):
    srcs, refs = refs[:n_list], refs[n_list:]
    recs, refs = refs[:n_rec], refs[n_rec:]
    if final:
        before, ltab, out, wide, cross = refs
    else:
        out, wide = refs
    for k in range(n_list):
        wide[k * n_src * count : (k + 1) * n_src * count, :] = srcs[k][0].astype(jnp.float32)
    block = 8 if n_list * n_src % 8 == 0 else n_src
    tiles = NB // LANE

    @pl.loop(0, n_list * n_src // block * tiles)
    def _(step):
        at = step // tiles * block
        lo = pl.ds(pl.multiple_of(step % tiles * LANE, LANE), LANE)
        hi = pl.ds(pl.multiple_of(step % tiles * LANE + NB, LANE), LANE)
        src_row = pl.multiple_of(at * count, block * count)
        src = wide.at[pl.ds(src_row, block * count)]
        for q in range(n_rec):
            rows = [
                pl.ds(pl.multiple_of(((at + s) * n_rec + q) * c_dev, c_dev), c_dev) for s in range(block)
            ]
            sums = []
            for s in range(block):
                if final:
                    sums.append([before[rows[s], lo], before[rows[s], hi]])
                else:
                    sums.append([0.0, 0.0])
            for w in range(count):
                row = slice(w * c_dev, (w + 1) * c_dev)
                rec_real = recs[q][row, lo].astype(jnp.float32)
                rec_imag = recs[q][row, hi].astype(jnp.float32)
                for s in range(block):
                    src_real = src[s * count + w : s * count + w + 1, lo]
                    src_imag = src[s * count + w : s * count + w + 1, hi]
                    sums[s][0] += src_real * rec_real + src_imag * rec_imag
                    sums[s][1] += src_real * rec_imag - src_imag * rec_real
            for s in range(block):
                if final:
                    cross[rows[s], lo] = sums[s][0].astype(jnp.bfloat16)
                    cross[rows[s], hi] = sums[s][1].astype(jnp.bfloat16)
                else:
                    out[rows[s], lo] = sums[s][0]
                    out[rows[s], hi] = sums[s][1]

    if final:
        lagged = jnp.dot(cross[...], ltab[...], preferred_element_type=jnp.float32)
        out[...] = (lagged * scale).astype(jnp.bfloat16)


def cross_call(srcs, recs, before, ltab, n_src, count, c_dev, scale):
    n_list, n_rec = len(srcs), len(recs)
    groups = srcs[0].shape[0]
    final = before is not None
    rows = n_list * n_src * n_rec * c_dev
    whole = pl.BlockSpec(memory_space=pltpu.VMEM)
    src_spec = pl.BlockSpec((1,) + srcs[0].shape[1:], lambda g: (g, 0, 0))
    scratch = [pltpu.VMEM((n_list * n_src * count, 2 * NB), jnp.float32)]
    if final:
        scratch.append(pltpu.VMEM((rows, 2 * NB), jnp.bfloat16))
        out_shape = jax.ShapeDtypeStruct((groups * rows, LAGS), jnp.bfloat16)
    else:
        out_shape = jax.ShapeDtypeStruct((groups * rows, 2 * NB), jnp.float32)
    row_block = lambda width: pl.BlockSpec((rows, width), lambda g: (g, 0))
    return pl.pallas_call(
        functools.partial(cross_kernel, n_list, n_rec, n_src, count, c_dev, final, scale),
        grid=(groups,),
        out_shape=out_shape,
        in_specs=[src_spec] * n_list + [whole] * n_rec + ([row_block(2 * NB), whole] if final else []),
        out_specs=row_block(out_shape.shape[1]),
        scratch_shapes=scratch,
        compiler_params=pltpu.CompilerParams(vmem_limit_bytes=48 << 20),
        cost_estimate=pl.CostEstimate(
            flops=groups * rows * count * NB * 40, bytes_accessed=4 << 20, transcendentals=0
        ),
        name="cross",
    )(*srcs, *recs, *([before, ltab] if final else []))


def body(record, offsets, src_idx):
    c_dev = record.shape[0]
    n_win = offsets.shape[0]
    n_src = src_idx.shape[0]
    n_tm = lax.axis_size("tm")
    n_fibre = lax.axis_size("fibre")
    n_group = n_fibre // 2
    fibre = lax.axis_index("fibre")
    tm = lax.axis_index("tm")
    early = n_win * 3 // 4
    scale = 1.0 / math.sqrt(n_win * n_tm * NB)
    tables = [jnp.asarray(t) for t in (half_tables(), taper_table(), smoothing())]
    ltab = jnp.asarray(lag_table())
    swap = [(i, i ^ 1) for i in range(n_fibre)]
    direct = n_group == 4 and n_tm == 4

    def spread(rec, src):
        other = lax.ppermute(rec, "fibre", swap)
        if direct:
            srcs = [src[None]] + [
                lax.ppermute(src, "fibre", [(i, i ^ (2 * k)) for i in range(n_fibre)])[None]
                for k in range(1, n_group)
            ]
        else:
            ranks = [[2 * j + p for j in range(n_group)] for p in range(2)]
            srcs = [lax.all_gather(src, "fibre", axis=0, axis_index_groups=ranks)]
        return srcs, [rec, other]

    rec, src, edge = spectra_call(record, None, offsets, src_idx, tables, 0, early)
    halo = lax.ppermute(edge, "tm", [(i, i - 1) for i in range(1, n_tm)])
    first = spread(rec, src)
    late = n_win - early
    second = spread(*spectra_call(record, halo, offsets, src_idx, tables, early, late))
    before = cross_call(*first, None, None, n_src, early, c_dev, scale)
    lagged = cross_call(*second, before, ltab, n_src, late, c_dev, scale)
    lagged = lagged.reshape(n_group, n_src, 2, c_dev, LAGS)

    def piece(owner, side):
        if direct:
            return lax.dynamic_index_in_dim(lagged[:, :, side], (fibre // 2) ^ owner, 0, keepdims=True)
        share = n_group // n_tm
        return lax.dynamic_slice_in_dim(lagged[:, :, side], owner * share, share, 0)

    totals = []
    for side in range(2):
        total = None
        for k in range(n_tm):
            mine = piece(tm ^ k, side)
            if side or k:
                pairs = [
                    (i * n_tm + t, (i ^ side) * n_tm + (t ^ k)) for i in range(n_fibre) for t in range(n_tm)
                ]
                mine = lax.ppermute(mine, ("fibre", "tm"), pairs)
            mine = mine.astype(jnp.float32)
            total = mine if total is None else total + mine
        totals.append(total)
    even = fibre % 2 == 0
    near, far = totals
    out = jnp.stack([jnp.where(even, near, far), jnp.where(even, far, near)], axis=1)
    return out.reshape(-1, c_dev, LAGS)


def solution(mesh):
    return jax.shard_map(
        body,
        mesh=mesh,
        in_specs=(P("fibre", "tm"), P("tm"), P("fibre")),
        out_specs=P("tm", "fibre", None),
        check_vma=False,
    )
```

```python
import functools
import math

import jax
import jax.numpy as jnp
import numpy as np
from jax import lax
from jax.experimental import pallas as pl
from jax.experimental.pallas import tpu as pltpu
from jax.sharding import PartitionSpec as P

W = 2048
HOP = 1024
NB = 384
B0 = 20
SMOOTH = 64
LAGS = 256
LANE = 128
CUT = W + LANE
FOLD = W // 2
BINS = np.concatenate(
    [np.arange(0, 256, 2), np.arange(1, 256, 2), np.arange(256, NB, 2), np.arange(257, NB, 2)]
)


def taper_table():
    return (0.5 - 0.5 * np.cos(np.arange(W) * (2.0 * math.pi / W))).astype(np.float32)[None, :]


def half_tables():
    samples = np.arange(FOLD, dtype=np.int64)[:, None]

    def waves(bins):
        turns = (samples * (B0 + bins)[None, :] % W) * (2.0 * math.pi / W)
        return np.cos(turns), -np.sin(turns)

    even_cos, even_sin = waves(np.arange(0, NB, 2))
    odd_cos, odd_sin = waves(np.arange(1, NB, 2))
    cut = LANE
    columns = [
        even_cos[:, :cut], even_sin[:, :cut], even_cos[:, cut:], even_sin[:, cut:],
        odd_cos[:, :cut], odd_sin[:, :cut], odd_sin[:, cut:], odd_cos[:, cut:],
    ]
    return np.concatenate(columns, axis=1).astype(np.float32).astype(jnp.bfloat16)


def smoothing():
    rows = BINS[:, None]
    cols = BINS[None, :]
    first = np.clip(cols - SMOOTH // 2, 0, NB - SMOOTH)
    return np.where((rows >= first) & (rows < first + SMOOTH), 1.0 / SMOOTH, 0.0).astype(jnp.bfloat16)


def lag_table():
    shifts = np.arange(LAGS, dtype=np.int64) - LAGS // 2
    turns = ((B0 + BINS)[:, None] * shifts[None, :] % W) * (2.0 * math.pi / W)
    table = np.concatenate([np.cos(turns), -np.sin(turns)], axis=0)
    return table.astype(np.float32).astype(jnp.bfloat16)


def spectra_kernel(first, count, late, c_dev, n_src, *refs):
    if late:
        offs, sources, rec, halo, table_v, taper_v, smooth_v, before_s, out_r, out_s, *refs = refs
        sums, diffs, held, offs_v, sources_v, sems = refs
    else:
        offs, sources, rec, table, taper, smooth, out_r, out_s, table_v, taper_v, smooth_v, *refs = refs
        sums, diffs, held, offs_v, sources_v, sems = refs
    begin = first * HOP
    width = (count + 2) * HOP
    copies = []

    def fetch(source, target):
        copy = pltpu.make_async_copy(source, target, sems.at[len(copies)])
        copy.start()
        copies.append(copy)

    fetch(offs, offs_v)
    fetch(sources, sources_v)
    inside = width - (W if late else 0)
    step = inside // 2
    if not late:
        fetch(taper, taper_v)
    for at in range(0, inside, step):
        fetch(rec.at[:, pl.ds(begin + at, step)], held.at[:, pl.ds(at, step)])
    ready = len(copies)
    if late:
        held[:, inside:] = halo[...]
    else:
        rows = FOLD // 4
        for at in range(0, FOLD, rows):
            fetch(table.at[pl.ds(at, rows)], table_v.at[pl.ds(at, rows)])
        fetch(smooth, smooth_v)
    for copy in copies[:ready]:
        copy.wait()

    lanes = lax.broadcasted_iota(jnp.int32, (c_dev, LANE), 1)

    def cut(slot):
        start = slot * HOP + offs_v[first + slot]
        rest = start % LANE
        keep = lanes < LANE - rest
        shift = (LANE - rest) % LANE
        chunk = held[:, pl.ds(pl.multiple_of(start // LANE * LANE, LANE), CUT)].astype(jnp.float32)
        turned = [pltpu.roll(chunk[:, i * LANE : (i + 1) * LANE], shift, 1) for i in range(CUT // LANE)]
        row = pl.ds(pl.multiple_of(slot * c_dev, c_dev), c_dev)
        tiles = FOLD // LANE
        for i in range(tiles):
            lo = slice(i * LANE, (i + 1) * LANE)
            hi = slice(FOLD + i * LANE, FOLD + (i + 1) * LANE)
            near = jnp.where(keep, turned[i], turned[i + 1]) * taper_v[:, lo]
            far = jnp.where(keep, turned[tiles + i], turned[tiles + i + 1]) * taper_v[:, hi]
            sums[row, lo] = (near + far).astype(jnp.bfloat16)
            diffs[row, lo] = (near - far).astype(jnp.bfloat16)

    pl.loop(0, count, unroll=4)(cut)
    for copy in copies[ready:]:
        copy.wait()

    split = 3 * LANE
    even = jnp.dot(sums[...], table_v[:, :split], preferred_element_type=jnp.float32)
    odd = jnp.dot(diffs[...], table_v[:, split:], preferred_element_type=jnp.float32)
    left = lax.broadcasted_iota(jnp.int32, (1, LANE), 1) < LANE // 2
    mixed_even, mixed_odd = even[:, 2 * LANE :], odd[:, 2 * LANE :]
    real = [even[:, :LANE], odd[:, :LANE], jnp.where(left, mixed_even, mixed_odd)]
    swapped = pltpu.roll(jnp.where(left, mixed_odd, mixed_even), LANE // 2, 1)
    imag = [even[:, LANE : 2 * LANE], odd[:, LANE : 2 * LANE], swapped]
    power = jnp.concatenate([r * r + i * i for r, i in zip(real, imag)], axis=1).astype(jnp.bfloat16)
    smoothed = jnp.dot(power, smooth_v[...], preferred_element_type=jnp.float32)
    factor = lax.rsqrt(smoothed + 1e-05)
    for i in range(NB // LANE):
        lo = slice(i * LANE, (i + 1) * LANE)
        hi = slice(NB + i * LANE, NB + (i + 1) * LANE)
        out_r[:, lo] = (real[i] * factor[:, lo]).astype(jnp.bfloat16)
        out_r[:, hi] = (imag[i] * factor[:, lo]).astype(jnp.bfloat16)
    rows = lax.broadcasted_iota(jnp.int32, (n_src * count, 1), 0)
    cols = lax.broadcasted_iota(jnp.int32, (n_src * count, count * c_dev), 1)
    wanted = jnp.zeros_like(rows)
    for s in range(n_src):
        wanted = jnp.where(rows // count == s, sources_v[s] % c_dev + (rows % count) * c_dev, wanted)
    picker = jnp.where(cols == wanted, 1.0, 0.0).astype(jnp.bfloat16)
    at = 0
    if late:
        at = before_s.shape[0]
        out_s[:at] = before_s[...]
    out_s[at:] = jnp.dot(picker, out_r[...], preferred_element_type=jnp.float32).astype(jnp.bfloat16)


def spectra_call(record, offsets, src_idx, tables, first, count, late=None):
    c_dev = record.shape[0]
    n_src = src_idx.shape[0]
    vmem = pl.BlockSpec(memory_space=pltpu.VMEM)
    hbm = pl.BlockSpec(memory_space=pltpu.HBM)
    arrays = [offsets, src_idx, record]
    specs = [hbm] * 3
    out_rows = n_src * count
    if late is None:
        arrays += tables
        specs += [hbm] * 3
    else:
        halo, earlier = late
        arrays += [halo, *tables, earlier]
        specs += [vmem] * 5
        out_rows += earlier.shape[0]
    out_shape = [
        jax.ShapeDtypeStruct((count * c_dev, 2 * NB), jnp.bfloat16),
        jax.ShapeDtypeStruct((out_rows, 2 * NB), jnp.bfloat16),
    ]
    if late is None:
        out_shape += [jax.ShapeDtypeStruct(t.shape, t.dtype) for t in tables]
    return pl.pallas_call(
        functools.partial(spectra_kernel, first, count, late is not None, c_dev, n_src),
        out_shape=out_shape,
        in_specs=specs,
        out_specs=[vmem] * len(out_shape),
        scratch_shapes=[
            pltpu.VMEM((count * c_dev, FOLD), jnp.bfloat16),
            pltpu.VMEM((count * c_dev, FOLD), jnp.bfloat16),
            pltpu.VMEM((c_dev, (count + 2) * HOP), jnp.bfloat16),
            pltpu.SMEM(offsets.shape, jnp.int32),
            pltpu.SMEM(src_idx.shape, jnp.int32),
            pltpu.SemaphoreType.DMA((16,)),
        ],
        compiler_params=pltpu.CompilerParams(vmem_limit_bytes=24 << 20),
        cost_estimate=pl.CostEstimate(
            flops=2 * count * c_dev * W * 2 * NB, bytes_accessed=4 << 20, transcendentals=0
        ),
        name="spectra",
    )(*arrays)


def cross_kernel(n_list, sides, cuts, n_src, c_dev, scale, has_before, last, *refs):
    srcs, refs = refs[:n_list], refs[n_list:]
    recs = []
    for parts in sides:
        recs.append([(refs[i], part) for i, part in enumerate(parts)])
        refs = refs[len(parts) :]
    if has_before:
        before, *refs = refs
    if last:
        ltab, out, wide, cross = refs
    else:
        out, wide = refs
    n_win = cuts[-1]
    for k in range(n_list):
        wide[k * n_src * n_win : (k + 1) * n_src * n_win, :] = srcs[k][0].astype(jnp.float32)
    tiles = NB // LANE
    block = 8 if n_list * n_src % 8 == 0 else n_src
    groups = block // n_src
    n_side = len(sides)

    @pl.loop(0, n_list // groups * tiles)
    def _(step):
        group = step // tiles * groups
        lo = pl.ds(pl.multiple_of(step % tiles * LANE, LANE), LANE)
        hi = pl.ds(pl.multiple_of(step % tiles * LANE + NB, LANE), LANE)
        base = pl.multiple_of(group * (n_src * n_win), 8)
        src = wide.at[pl.ds(base, groups * n_src * n_win)]
        for q, parts in enumerate(recs):
            rows = [
                pl.ds(pl.multiple_of(((group * n_src + s) * n_side + q) * c_dev, c_dev), c_dev)
                for s in range(block)
            ]
            sums = [[before[r, lo], before[r, hi]] if has_before else [0.0, 0.0] for r in rows]
            for rec, part in parts:
                start, stop = cuts[part], cuts[part + 1]
                for w in range(stop - start):
                    row = slice(w * c_dev, (w + 1) * c_dev)
                    rec_real = rec[row, lo].astype(jnp.float32)
                    rec_imag = rec[row, hi].astype(jnp.float32)
                    for s in range(block):
                        at = s // n_src * n_src * n_win
                        at += start * n_src + s % n_src * (stop - start) + w
                        src_real = src[at : at + 1, lo]
                        src_imag = src[at : at + 1, hi]
                        sums[s][0] += src_real * rec_real + src_imag * rec_imag
                        sums[s][1] += src_real * rec_imag - src_imag * rec_real
            target = cross if last else out
            for s in range(block):
                for i, place in enumerate((lo, hi)):
                    target[rows[s], place] = (sums[s][i] + jnp.zeros((c_dev, LANE), jnp.float32)).astype(
                        target.dtype
                    )

    if last:
        lagged = jnp.dot(cross[...], ltab[...], preferred_element_type=jnp.float32)
        out[...] = (lagged * scale).astype(jnp.bfloat16)


def cross_call(srcs, sides, cuts, n_src, c_dev, scale, before=None, ltab=None):
    n_list, n_side = len(srcs), len(sides)
    groups = srcs[0].shape[0]
    last = ltab is not None
    rows = n_list * n_src * n_side * c_dev
    whole = pl.BlockSpec(memory_space=pltpu.VMEM)
    src_spec = pl.BlockSpec((1,) + srcs[0].shape[1:], lambda g: (g, 0, 0))
    row_block = lambda width: pl.BlockSpec((rows, width), lambda g: (g, 0))
    arrays, specs = list(srcs), [src_spec] * n_list
    for parts in sides:
        arrays += list(parts.values())
        specs += [whole] * len(parts)
    if before is not None:
        arrays.append(before)
        specs.append(row_block(2 * NB))
    scratch = [pltpu.VMEM((n_list * n_src * cuts[-1], 2 * NB), jnp.float32)]
    if last:
        arrays.append(ltab)
        specs.append(whole)
        scratch.append(pltpu.VMEM((rows, 2 * NB), jnp.bfloat16))
        out_shape = jax.ShapeDtypeStruct((groups * rows, LAGS), jnp.bfloat16)
    else:
        out_shape = jax.ShapeDtypeStruct((groups * rows, 2 * NB), jnp.float32)
    windows = sum(cuts[p + 1] - cuts[p] for parts in sides for p in parts) // n_side
    return pl.pallas_call(
        functools.partial(
            cross_kernel, n_list, [list(p) for p in sides], cuts, n_src, c_dev, scale,
            before is not None, last,
        ),
        grid=(groups,),
        out_shape=out_shape,
        in_specs=specs,
        out_specs=row_block(out_shape.shape[1]),
        scratch_shapes=scratch,
        compiler_params=pltpu.CompilerParams(vmem_limit_bytes=24 << 20),
        cost_estimate=pl.CostEstimate(
            flops=groups * rows * windows * NB * 40, bytes_accessed=4 << 20, transcendentals=0
        ),
        name="cross",
    )(*arrays)


def body(record, offsets, src_idx):
    c_dev = record.shape[0]
    n_win = offsets.shape[0]
    n_src = src_idx.shape[0]
    n_tm = lax.axis_size("tm")
    n_fibre = lax.axis_size("fibre")
    n_group = n_fibre // 2
    fibre = lax.axis_index("fibre")
    tm = lax.axis_index("tm")
    early = n_win * 5 // 8
    cuts = (0, early, n_win)
    scale = 1.0 / math.sqrt(n_win * n_tm * NB)
    tables = [jnp.asarray(t) for t in (half_tables(), taper_table(), smoothing())]
    ltab = jnp.asarray(lag_table())
    direct = n_group == 4 and n_tm == 4

    def trade(array, by):
        return lax.ppermute(array, "fibre", [(i, i ^ by) for i in range(n_fibre)])

    halo = lax.ppermute(record[:, :W], "tm", [(i, i - 1) for i in range(1, n_tm)])
    rec_a, src_a, *tables = spectra_call(record, offsets, src_idx, tables, 0, early)
    far_a = trade(rec_a, 1)
    rec_b, src = spectra_call(record, offsets, src_idx, tables, early, n_win - early, (halo, src_a))
    cross = functools.partial(cross_call, cuts=cuts, n_src=n_src, c_dev=c_dev, scale=scale)
    if direct:
        by_2 = trade(src, 4)
        by_1 = trade(src, 2)
        far_b = trade(rec_b, 1)
        by_3 = trade(by_2, 2)
        srcs = [s[None] for s in (src, by_1, by_2, by_3)]
        part = cross(srcs[:3], [{0: rec_a, 1: rec_b}, {0: far_a}])
        near = cross(srcs[:3], [{}, {1: far_b}], before=part, ltab=ltab)
        last = cross(srcs[3:], [{0: rec_a, 1: rec_b}, {0: far_a, 1: far_b}], ltab=ltab)
        lagged = jnp.concatenate([near, last], axis=0)
    else:
        ranks = [[2 * j + p for j in range(n_group)] for p in range(2)]
        srcs = [lax.all_gather(src, "fibre", axis=0, axis_index_groups=ranks)]
        far_b = trade(rec_b, 1)
        lagged = cross(srcs, [{0: rec_a, 1: rec_b}, {0: far_a, 1: far_b}], ltab=ltab)
    lagged = lagged.reshape(n_group, n_src, 2, c_dev, LAGS)

    def piece(owner, side):
        if direct:
            return lax.dynamic_index_in_dim(lagged[:, :, side], (fibre // 2) ^ owner, 0, keepdims=True)
        share = n_group // n_tm
        return lax.dynamic_slice_in_dim(lagged[:, :, side], owner * share, share, 0)

    totals = []
    for side in range(2):
        total = None
        for k in range(n_tm):
            mine = piece(tm ^ k, side)
            if side or k:
                pairs = [
                    (i * n_tm + t, (i ^ side) * n_tm + (t ^ k)) for i in range(n_fibre) for t in range(n_tm)
                ]
                mine = lax.ppermute(mine, ("fibre", "tm"), pairs)
            mine = mine.astype(jnp.float32)
            total = mine if total is None else total + mine
        totals.append(total)
    even = fibre % 2 == 0
    near, far = totals
    out = jnp.stack([jnp.where(even, near, far), jnp.where(even, far, near)], axis=1)
    return out.reshape(-1, c_dev, LAGS)


def solution(mesh):
    return jax.shard_map(
        body,
        mesh=mesh,
        in_specs=(P("fibre", "tm"), P("tm"), P("fibre")),
        out_specs=P("tm", "fibre", None),
        check_vma=False,
    )
```

```python
import functools
import math

import jax
import jax.numpy as jnp
import numpy as np
from jax import lax
from jax.experimental import pallas as pl
from jax.experimental.pallas import tpu as pltpu
from jax.sharding import PartitionSpec as P

W = 2048
HOP = 1024
NB = 384
B0 = 20
SMOOTH = 64
LAGS = 256
LANE = 128
CUT = W + LANE
FOLD = W // 2
BINS = np.concatenate(
    [np.arange(0, 256, 2), np.arange(1, 256, 2), np.arange(256, NB, 2), np.arange(257, NB, 2)]
)


def taper_table():
    return (0.5 - 0.5 * np.cos(np.arange(W) * (2.0 * math.pi / W))).astype(np.float32)[None, :]


def half_tables():
    samples = np.arange(FOLD, dtype=np.int64)[:, None]

    def waves(bins):
        turns = (samples * (B0 + bins)[None, :] % W) * (2.0 * math.pi / W)
        return np.cos(turns), -np.sin(turns)

    even_cos, even_sin = waves(np.arange(0, NB, 2))
    odd_cos, odd_sin = waves(np.arange(1, NB, 2))
    cut = LANE
    columns = [
        even_cos[:, :cut], even_sin[:, :cut], even_cos[:, cut:], even_sin[:, cut:],
        odd_cos[:, :cut], odd_sin[:, :cut], odd_sin[:, cut:], odd_cos[:, cut:],
    ]
    return np.concatenate(columns, axis=1).astype(np.float32).astype(jnp.bfloat16)


def smoothing():
    rows = BINS[:, None]
    cols = BINS[None, :]
    first = np.clip(cols - SMOOTH // 2, 0, NB - SMOOTH)
    return np.where((rows >= first) & (rows < first + SMOOTH), 1.0 / SMOOTH, 0.0).astype(jnp.bfloat16)


def lag_table():
    shifts = np.arange(LAGS, dtype=np.int64) - LAGS // 2
    turns = ((B0 + BINS)[:, None] * shifts[None, :] % W) * (2.0 * math.pi / W)
    table = np.concatenate([np.cos(turns), -np.sin(turns)], axis=0)
    return table.astype(np.float32).astype(jnp.bfloat16)


def spectra_kernel(first, count, late, c_dev, n_src, *refs):
    if late:
        offs, sources, rec, halo, table_v, taper_v, smooth_v, before_s, out_r, out_s, out_all, *refs = refs
        sums, diffs, held, offs_v, sources_v, sems = refs
    else:
        offs, sources, rec, table, taper, smooth, out_r, out_s, table_v, taper_v, smooth_v, *refs = refs
        sums, diffs, held, offs_v, sources_v, sems = refs
    begin = first * HOP
    width = (count + 2) * HOP
    copies = []

    def fetch(source, target):
        copy = pltpu.make_async_copy(source, target, sems.at[len(copies)])
        copy.start()
        copies.append(copy)

    fetch(offs, offs_v)
    fetch(sources, sources_v)
    inside = width - (W if late else 0)
    step = inside // 2
    if not late:
        fetch(taper, taper_v)
    for at in range(0, inside, step):
        fetch(rec.at[:, pl.ds(begin + at, step)], held.at[:, pl.ds(at, step)])
    ready = len(copies)
    if late:
        held[:, inside:] = halo[...]
    else:
        rows = FOLD // 4
        for at in range(0, FOLD, rows):
            fetch(table.at[pl.ds(at, rows)], table_v.at[pl.ds(at, rows)])
        fetch(smooth, smooth_v)
    for copy in copies[:ready]:
        copy.wait()

    lanes = lax.broadcasted_iota(jnp.int32, (c_dev, LANE), 1)

    def cut(slot):
        start = slot * HOP + offs_v[first + slot]
        rest = start % LANE
        keep = lanes < LANE - rest
        shift = (LANE - rest) % LANE
        chunk = held[:, pl.ds(pl.multiple_of(start // LANE * LANE, LANE), CUT)].astype(jnp.float32)
        turned = [pltpu.roll(chunk[:, i * LANE : (i + 1) * LANE], shift, 1) for i in range(CUT // LANE)]
        row = pl.ds(pl.multiple_of(slot * c_dev, c_dev), c_dev)
        tiles = FOLD // LANE
        for i in range(tiles):
            lo = slice(i * LANE, (i + 1) * LANE)
            hi = slice(FOLD + i * LANE, FOLD + (i + 1) * LANE)
            near = jnp.where(keep, turned[i], turned[i + 1]) * taper_v[:, lo]
            far = jnp.where(keep, turned[tiles + i], turned[tiles + i + 1]) * taper_v[:, hi]
            sums[row, lo] = (near + far).astype(jnp.bfloat16)
            diffs[row, lo] = (near - far).astype(jnp.bfloat16)

    pl.loop(0, count, unroll=4)(cut)
    for copy in copies[ready:]:
        copy.wait()

    split = 3 * LANE
    even = jnp.dot(sums[...], table_v[:, :split], preferred_element_type=jnp.float32)
    odd = jnp.dot(diffs[...], table_v[:, split:], preferred_element_type=jnp.float32)
    left = lax.broadcasted_iota(jnp.int32, (1, LANE), 1) < LANE // 2
    mixed_even, mixed_odd = even[:, 2 * LANE :], odd[:, 2 * LANE :]
    real = [even[:, :LANE], odd[:, :LANE], jnp.where(left, mixed_even, mixed_odd)]
    swapped = pltpu.roll(jnp.where(left, mixed_odd, mixed_even), LANE // 2, 1)
    imag = [even[:, LANE : 2 * LANE], odd[:, LANE : 2 * LANE], swapped]
    power = jnp.concatenate([r * r + i * i for r, i in zip(real, imag)], axis=1).astype(jnp.bfloat16)
    smoothed = jnp.dot(power, smooth_v[...], preferred_element_type=jnp.float32)
    factor = lax.rsqrt(smoothed + 1e-05)
    for i in range(NB // LANE):
        lo = slice(i * LANE, (i + 1) * LANE)
        hi = slice(NB + i * LANE, NB + (i + 1) * LANE)
        out_r[:, lo] = (real[i] * factor[:, lo]).astype(jnp.bfloat16)
        out_r[:, hi] = (imag[i] * factor[:, lo]).astype(jnp.bfloat16)
    rows = lax.broadcasted_iota(jnp.int32, (n_src * count, 1), 0)
    cols = lax.broadcasted_iota(jnp.int32, (n_src * count, count * c_dev), 1)
    wanted = jnp.zeros_like(rows)
    for s in range(n_src):
        wanted = jnp.where(rows // count == s, sources_v[s] % c_dev + (rows % count) * c_dev, wanted)
    picker = jnp.where(cols == wanted, 1.0, 0.0).astype(jnp.bfloat16)
    out_s[...] = jnp.dot(picker, out_r[...], preferred_element_type=jnp.float32).astype(jnp.bfloat16)
    if late:
        at = before_s.shape[0]
        out_all[:at] = before_s[...]
        out_all[at:] = out_s[...]


def spectra_call(record, offsets, src_idx, tables, first, count, late=None):
    c_dev = record.shape[0]
    n_src = src_idx.shape[0]
    vmem = pl.BlockSpec(memory_space=pltpu.VMEM)
    hbm = pl.BlockSpec(memory_space=pltpu.HBM)
    arrays = [offsets, src_idx, record]
    if late is None:
        arrays += tables
    arrays = [pltpu.with_memory_space_constraint(a, pltpu.HBM) for a in arrays]
    specs = [hbm] * len(arrays)
    out_shape = [
        jax.ShapeDtypeStruct((count * c_dev, 2 * NB), jnp.bfloat16),
        jax.ShapeDtypeStruct((n_src * count, 2 * NB), jnp.bfloat16),
    ]
    if late is None:
        out_shape += [jax.ShapeDtypeStruct(t.shape, t.dtype) for t in tables]
    else:
        halo, earlier = late
        arrays += [halo, *tables, earlier]
        specs += [vmem] * 5
        out_shape.append(jax.ShapeDtypeStruct((earlier.shape[0] + n_src * count, 2 * NB), jnp.bfloat16))
    return pl.pallas_call(
        functools.partial(spectra_kernel, first, count, late is not None, c_dev, n_src),
        out_shape=out_shape,
        in_specs=specs,
        out_specs=[vmem] * len(out_shape),
        scratch_shapes=[
            pltpu.VMEM((count * c_dev, FOLD), jnp.bfloat16),
            pltpu.VMEM((count * c_dev, FOLD), jnp.bfloat16),
            pltpu.VMEM((c_dev, (count + 2) * HOP), jnp.bfloat16),
            pltpu.SMEM(offsets.shape, jnp.int32),
            pltpu.SMEM(src_idx.shape, jnp.int32),
            pltpu.SemaphoreType.DMA((16,)),
        ],
        compiler_params=pltpu.CompilerParams(vmem_limit_bytes=24 << 20),
        cost_estimate=pl.CostEstimate(
            flops=2 * count * c_dev * W * 2 * NB, bytes_accessed=4 << 20, transcendentals=0
        ),
        name="spectra",
    )(*arrays)


def cross_kernel(shares, sides, cuts, n_src, c_dev, scale, n_before, last, *refs):
    n_list = len(shares)
    srcs = []
    for share in shares:
        srcs.append(refs[:share])
        refs = refs[share:]
    recs = []
    for parts in sides:
        recs.append([(refs[i], part) for i, part in enumerate(parts)])
        refs = refs[len(parts) :]
    before, refs = refs[:n_before], refs[n_before:]
    if last:
        ltab, out, wide, cross = refs
    else:
        out, wide = refs
    n_win = cuts[-1]
    at = 0
    for src in srcs:
        for part in src:
            height = part.shape[1]
            wide[at : at + height, :] = part[0].astype(jnp.float32)
            at += height
    tiles = NB // LANE
    block = 8 if n_list * n_src % 8 == 0 else n_src
    groups = block // n_src
    n_side = len(sides)

    span = n_list // max(len(before), 1)

    def run(step, first, earlier):
        local = step // tiles * groups
        group = first + local
        lo = pl.ds(pl.multiple_of(step % tiles * LANE, LANE), LANE)
        hi = pl.ds(pl.multiple_of(step % tiles * LANE + NB, LANE), LANE)
        base = pl.multiple_of(group * (n_src * n_win), 8)
        src = wide.at[pl.ds(base, groups * n_src * n_win)]

        def places(group, q):
            starts = [((group * n_src + s) * n_side + q) * c_dev for s in range(block)]
            return [pl.ds(pl.multiple_of(start, c_dev), c_dev) for start in starts]

        for q, parts in enumerate(recs):
            sums = [[0.0, 0.0] for _ in range(block)]
            if earlier is not None:
                sums = [[earlier[r, lo], earlier[r, hi]] for r in places(local, q)]
            for rec, part in parts:
                start, stop = cuts[part], cuts[part + 1]
                for w in range(stop - start):
                    row = slice(w * c_dev, (w + 1) * c_dev)
                    rec_real = rec[row, lo].astype(jnp.float32)
                    rec_imag = rec[row, hi].astype(jnp.float32)
                    for s in range(block):
                        at = s // n_src * n_src * n_win
                        at += start * n_src + s % n_src * (stop - start) + w
                        src_real = src[at : at + 1, lo]
                        src_imag = src[at : at + 1, hi]
                        sums[s][0] += src_real * rec_real + src_imag * rec_imag
                        sums[s][1] += src_real * rec_imag - src_imag * rec_real
            target = cross if last else out
            for r, pair in zip(places(group, q), sums):
                for place, value in zip((lo, hi), pair):
                    target[r, place] = jnp.broadcast_to(value, (c_dev, LANE)).astype(target.dtype)

    for i in range(max(len(before), 1)):
        earlier = before[i] if before else None
        pl.loop(0, span // groups * tiles)(functools.partial(run, first=i * span, earlier=earlier))

    if last:
        lagged = jnp.dot(cross[...], ltab[...], preferred_element_type=jnp.float32)
        out[...] = (lagged * scale).astype(jnp.bfloat16)


def cross_call(srcs, sides, cuts, n_src, c_dev, scale, before=None, ltab=None):
    n_list, n_side = len(srcs), len(sides)
    groups = srcs[0][0].shape[0]
    last = ltab is not None
    rows = n_list * n_src * n_side * c_dev
    whole = pl.BlockSpec(memory_space=pltpu.VMEM)
    row_block = lambda width: pl.BlockSpec((rows, width), lambda g: (g, 0))
    arrays = [part for src in srcs for part in src]
    specs = [pl.BlockSpec((1,) + a.shape[1:], lambda g: (g, 0, 0)) for a in arrays]
    for parts in sides:
        arrays += list(parts.values())
        specs += [whole] * len(parts)
    if before is not None:
        arrays += before
        specs += [whole] * len(before)
    scratch = [pltpu.VMEM((n_list * n_src * cuts[-1], 2 * NB), jnp.float32)]
    if last:
        arrays.append(ltab)
        specs.append(whole)
        scratch.append(pltpu.VMEM((rows, 2 * NB), jnp.bfloat16))
        out_shape = jax.ShapeDtypeStruct((groups * rows, LAGS), jnp.bfloat16)
    else:
        out_shape = jax.ShapeDtypeStruct((groups * rows, 2 * NB), jnp.float32)
    windows = sum(cuts[p + 1] - cuts[p] for parts in sides for p in parts) // n_side
    return pl.pallas_call(
        functools.partial(
            cross_kernel, [len(src) for src in srcs], [list(p) for p in sides], cuts, n_src, c_dev, scale,
            0 if before is None else len(before), last,
        ),
        grid=(groups,),
        out_shape=out_shape,
        in_specs=specs,
        out_specs=row_block(out_shape.shape[1]),
        scratch_shapes=scratch,
        compiler_params=pltpu.CompilerParams(vmem_limit_bytes=24 << 20),
        cost_estimate=pl.CostEstimate(
            flops=groups * rows * windows * NB * 40, bytes_accessed=4 << 20, transcendentals=0
        ),
        name="cross",
    )(*arrays)


def body(record, offsets, src_idx):
    c_dev = record.shape[0]
    n_win = offsets.shape[0]
    n_src = src_idx.shape[0]
    n_tm = lax.axis_size("tm")
    n_fibre = lax.axis_size("fibre")
    n_group = n_fibre // 2
    fibre = lax.axis_index("fibre")
    tm = lax.axis_index("tm")
    early = n_win * 3 // 4
    cuts = (0, early, n_win)
    scale = 1.0 / math.sqrt(n_win * n_tm * NB)
    tables = [jnp.asarray(t) for t in (half_tables(), taper_table(), smoothing())]
    ltab = jnp.asarray(lag_table())
    direct = n_group == 4 and n_tm == 4

    def trade(array, by):
        return lax.ppermute(array, "fibre", [(i, i ^ by) for i in range(n_fibre)])

    halo = lax.ppermute(record[:, :W], "tm", [(i, i - 1) for i in range(1, n_tm)])
    rec_a, src_a, *tables = spectra_call(record, offsets, src_idx, tables, 0, early)
    far_a = trade(rec_a, 1)
    if direct:
        by_2a = trade(src_a, 4)
    rec_b, src_b, src = spectra_call(record, offsets, src_idx, tables, early, n_win - early, (halo, src_a))
    cross = functools.partial(cross_call, cuts=cuts, n_src=n_src, c_dev=c_dev, scale=scale)
    if direct:
        far_b = trade(rec_b, 1)
        by_2b = trade(src_b, 4)
        by_1 = trade(src, 2)
        by_3a = trade(by_2a, 2)
        by_3b = trade(by_2b, 2)
        srcs = [[part[None] for part in s] for s in ([src], [by_1], [by_2a, by_2b], [by_3a, by_3b])]
        sides = [{0: rec_a, 1: rec_b}, {0: far_a}]
        parts = [cross(srcs[:2], sides), cross(srcs[2:], sides)]
        lagged = cross(srcs, [{}, {1: far_b}], before=parts, ltab=ltab)
    else:
        ranks = [[2 * j + p for j in range(n_group)] for p in range(2)]
        srcs = [[lax.all_gather(src, "fibre", axis=0, axis_index_groups=ranks)]]
        far_b = trade(rec_b, 1)
        lagged = cross(srcs, [{0: rec_a, 1: rec_b}, {0: far_a, 1: far_b}], ltab=ltab)
    lagged = lagged.reshape(n_group, n_src, 2, c_dev, LAGS)

    def piece(owner):
        if direct:
            return lax.dynamic_index_in_dim(lagged, (fibre // 2) ^ owner, 0, keepdims=True)
        share = n_group // n_tm
        return lax.dynamic_slice_in_dim(lagged, owner * share, share, 0)

    keep = jnp.stack([piece(tm ^ k) for k in range(0, n_tm, 2)])
    give = jnp.stack([piece(tm ^ k) for k in range(1, n_tm, 2)])
    got = lax.ppermute(give, "tm", [(i, i ^ 1) for i in range(n_tm)])
    pairs = keep.astype(jnp.float32) + got.astype(jnp.float32)
    totals = []
    for side in range(2):
        total = None
        for k in range(n_tm // 2):
            mine = pairs[k, :, :, side]
            if side or k:
                routes = [
                    (i * n_tm + t, (i ^ side) * n_tm + (t ^ (2 * k)))
                    for i in range(n_fibre)
                    for t in range(n_tm)
                ]
                mine = lax.ppermute(mine.astype(jnp.bfloat16), ("fibre", "tm"), routes)
                mine = mine.astype(jnp.float32)
            total = mine if total is None else total + mine
        totals.append(total)
    even = fibre % 2 == 0
    near, far = totals
    out = jnp.stack([jnp.where(even, near, far), jnp.where(even, far, near)], axis=1)
    return out.reshape(-1, c_dev, LAGS)


def solution(mesh):
    return jax.shard_map(
        body,
        mesh=mesh,
        in_specs=(P("fibre", "tm"), P("tm"), P("fibre")),
        out_specs=P("tm", "fibre", None),
        check_vma=False,
    )
```

```python
import functools
import math

import jax
import jax.numpy as jnp
import numpy as np
from jax import lax
from jax.experimental import pallas as pl
from jax.experimental.pallas import tpu as pltpu
from jax.sharding import PartitionSpec as P

W = 2048
HOP = 1024
NB = 384
B0 = 20
SMOOTH = 64
LAGS = 256
LANE = 128
CUT = W + LANE
FOLD = W // 2
BINS = np.concatenate(
    [np.arange(0, 256, 2), np.arange(1, 256, 2), np.arange(256, NB, 2), np.arange(257, NB, 2)]
)


def taper_table():
    return (0.5 - 0.5 * np.cos(np.arange(W) * (2.0 * math.pi / W))).astype(np.float32)[None, :]


def half_tables():
    samples = np.arange(FOLD, dtype=np.int64)[:, None]

    def waves(bins):
        turns = (samples * (B0 + bins)[None, :] % W) * (2.0 * math.pi / W)
        return np.cos(turns), -np.sin(turns)

    even_cos, even_sin = waves(np.arange(0, NB, 2))
    odd_cos, odd_sin = waves(np.arange(1, NB, 2))
    cut = LANE
    columns = [
        even_cos[:, :cut], even_sin[:, :cut], even_cos[:, cut:], even_sin[:, cut:],
        odd_cos[:, :cut], odd_sin[:, :cut], odd_sin[:, cut:], odd_cos[:, cut:],
    ]
    return np.concatenate(columns, axis=1).astype(np.float32).astype(jnp.bfloat16)


def smoothing():
    rows = BINS[:, None]
    cols = BINS[None, :]
    first = np.clip(cols - SMOOTH // 2, 0, NB - SMOOTH)
    return np.where((rows >= first) & (rows < first + SMOOTH), 1.0 / SMOOTH, 0.0).astype(jnp.bfloat16)


def lag_table():
    shifts = np.arange(LAGS, dtype=np.int64) - LAGS // 2
    turns = ((B0 + BINS)[:, None] * shifts[None, :] % W) * (2.0 * math.pi / W)
    table = np.concatenate([np.cos(turns), -np.sin(turns)], axis=0)
    return table.astype(np.float32).astype(jnp.bfloat16)


def spectra_kernel(first, count, late, c_dev, n_src, *refs):
    if late:
        offs, sources, rec, halo, table_v, taper_v, smooth_v, before_s, out_r, out_s, out_all, *refs = refs
        sums, diffs, held, offs_v, sources_v, sems = refs
    else:
        offs, sources, rec, table, taper, smooth, *refs = refs
        out_r, out_s, out_edge, table_v, taper_v, smooth_v, *refs = refs
        sums, diffs, held, offs_v, sources_v, sems = refs
    begin = first * HOP
    width = (count + 2) * HOP
    copies = []

    def fetch(source, target):
        copy = pltpu.make_async_copy(source, target, sems.at[len(copies)])
        copy.start()
        copies.append(copy)

    fetch(offs, offs_v)
    fetch(sources, sources_v)
    inside = width - (W if late else 0)
    step = inside // 2
    if not late:
        fetch(taper, taper_v)
    for at in range(0, inside, step):
        fetch(rec.at[:, pl.ds(begin + at, step)], held.at[:, pl.ds(at, step)])
    ready = len(copies)
    if late:
        held[:, inside:] = halo[...]
    else:
        rows = FOLD // 4
        for at in range(0, FOLD, rows):
            fetch(table.at[pl.ds(at, rows)], table_v.at[pl.ds(at, rows)])
        fetch(smooth, smooth_v)
        fetch(rec.at[:, pl.ds(0, W)], out_edge)
    for copy in copies[:ready]:
        copy.wait()

    lanes = lax.broadcasted_iota(jnp.int32, (c_dev, LANE), 1)

    def cut(slot):
        start = slot * HOP + offs_v[first + slot]
        rest = start % LANE
        keep = lanes < LANE - rest
        shift = (LANE - rest) % LANE
        chunk = held[:, pl.ds(pl.multiple_of(start // LANE * LANE, LANE), CUT)].astype(jnp.float32)
        turned = [pltpu.roll(chunk[:, i * LANE : (i + 1) * LANE], shift, 1) for i in range(CUT // LANE)]
        row = pl.ds(pl.multiple_of(slot * c_dev, c_dev), c_dev)
        tiles = FOLD // LANE
        for i in range(tiles):
            lo = slice(i * LANE, (i + 1) * LANE)
            hi = slice(FOLD + i * LANE, FOLD + (i + 1) * LANE)
            near = jnp.where(keep, turned[i], turned[i + 1]) * taper_v[:, lo]
            far = jnp.where(keep, turned[tiles + i], turned[tiles + i + 1]) * taper_v[:, hi]
            sums[row, lo] = (near + far).astype(jnp.bfloat16)
            diffs[row, lo] = (near - far).astype(jnp.bfloat16)

    pl.loop(0, count, unroll=4)(cut)
    for copy in copies[ready:]:
        copy.wait()

    split = 3 * LANE
    even = jnp.dot(sums[...], table_v[:, :split], preferred_element_type=jnp.float32)
    odd = jnp.dot(diffs[...], table_v[:, split:], preferred_element_type=jnp.float32)
    left = lax.broadcasted_iota(jnp.int32, (1, LANE), 1) < LANE // 2
    mixed_even, mixed_odd = even[:, 2 * LANE :], odd[:, 2 * LANE :]
    real = [even[:, :LANE], odd[:, :LANE], jnp.where(left, mixed_even, mixed_odd)]
    swapped = pltpu.roll(jnp.where(left, mixed_odd, mixed_even), LANE // 2, 1)
    imag = [even[:, LANE : 2 * LANE], odd[:, LANE : 2 * LANE], swapped]
    power = jnp.concatenate([r * r + i * i for r, i in zip(real, imag)], axis=1).astype(jnp.bfloat16)
    smoothed = jnp.dot(power, smooth_v[...], preferred_element_type=jnp.float32)
    factor = lax.rsqrt(smoothed + 1e-05)
    for i in range(NB // LANE):
        lo = slice(i * LANE, (i + 1) * LANE)
        hi = slice(NB + i * LANE, NB + (i + 1) * LANE)
        out_r[:, lo] = (real[i] * factor[:, lo]).astype(jnp.bfloat16)
        out_r[:, hi] = (imag[i] * factor[:, lo]).astype(jnp.bfloat16)
    rows = lax.broadcasted_iota(jnp.int32, (n_src * count, 1), 0)
    cols = lax.broadcasted_iota(jnp.int32, (n_src * count, count * c_dev), 1)
    wanted = jnp.zeros_like(rows)
    for s in range(n_src):
        wanted = jnp.where(rows // count == s, sources_v[s] % c_dev + (rows % count) * c_dev, wanted)
    picker = jnp.where(cols == wanted, 1.0, 0.0).astype(jnp.bfloat16)
    out_s[...] = jnp.dot(picker, out_r[...], preferred_element_type=jnp.float32).astype(jnp.bfloat16)
    if late:
        at = before_s.shape[0]
        out_all[:at] = before_s[...]
        out_all[at:] = out_s[...]


def spectra_call(record, offsets, src_idx, tables, first, count, late=None):
    c_dev = record.shape[0]
    n_src = src_idx.shape[0]
    vmem = pl.BlockSpec(memory_space=pltpu.VMEM)
    hbm = pl.BlockSpec(memory_space=pltpu.HBM)
    arrays = [offsets, src_idx, record]
    if late is None:
        arrays += tables
    arrays = [pltpu.with_memory_space_constraint(a, pltpu.HBM) for a in arrays]
    specs = [hbm] * len(arrays)
    out_shape = [
        jax.ShapeDtypeStruct((count * c_dev, 2 * NB), jnp.bfloat16),
        jax.ShapeDtypeStruct((n_src * count, 2 * NB), jnp.bfloat16),
    ]
    if late is None:
        out_shape.append(jax.ShapeDtypeStruct((c_dev, W), record.dtype))
        out_shape += [jax.ShapeDtypeStruct(t.shape, t.dtype) for t in tables]
    else:
        halo, earlier = late
        arrays += [halo, *tables, earlier]
        specs += [vmem] * 5
        out_shape.append(jax.ShapeDtypeStruct((earlier.shape[0] + n_src * count, 2 * NB), jnp.bfloat16))
    return pl.pallas_call(
        functools.partial(spectra_kernel, first, count, late is not None, c_dev, n_src),
        out_shape=out_shape,
        in_specs=specs,
        out_specs=[vmem] * len(out_shape),
        scratch_shapes=[
            pltpu.VMEM((count * c_dev, FOLD), jnp.bfloat16),
            pltpu.VMEM((count * c_dev, FOLD), jnp.bfloat16),
            pltpu.VMEM((c_dev, (count + 2) * HOP), jnp.bfloat16),
            pltpu.SMEM(offsets.shape, jnp.int32),
            pltpu.SMEM(src_idx.shape, jnp.int32),
            pltpu.SemaphoreType.DMA((16,)),
        ],
        compiler_params=pltpu.CompilerParams(vmem_limit_bytes=24 << 20),
        cost_estimate=pl.CostEstimate(
            flops=2 * count * c_dev * W * 2 * NB, bytes_accessed=4 << 20, transcendentals=0
        ),
        name="spectra",
    )(*arrays)


def cross_kernel(shares, sides, cuts, n_src, c_dev, scale, n_before, last, *refs):
    n_list = len(shares)
    srcs = []
    for share in shares:
        srcs.append(refs[:share])
        refs = refs[share:]
    recs = []
    for parts in sides:
        recs.append([(refs[i], part) for i, part in enumerate(parts)])
        refs = refs[len(parts) :]
    before, refs = refs[:n_before], refs[n_before:]
    if last:
        ltab, out, wide, cross = refs
    else:
        out, wide = refs
    n_win = cuts[-1]
    at = 0
    for src in srcs:
        for part in src:
            height = part.shape[1]
            wide[at : at + height, :] = part[0].astype(jnp.float32)
            at += height
    tiles = NB // LANE
    block = 8 if n_list * n_src % 8 == 0 else n_src
    groups = block // n_src
    n_side = len(sides)

    span = n_list // max(len(before), 1)

    def run(step, first, earlier):
        local = step // tiles * groups
        group = first + local
        lo = pl.ds(pl.multiple_of(step % tiles * LANE, LANE), LANE)
        hi = pl.ds(pl.multiple_of(step % tiles * LANE + NB, LANE), LANE)
        base = pl.multiple_of(group * (n_src * n_win), 8)
        src = wide.at[pl.ds(base, groups * n_src * n_win)]

        def places(group, q):
            starts = [((group * n_src + s) * n_side + q) * c_dev for s in range(block)]
            return [pl.ds(pl.multiple_of(start, c_dev), c_dev) for start in starts]

        for q, parts in enumerate(recs):
            sums = [[0.0, 0.0] for _ in range(block)]
            if earlier is not None:
                sums = [[earlier[r, lo], earlier[r, hi]] for r in places(local, q)]
            for rec, part in parts:
                start, stop = cuts[part], cuts[part + 1]
                for w in range(stop - start):
                    row = slice(w * c_dev, (w + 1) * c_dev)
                    rec_real = rec[row, lo].astype(jnp.float32)
                    rec_imag = rec[row, hi].astype(jnp.float32)
                    for s in range(block):
                        at = s // n_src * n_src * n_win
                        at += start * n_src + s % n_src * (stop - start) + w
                        src_real = src[at : at + 1, lo]
                        src_imag = src[at : at + 1, hi]
                        sums[s][0] += src_real * rec_real + src_imag * rec_imag
                        sums[s][1] += src_real * rec_imag - src_imag * rec_real
            target = cross if last else out
            for r, pair in zip(places(group, q), sums):
                for place, value in zip((lo, hi), pair):
                    target[r, place] = jnp.broadcast_to(value, (c_dev, LANE)).astype(target.dtype)

    for i in range(max(len(before), 1)):
        earlier = before[i] if before else None
        pl.loop(0, span // groups * tiles)(functools.partial(run, first=i * span, earlier=earlier))

    if last:
        lagged = jnp.dot(cross[...], ltab[...], preferred_element_type=jnp.float32)
        out[...] = (lagged * scale).astype(jnp.bfloat16)


def cross_call(srcs, sides, cuts, n_src, c_dev, scale, before=None, ltab=None):
    n_list, n_side = len(srcs), len(sides)
    groups = srcs[0][0].shape[0]
    last = ltab is not None
    rows = n_list * n_src * n_side * c_dev
    whole = pl.BlockSpec(memory_space=pltpu.VMEM)
    row_block = lambda width: pl.BlockSpec((rows, width), lambda g: (g, 0))
    arrays = [part for src in srcs for part in src]
    specs = [pl.BlockSpec((1,) + a.shape[1:], lambda g: (g, 0, 0)) for a in arrays]
    for parts in sides:
        arrays += list(parts.values())
        specs += [whole] * len(parts)
    if before is not None:
        arrays += before
        specs += [whole] * len(before)
    scratch = [pltpu.VMEM((n_list * n_src * cuts[-1], 2 * NB), jnp.float32)]
    if last:
        arrays.append(ltab)
        specs.append(whole)
        scratch.append(pltpu.VMEM((rows, 2 * NB), jnp.bfloat16))
        out_shape = jax.ShapeDtypeStruct((groups * rows, LAGS), jnp.bfloat16)
    else:
        out_shape = jax.ShapeDtypeStruct((groups * rows, 2 * NB), jnp.float32)
    windows = sum(cuts[p + 1] - cuts[p] for parts in sides for p in parts) // n_side
    return pl.pallas_call(
        functools.partial(
            cross_kernel, [len(src) for src in srcs], [list(p) for p in sides], cuts, n_src, c_dev, scale,
            0 if before is None else len(before), last,
        ),
        grid=(groups,),
        out_shape=out_shape,
        in_specs=specs,
        out_specs=row_block(out_shape.shape[1]),
        scratch_shapes=scratch,
        compiler_params=pltpu.CompilerParams(vmem_limit_bytes=24 << 20),
        cost_estimate=pl.CostEstimate(
            flops=groups * rows * windows * NB * 40, bytes_accessed=4 << 20, transcendentals=0
        ),
        name="cross",
    )(*arrays)


def body(record, offsets, src_idx):
    c_dev = record.shape[0]
    n_win = offsets.shape[0]
    n_src = src_idx.shape[0]
    n_tm = lax.axis_size("tm")
    n_fibre = lax.axis_size("fibre")
    n_group = n_fibre // 2
    fibre = lax.axis_index("fibre")
    tm = lax.axis_index("tm")
    early = n_win * 3 // 4
    cuts = (0, early, n_win)
    scale = 1.0 / math.sqrt(n_win * n_tm * NB)
    tables = [jnp.asarray(t) for t in (half_tables(), taper_table(), smoothing())]
    ltab = jnp.asarray(lag_table())
    direct = n_group == 4 and n_tm == 4

    def trade(array, by):
        return lax.ppermute(array, "fibre", [(i, i ^ by) for i in range(n_fibre)])

    rec_a, src_a, edge, *tables = spectra_call(record, offsets, src_idx, tables, 0, early)
    far_a = trade(rec_a, 1)
    if direct:
        by_2a = trade(src_a, 4)
    halo = lax.ppermute(edge, "tm", [(i, i - 1) for i in range(1, n_tm)])
    rec_b, src_b, src = spectra_call(record, offsets, src_idx, tables, early, n_win - early, (halo, src_a))
    far_b = trade(rec_b, 1)
    cross = functools.partial(cross_call, cuts=cuts, n_src=n_src, c_dev=c_dev, scale=scale)
    own = [{0: rec_a, 1: rec_b}]
    if direct:
        by_2 = jnp.concatenate([by_2a, trade(src_b, 4)], axis=0)
        by_1 = trade(src, 2)
        by_3 = trade(by_2, 2)
        srcs = [[part[None]] for part in (src, by_1, by_2, by_3)]
        halves = (srcs[:2], srcs[2:])
        near = [cross(half, own, ltab=ltab) for half in halves]
        near = jnp.concatenate(near, axis=0)
        parts = [cross(half, [{0: far_a}]) for half in halves]
        far = cross(srcs, [{1: far_b}], before=parts, ltab=ltab)
    else:
        ranks = [[2 * j + p for j in range(n_group)] for p in range(2)]
        srcs = [[lax.all_gather(src, "fibre", axis=0, axis_index_groups=ranks)]]
        near = cross(srcs, own, ltab=ltab)
        far = cross(srcs, [{0: far_a, 1: far_b}], ltab=ltab)
    near, far = (r.reshape(n_group, n_src, c_dev, LAGS) for r in (near, far))

    def piece(lagged, owner):
        if direct:
            return lax.dynamic_index_in_dim(lagged, (fibre // 2) ^ owner, 0, keepdims=True)
        share = n_group // n_tm
        return lax.dynamic_slice_in_dim(lagged, owner * share, share, 0)

    keep = jnp.stack([piece(r, tm ^ k) for r in (near, far) for k in range(0, n_tm, 2)])
    give = jnp.stack([piece(r, tm ^ k) for r in (near, far) for k in range(1, n_tm, 2)])
    got = lax.ppermute(give, "tm", [(i, i ^ 1) for i in range(n_tm)])
    pairs = keep.astype(jnp.float32) + got.astype(jnp.float32)
    totals = []
    for side in range(2):
        total = None
        for k in range(n_tm // 2):
            mine = pairs[side * (n_tm // 2) + k]
            if side or k:
                routes = [
                    (i * n_tm + t, (i ^ side) * n_tm + (t ^ (2 * k)))
                    for i in range(n_fibre)
                    for t in range(n_tm)
                ]
                mine = lax.ppermute(mine.astype(jnp.bfloat16), ("fibre", "tm"), routes)
                mine = mine.astype(jnp.float32)
            total = mine if total is None else total + mine
        totals.append(total)
    even = fibre % 2 == 0
    near, far = totals
    out = jnp.stack([jnp.where(even, near, far), jnp.where(even, far, near)], axis=1)
    return out.reshape(-1, c_dev, LAGS)


def solution(mesh):
    return jax.shard_map(
        body,
        mesh=mesh,
        in_specs=(P("fibre", "tm"), P("tm"), P("fibre")),
        out_specs=P("tm", "fibre", None),
        check_vma=False,
    )
```

```python
import functools
import math

import jax
import jax.numpy as jnp
import numpy as np
from jax import lax
from jax.experimental import pallas as pl
from jax.experimental.pallas import tpu as pltpu
from jax.sharding import PartitionSpec as P

W = 2048
HOP = 1024
NB = 384
B0 = 20
SMOOTH = 64
LAGS = 256
LANE = 128
CUT = W + LANE
FOLD = W // 2
BINS = np.concatenate(
    [np.arange(0, 256, 2), np.arange(1, 256, 2), np.arange(256, NB, 2), np.arange(257, NB, 2)]
)


def taper_table():
    return (0.5 - 0.5 * np.cos(np.arange(W) * (2.0 * math.pi / W))).astype(np.float32)[None, :]


def half_tables():
    samples = np.arange(FOLD, dtype=np.int64)[:, None]

    def waves(bins):
        turns = (samples * (B0 + bins)[None, :] % W) * (2.0 * math.pi / W)
        return np.cos(turns), -np.sin(turns)

    even_cos, even_sin = waves(np.arange(0, NB, 2))
    odd_cos, odd_sin = waves(np.arange(1, NB, 2))
    cut = LANE
    columns = [
        even_cos[:, :cut], even_sin[:, :cut], even_cos[:, cut:], even_sin[:, cut:],
        odd_cos[:, :cut], odd_sin[:, :cut], odd_sin[:, cut:], odd_cos[:, cut:],
    ]
    return np.concatenate(columns, axis=1).astype(np.float32).astype(jnp.bfloat16)


def smoothing():
    rows = BINS[:, None]
    cols = BINS[None, :]
    first = np.clip(cols - SMOOTH // 2, 0, NB - SMOOTH)
    return np.where((rows >= first) & (rows < first + SMOOTH), 1.0 / SMOOTH, 0.0).astype(jnp.bfloat16)


def lag_table():
    shifts = np.arange(LAGS, dtype=np.int64) - LAGS // 2
    turns = ((B0 + BINS)[:, None] * shifts[None, :] % W) * (2.0 * math.pi / W)
    table = np.concatenate([np.cos(turns), -np.sin(turns)], axis=0)
    return table.astype(np.float32).astype(jnp.bfloat16)


def spectra_kernel(first, count, late, c_dev, n_src, *refs):
    if late:
        offs, sources, rest_v, halo, table_v, taper_v, smooth_v, before_s, out_r, out_s, out_all, *refs = refs
        sums, diffs, held, offs_v, sources_v, sems = refs
    else:
        offs, sources, rec, table, taper, smooth, *refs = refs
        out_r, out_s, out_edge, rest_v, table_v, taper_v, smooth_v, *refs = refs
        sums, diffs, held, offs_v, sources_v, sems = refs
    width = (count + 2) * HOP
    copies = []

    def fetch(source, target):
        copy = pltpu.make_async_copy(source, target, sems.at[len(copies)])
        copy.start()
        copies.append(copy)

    fetch(offs, offs_v)
    fetch(sources, sources_v)
    if late:
        held[:, : width - W] = rest_v[...]
        held[:, width - W :] = halo[...]
        ready = len(copies)
    else:
        fetch(taper, taper_v)
        for at in range(0, width, width // 2):
            fetch(rec.at[:, pl.ds(at, width // 2)], held.at[:, pl.ds(at, width // 2)])
        ready = len(copies)
        rows = FOLD // 4
        for at in range(0, FOLD, rows):
            fetch(table.at[pl.ds(at, rows)], table_v.at[pl.ds(at, rows)])
        fetch(smooth, smooth_v)
        fetch(rec.at[:, pl.ds(0, W)], out_edge)
        fetch(rec.at[:, pl.ds(count * HOP, rest_v.shape[1])], rest_v)
    for copy in copies[:ready]:
        copy.wait()

    lanes = lax.broadcasted_iota(jnp.int32, (c_dev, LANE), 1)

    def cut(slot):
        start = slot * HOP + offs_v[first + slot]
        rest = start % LANE
        keep = lanes < LANE - rest
        shift = (LANE - rest) % LANE
        chunk = held[:, pl.ds(pl.multiple_of(start // LANE * LANE, LANE), CUT)].astype(jnp.float32)
        turned = [pltpu.roll(chunk[:, i * LANE : (i + 1) * LANE], shift, 1) for i in range(CUT // LANE)]
        row = pl.ds(pl.multiple_of(slot * c_dev, c_dev), c_dev)
        tiles = FOLD // LANE
        for i in range(tiles):
            lo = slice(i * LANE, (i + 1) * LANE)
            hi = slice(FOLD + i * LANE, FOLD + (i + 1) * LANE)
            near = jnp.where(keep, turned[i], turned[i + 1]) * taper_v[:, lo]
            far = jnp.where(keep, turned[tiles + i], turned[tiles + i + 1]) * taper_v[:, hi]
            sums[row, lo] = (near + far).astype(jnp.bfloat16)
            diffs[row, lo] = (near - far).astype(jnp.bfloat16)

    pl.loop(0, count, unroll=4)(cut)
    for copy in copies[ready:]:
        copy.wait()

    split = 3 * LANE
    even = jnp.dot(sums[...], table_v[:, :split], preferred_element_type=jnp.float32)
    odd = jnp.dot(diffs[...], table_v[:, split:], preferred_element_type=jnp.float32)
    left = lax.broadcasted_iota(jnp.int32, (1, LANE), 1) < LANE // 2
    mixed_even, mixed_odd = even[:, 2 * LANE :], odd[:, 2 * LANE :]
    real = [even[:, :LANE], odd[:, :LANE], jnp.where(left, mixed_even, mixed_odd)]
    swapped = pltpu.roll(jnp.where(left, mixed_odd, mixed_even), LANE // 2, 1)
    imag = [even[:, LANE : 2 * LANE], odd[:, LANE : 2 * LANE], swapped]
    power = jnp.concatenate([r * r + i * i for r, i in zip(real, imag)], axis=1).astype(jnp.bfloat16)
    smoothed = jnp.dot(power, smooth_v[...], preferred_element_type=jnp.float32)
    factor = lax.rsqrt(smoothed + 1e-05)
    for i in range(NB // LANE):
        lo = slice(i * LANE, (i + 1) * LANE)
        hi = slice(NB + i * LANE, NB + (i + 1) * LANE)
        out_r[:, lo] = (real[i] * factor[:, lo]).astype(jnp.bfloat16)
        out_r[:, hi] = (imag[i] * factor[:, lo]).astype(jnp.bfloat16)
    rows = lax.broadcasted_iota(jnp.int32, (n_src * count, 1), 0)
    cols = lax.broadcasted_iota(jnp.int32, (n_src * count, count * c_dev), 1)
    wanted = jnp.zeros_like(rows)
    for s in range(n_src):
        wanted = jnp.where(rows // count == s, sources_v[s] % c_dev + (rows % count) * c_dev, wanted)
    picker = jnp.where(cols == wanted, 1.0, 0.0).astype(jnp.bfloat16)
    out_s[...] = jnp.dot(picker, out_r[...], preferred_element_type=jnp.float32).astype(jnp.bfloat16)
    if late:
        at = before_s.shape[0]
        out_all[:at] = before_s[...]
        out_all[at:] = out_s[...]


def spectra_call(record, offsets, src_idx, tables, first, count, late=None):
    c_dev = record.shape[0]
    n_rest = record.shape[1] - count * HOP
    n_src = src_idx.shape[0]
    vmem = pl.BlockSpec(memory_space=pltpu.VMEM)
    hbm = pl.BlockSpec(memory_space=pltpu.HBM)
    arrays = [offsets, src_idx]
    if late is None:
        arrays += [record, *tables]
    arrays = [pltpu.with_memory_space_constraint(a, pltpu.HBM) for a in arrays]
    specs = [hbm] * len(arrays)
    out_shape = [
        jax.ShapeDtypeStruct((count * c_dev, 2 * NB), jnp.bfloat16),
        jax.ShapeDtypeStruct((n_src * count, 2 * NB), jnp.bfloat16),
    ]
    if late is None:
        out_shape += [jax.ShapeDtypeStruct((c_dev, n), record.dtype) for n in (W, n_rest)]
        out_shape += [jax.ShapeDtypeStruct(t.shape, t.dtype) for t in tables]
    else:
        halo, earlier = late
        arrays += [record, halo, *tables, earlier]
        specs += [vmem] * 6
        out_shape.append(jax.ShapeDtypeStruct((earlier.shape[0] + n_src * count, 2 * NB), jnp.bfloat16))
    return pl.pallas_call(
        functools.partial(spectra_kernel, first, count, late is not None, c_dev, n_src),
        out_shape=out_shape,
        in_specs=specs,
        out_specs=[vmem] * len(out_shape),
        scratch_shapes=[
            pltpu.VMEM((count * c_dev, FOLD), jnp.bfloat16),
            pltpu.VMEM((count * c_dev, FOLD), jnp.bfloat16),
            pltpu.VMEM((c_dev, (count + 2) * HOP), jnp.bfloat16),
            pltpu.SMEM(offsets.shape, jnp.int32),
            pltpu.SMEM(src_idx.shape, jnp.int32),
            pltpu.SemaphoreType.DMA((16,)),
        ],
        compiler_params=pltpu.CompilerParams(vmem_limit_bytes=24 << 20),
        cost_estimate=pl.CostEstimate(
            flops=int((1.5 + 0.1 * count) * 1.15e9), bytes_accessed=1 << 20, transcendentals=0
        ),
        name="spectra",
    )(*arrays)


def cross_kernel(shares, sides, cuts, n_src, c_dev, scale, spans, last, n_done, *refs):
    n_list = len(shares)
    srcs = []
    for share in shares:
        srcs.append(refs[:share])
        refs = refs[share:]
    recs = []
    for parts in sides:
        recs.append([(refs[i], part) for i, part in enumerate(parts)])
        refs = refs[len(parts) :]
    before, refs = refs[: len(spans)], refs[len(spans) :]
    done, refs = refs[:n_done], refs[n_done:]
    if last:
        ltab, *outs, wide, cross = refs
    else:
        out, wide = refs
    n_win = cuts[-1]
    at = 0
    for src in srcs:
        for part in src:
            rows = slice(at, at + part.shape[1])
            real = part[0, :, :NB].astype(jnp.float32)
            imag = part[0, :, NB:].astype(jnp.float32)
            wide[rows, :NB] = real
            wide[rows, NB : 2 * NB] = real + imag
            wide[rows, 2 * NB :] = real - imag
            at += part.shape[1]
    tiles = NB // LANE
    n_side = len(sides)

    def run(step, first, groups, earlier):
        block = groups * n_src
        local = step // tiles * groups
        group = first + local
        lo, hi, top = (
            pl.ds(pl.multiple_of(step % tiles * LANE + i * NB, LANE), LANE) for i in range(3)
        )
        base = pl.multiple_of(group * (n_src * n_win), 8)
        src = wide.at[pl.ds(base, block * n_win)]

        def places(group, q):
            starts = [q * n_list * n_src * c_dev + (group * n_src + s) * c_dev for s in range(block)]
            return [pl.ds(pl.multiple_of(start, c_dev), c_dev) for start in starts]

        for q, parts in enumerate(recs):
            sums = [[jnp.zeros((c_dev, LANE), jnp.float32)] * 3 for _ in range(block)]
            for rec, part in parts:
                start, stop = cuts[part], cuts[part + 1]
                for w in range(stop - start):
                    row = slice(w * c_dev, (w + 1) * c_dev)
                    rec_real = rec[row, lo].astype(jnp.float32)
                    rec_imag = rec[row, hi].astype(jnp.float32)
                    rec_both = rec_real + rec_imag
                    for s in range(block):
                        at = s // n_src * n_src * n_win
                        at += start * n_src + s % n_src * (stop - start) + w
                        row = slice(at, at + 1)
                        both, plus, minus = sums[s]
                        sums[s] = [
                            both + src[row, lo] * rec_both,
                            plus + src[row, hi] * rec_real,
                            minus + src[row, top] * rec_imag,
                        ]
            target = cross if last else out
            near, far = places(group, q), places(local, 0)
            for s in range(block):
                both, plus, minus = sums[s]
                real, imag = both - minus, both - plus
                if earlier is not None:
                    real += earlier[far[s], lo]
                    imag += earlier[far[s], hi]
                target[near[s], lo] = real.astype(target.dtype)
                target[near[s], hi] = imag.astype(target.dtype)

    first = 0
    for span, earlier in zip(spans or [n_list], before or [None]):
        groups = 8 // n_src if span * n_src % 8 == 0 and 8 % n_src == 0 else 1
        pl.loop(0, span // groups * tiles)(
            functools.partial(run, first=first, groups=groups, earlier=earlier)
        )
        first += span

    if last:
        lagged = jnp.dot(cross[...], ltab[...], preferred_element_type=jnp.float32)
        lagged = (lagged * scale).astype(jnp.bfloat16)
        height = n_list * n_src * c_dev
        done = list(done)
        for q, out in enumerate(outs):
            at = 0
            while at < out.shape[0] - height:
                part = done.pop(0)
                out[at : at + part.shape[0], :] = part[...]
                at += part.shape[0]
            out[at:, :] = lagged[q * height : (q + 1) * height]


def cross_call(srcs, sides, cuts, n_src, c_dev, scale, before=(), ltab=None, done=()):
    n_list, n_side = len(srcs), len(sides)
    groups = srcs[0][0].shape[0]
    last = ltab is not None
    unit = n_src * c_dev
    rows = n_list * n_side * unit
    whole = pl.BlockSpec(memory_space=pltpu.VMEM)
    arrays = [part for src in srcs for part in src]
    specs = [pl.BlockSpec((1,) + a.shape[1:], lambda g: (g, 0, 0)) for a in arrays]
    others = [a for parts in sides for a in parts.values()] + list(before)
    scratch = [pltpu.VMEM((n_list * n_src * cuts[-1], 3 * NB), jnp.float32)]
    if last:
        others += list(done) + [ltab]
        scratch.append(pltpu.VMEM((rows, 2 * NB), jnp.bfloat16))
        heights = [n_list * unit + sum(a.shape[0] for a in done) // n_side] * n_side
        shapes = [jax.ShapeDtypeStruct((groups * h, LAGS), jnp.bfloat16) for h in heights]
    else:
        heights = [rows]
        shapes = [jax.ShapeDtypeStruct((groups * rows, 2 * NB), jnp.float32)]
    windows = sum(cuts[p + 1] - cuts[p] for parts in sides for p in parts)
    micros = 0.4 + groups * n_list * n_src * windows * 0.008
    return pl.pallas_call(
        functools.partial(
            cross_kernel, [len(src) for src in srcs], [list(p) for p in sides], cuts, n_src, c_dev,
            scale, [a.shape[0] // unit for a in before], last, len(done),
        ),
        grid=(groups,),
        out_shape=shapes,
        in_specs=specs + [whole] * len(others),
        out_specs=[pl.BlockSpec((h, a.shape[1]), lambda g: (g, 0)) for h, a in zip(heights, shapes)],
        scratch_shapes=scratch,
        compiler_params=pltpu.CompilerParams(vmem_limit_bytes=24 << 20),
        cost_estimate=pl.CostEstimate(
            flops=int(micros * 1.15e9), bytes_accessed=1 << 20, transcendentals=0
        ),
        name="cross",
    )(*arrays, *others)


def body(record, offsets, src_idx):
    c_dev = record.shape[0]
    n_win = offsets.shape[0]
    n_src = src_idx.shape[0]
    n_tm = lax.axis_size("tm")
    n_fibre = lax.axis_size("fibre")
    n_group = n_fibre // 2
    fibre = lax.axis_index("fibre")
    tm = lax.axis_index("tm")
    early = n_win * 3 // 4
    cuts = (0, early, n_win)
    scale = 1.0 / math.sqrt(n_win * n_tm * NB)
    tables = [jnp.asarray(t) for t in (half_tables(), taper_table(), smoothing())]
    ltab = jnp.asarray(lag_table())
    direct = n_group == 4 and n_tm == 4

    def trade(array, by):
        return lax.ppermute(array, "fibre", [(i, i ^ by) for i in range(n_fibre)])

    rec_a, src_a, edge, rest, *tables = spectra_call(record, offsets, src_idx, tables, 0, early)
    far_a = trade(rec_a, 1)
    if direct:
        by_2a = trade(src_a, 4)
    halo = lax.ppermute(edge, "tm", [(i, i - 1) for i in range(1, n_tm)])
    rec_b, src_b, src = spectra_call(rest, offsets, src_idx, tables, early, n_win - early, (halo, src_a))
    far_b = trade(rec_b, 1)
    cross = functools.partial(cross_call, cuts=cuts, n_src=n_src, c_dev=c_dev, scale=scale)
    own = [{0: rec_a, 1: rec_b}]
    if direct:
        by_2 = jnp.concatenate([by_2a, trade(src_b, 4)], axis=0)
        by_1 = trade(src, 2)
        by_3 = trade(by_2, 2)
        srcs = [[part[None]] for part in (src, by_1, by_2, by_3)]
        near = [cross(srcs[k : k + 1], own, ltab=ltab)[0] for k in range(3)]
        parts = [*cross(srcs[:2], [{0: far_a}]), *cross(srcs[2:3], [{0: far_a}])]
        far = cross(srcs[:3], [{1: far_b}], before=parts, ltab=ltab)
        near, far = cross(srcs[3:], own + [{0: far_a, 1: far_b}], ltab=ltab, done=[*near, *far])
    else:
        ranks = [[2 * j + p for j in range(n_group)] for p in range(2)]
        srcs = [[lax.all_gather(src, "fibre", axis=0, axis_index_groups=ranks)]]
        near, far = cross(srcs, own + [{0: far_a, 1: far_b}], ltab=ltab)
    near, far = (r.reshape(n_group, n_src, c_dev, LAGS) for r in (near, far))

    def piece(lagged, owner):
        if direct:
            return lax.dynamic_index_in_dim(lagged, (fibre // 2) ^ owner, 0, keepdims=True)
        share = n_group // n_tm
        return lax.dynamic_slice_in_dim(lagged, owner * share, share, 0)

    keep = jnp.stack([piece(r, tm ^ k) for r in (near, far) for k in range(0, n_tm, 2)])
    give = jnp.stack([piece(r, tm ^ k) for r in (near, far) for k in range(1, n_tm, 2)])
    got = lax.ppermute(give, "tm", [(i, i ^ 1) for i in range(n_tm)])
    pairs = keep.astype(jnp.float32) + got.astype(jnp.float32)
    totals = []
    for side in range(2):
        total = None
        for k in range(n_tm // 2):
            mine = pairs[side * (n_tm // 2) + k]
            if side or k:
                routes = [
                    (i * n_tm + t, (i ^ side) * n_tm + (t ^ (2 * k)))
                    for i in range(n_fibre)
                    for t in range(n_tm)
                ]
                mine = lax.ppermute(mine.astype(jnp.bfloat16), ("fibre", "tm"), routes)
                mine = mine.astype(jnp.float32)
            total = mine if total is None else total + mine
        totals.append(total)
    even = fibre % 2 == 0
    near, far = totals
    out = jnp.stack([jnp.where(even, near, far), jnp.where(even, far, near)], axis=1)
    return out.reshape(-1, c_dev, LAGS)


def solution(mesh):
    return jax.shard_map(
        body,
        mesh=mesh,
        in_specs=(P("fibre", "tm"), P("tm"), P("fibre")),
        out_specs=P("tm", "fibre", None),
        check_vma=False,
    )
```

```python
import functools
import math

import jax
import jax.numpy as jnp
import numpy as np
from jax import lax
from jax.experimental import pallas as pl
from jax.experimental.pallas import tpu as pltpu
from jax.sharding import PartitionSpec as P

W = 2048
HOP = 1024
NB = 384
B0 = 20
SMOOTH = 64
LAGS = 256
LANE = 128
CUT = W + LANE
FOLD = W // 2
BINS = np.concatenate(
    [np.arange(0, 256, 2), np.arange(1, 256, 2), np.arange(256, NB, 2), np.arange(257, NB, 2)]
)


def taper_table():
    return (0.5 - 0.5 * np.cos(np.arange(W) * (2.0 * math.pi / W))).astype(np.float32)[None, :]


def half_tables():
    samples = np.arange(FOLD, dtype=np.int64)[:, None]

    def waves(bins):
        turns = (samples * (B0 + bins)[None, :] % W) * (2.0 * math.pi / W)
        return np.cos(turns), -np.sin(turns)

    even_cos, even_sin = waves(np.arange(0, NB, 2))
    odd_cos, odd_sin = waves(np.arange(1, NB, 2))
    cut = LANE
    columns = [
        even_cos[:, :cut], even_sin[:, :cut], even_cos[:, cut:], even_sin[:, cut:],
        odd_cos[:, :cut], odd_sin[:, :cut], odd_sin[:, cut:], odd_cos[:, cut:],
    ]
    return np.concatenate(columns, axis=1).astype(np.float32).astype(jnp.bfloat16)


def smoothing():
    rows = BINS[:, None]
    cols = BINS[None, :]
    first = np.clip(cols - SMOOTH // 2, 0, NB - SMOOTH)
    return np.where((rows >= first) & (rows < first + SMOOTH), 1.0 / SMOOTH, 0.0).astype(jnp.bfloat16)


def lag_table():
    shifts = np.arange(LAGS, dtype=np.int64) - LAGS // 2
    turns = ((B0 + BINS)[:, None] * shifts[None, :] % W) * (2.0 * math.pi / W)
    table = np.concatenate([np.cos(turns), -np.sin(turns)], axis=0)
    return table.astype(np.float32).astype(jnp.bfloat16)


def spectra_kernel(first, count, late, c_dev, n_src, *refs):
    if late:
        offs, sources, rec, halo, table_v, taper_v, smooth_v, before_s, out_r, out_s, out_all, *refs = refs
        sums, diffs, held, offs_v, sources_v, sems = refs
    else:
        offs, sources, rec, table, taper, smooth, *refs = refs
        out_r, out_s, out_edge, table_v, taper_v, smooth_v, *refs = refs
        sums, diffs, held, offs_v, sources_v, sems = refs
    width = (count + 2) * HOP
    copies = []

    def fetch(source, target):
        copy = pltpu.make_async_copy(source, target, sems.at[len(copies)])
        copy.start()
        copies.append(copy)

    fetch(offs, offs_v)
    fetch(sources, sources_v)
    inside = width - (W if late else 0)
    for at in range(0, inside, inside // 2):
        fetch(rec.at[:, pl.ds(first * HOP + at, inside // 2)], held.at[:, pl.ds(at, inside // 2)])
    if late:
        held[:, inside:] = halo[...]
        ready = len(copies)
    else:
        fetch(taper, taper_v)
        ready = len(copies)
        rows = FOLD // 4
        for at in range(0, FOLD, rows):
            fetch(table.at[pl.ds(at, rows)], table_v.at[pl.ds(at, rows)])
        fetch(smooth, smooth_v)
        fetch(rec.at[:, pl.ds(0, W)], out_edge)
    for copy in copies[:ready]:
        copy.wait()

    lanes = lax.broadcasted_iota(jnp.int32, (c_dev, LANE), 1)

    def cut(slot):
        start = slot * HOP + offs_v[first + slot]
        rest = start % LANE
        keep = lanes < LANE - rest
        shift = (LANE - rest) % LANE
        chunk = held[:, pl.ds(pl.multiple_of(start // LANE * LANE, LANE), CUT)].astype(jnp.float32)
        turned = [pltpu.roll(chunk[:, i * LANE : (i + 1) * LANE], shift, 1) for i in range(CUT // LANE)]
        row = pl.ds(pl.multiple_of(slot * c_dev, c_dev), c_dev)
        tiles = FOLD // LANE
        for i in range(tiles):
            lo = slice(i * LANE, (i + 1) * LANE)
            hi = slice(FOLD + i * LANE, FOLD + (i + 1) * LANE)
            near = jnp.where(keep, turned[i], turned[i + 1]) * taper_v[:, lo]
            far = jnp.where(keep, turned[tiles + i], turned[tiles + i + 1]) * taper_v[:, hi]
            sums[row, lo] = (near + far).astype(jnp.bfloat16)
            diffs[row, lo] = (near - far).astype(jnp.bfloat16)

    pl.loop(0, count, unroll=4)(cut)
    for copy in copies[ready:]:
        copy.wait()

    split = 3 * LANE
    even = jnp.dot(sums[...], table_v[:, :split], preferred_element_type=jnp.float32)
    odd = jnp.dot(diffs[...], table_v[:, split:], preferred_element_type=jnp.float32)
    left = lax.broadcasted_iota(jnp.int32, (1, LANE), 1) < LANE // 2
    mixed_even, mixed_odd = even[:, 2 * LANE :], odd[:, 2 * LANE :]
    real = [even[:, :LANE], odd[:, :LANE], jnp.where(left, mixed_even, mixed_odd)]
    swapped = pltpu.roll(jnp.where(left, mixed_odd, mixed_even), LANE // 2, 1)
    imag = [even[:, LANE : 2 * LANE], odd[:, LANE : 2 * LANE], swapped]
    power = jnp.concatenate([r * r + i * i for r, i in zip(real, imag)], axis=1).astype(jnp.bfloat16)
    smoothed = jnp.dot(power, smooth_v[...], preferred_element_type=jnp.float32)
    factor = lax.rsqrt(smoothed + 1e-05)
    for i in range(NB // LANE):
        lo = slice(i * LANE, (i + 1) * LANE)
        hi = slice(NB + i * LANE, NB + (i + 1) * LANE)
        out_r[:, lo] = (real[i] * factor[:, lo]).astype(jnp.bfloat16)
        out_r[:, hi] = (imag[i] * factor[:, lo]).astype(jnp.bfloat16)
    rows = lax.broadcasted_iota(jnp.int32, (n_src * count, 1), 0)
    cols = lax.broadcasted_iota(jnp.int32, (n_src * count, count * c_dev), 1)
    wanted = jnp.zeros_like(rows)
    for s in range(n_src):
        wanted = jnp.where(rows // count == s, sources_v[s] % c_dev + (rows % count) * c_dev, wanted)
    picker = jnp.where(cols == wanted, 1.0, 0.0).astype(jnp.bfloat16)
    out_s[...] = jnp.dot(picker, out_r[...], preferred_element_type=jnp.float32).astype(jnp.bfloat16)
    if late:
        at = before_s.shape[0]
        out_all[:at] = before_s[...]
        out_all[at:] = out_s[...]


def spectra_call(record, offsets, src_idx, tables, first, count, late=None):
    c_dev = record.shape[0]
    n_src = src_idx.shape[0]
    vmem = pl.BlockSpec(memory_space=pltpu.VMEM)
    hbm = pl.BlockSpec(memory_space=pltpu.HBM)
    arrays = [offsets, src_idx, record]
    if late is None:
        arrays += tables
    arrays = [pltpu.with_memory_space_constraint(a, pltpu.HBM) for a in arrays]
    specs = [hbm] * len(arrays)
    out_shape = [
        jax.ShapeDtypeStruct((count * c_dev, 2 * NB), jnp.bfloat16),
        jax.ShapeDtypeStruct((n_src * count, 2 * NB), jnp.bfloat16),
    ]
    if late is None:
        out_shape.append(jax.ShapeDtypeStruct((c_dev, W), record.dtype))
        out_shape += [jax.ShapeDtypeStruct(t.shape, t.dtype) for t in tables]
    else:
        halo, earlier = late
        arrays += [halo, *tables, earlier]
        specs += [vmem] * 5
        out_shape.append(jax.ShapeDtypeStruct((earlier.shape[0] + n_src * count, 2 * NB), jnp.bfloat16))
    return pl.pallas_call(
        functools.partial(spectra_kernel, first, count, late is not None, c_dev, n_src),
        out_shape=out_shape,
        in_specs=specs,
        out_specs=[vmem] * len(out_shape),
        scratch_shapes=[
            pltpu.VMEM((count * c_dev, FOLD), jnp.bfloat16),
            pltpu.VMEM((count * c_dev, FOLD), jnp.bfloat16),
            pltpu.VMEM((c_dev, (count + 2) * HOP), jnp.bfloat16),
            pltpu.SMEM(offsets.shape, jnp.int32),
            pltpu.SMEM(src_idx.shape, jnp.int32),
            pltpu.SemaphoreType.DMA((16,)),
        ],
        compiler_params=pltpu.CompilerParams(vmem_limit_bytes=24 << 20),
        cost_estimate=pl.CostEstimate(
            flops=int((1.5 + 0.1 * count) * 1.15e9), bytes_accessed=1 << 20, transcendentals=0
        ),
        name="spectra",
    )(*arrays)


def cross_kernel(plan, n_src, n_win, c_dev, scale, n_done, n_after, last, *refs):
    runs = []
    for n_group, parts, has_before in plan:
        srcs, refs = refs[:n_group], refs[n_group:]
        recs, refs = refs[: len(parts)], refs[len(parts) :]
        before, refs = refs[: int(has_before)], refs[int(has_before) :]
        runs.append((srcs, list(zip(recs, parts)), before))
    done, refs = refs[:n_done], refs[n_done:]
    if last:
        ltab, refs = refs[0], refs[1:]
    refs = refs[n_after:]
    if last:
        out, *assembled, wide, cross = refs
    else:
        out, wide = refs
        cross = out
    at = 0
    for srcs, _, _ in runs:
        for src in srcs:
            rows = slice(at, at + src.shape[1])
            real = src[0, :, :NB].astype(jnp.float32)
            imag = src[0, :, NB:].astype(jnp.float32)
            wide[rows, :NB] = real
            wide[rows, NB : 2 * NB] = real + imag
            wide[rows, 2 * NB :] = real - imag
            at += src.shape[1]
    tiles = NB // LANE

    def run(step, first, groups, recs, before):
        block = groups * n_src
        local = step // tiles * groups
        lo, hi, top = (
            pl.ds(pl.multiple_of(step % tiles * LANE + i * NB, LANE), LANE) for i in range(3)
        )
        base = pl.multiple_of((first + local) * (n_src * n_win), 8)
        src = wide.at[pl.ds(base, block * n_win)]

        def place(group, s):
            return pl.ds(pl.multiple_of((group * n_src + s) * c_dev, c_dev), c_dev)

        sums = [[jnp.zeros((c_dev, LANE), jnp.float32)] * 3 for _ in range(block)]
        for rec, (start, stop) in recs:
            for w in range(stop - start):
                row = slice(w * c_dev, (w + 1) * c_dev)
                rec_real = rec[row, lo].astype(jnp.float32)
                rec_imag = rec[row, hi].astype(jnp.float32)
                rec_both = rec_real + rec_imag
                for s in range(block):
                    at = s // n_src * n_src * n_win
                    at += start * n_src + s % n_src * (stop - start) + w
                    row = slice(at, at + 1)
                    both, plus, minus = sums[s]
                    sums[s] = [
                        both + src[row, lo] * rec_both,
                        plus + src[row, hi] * rec_real,
                        minus + src[row, top] * rec_imag,
                    ]
        for s in range(block):
            both, plus, minus = sums[s]
            real, imag = both - minus, both - plus
            for earlier in before:
                real += earlier[place(local, s), lo]
                imag += earlier[place(local, s), hi]
            cross[place(first + local, s), lo] = real.astype(cross.dtype)
            cross[place(first + local, s), hi] = imag.astype(cross.dtype)

    first = 0
    for srcs, recs, before in runs:
        groups = 8 // n_src if len(srcs) * n_src % 8 == 0 and 8 % n_src == 0 else 1
        pl.loop(0, len(srcs) // groups * tiles)(
            functools.partial(run, first=first, groups=groups, recs=recs, before=before)
        )
        first += len(srcs)

    if last:
        lagged = jnp.dot(cross[...], ltab[...], preferred_element_type=jnp.float32)
        out[...] = (lagged * scale).astype(jnp.bfloat16)
    at = 0
    for part in done:
        assembled[0][at : at + part.shape[0], :] = part[...]
        at += part.shape[0]


def cross_call(runs, n_src, n_win, c_dev, scale, ltab=None, done=(), after=()):
    grid = runs[0][0][0].shape[0]
    last = ltab is not None
    n_list = sum(len(srcs) for srcs, _, _ in runs)
    rows = n_list * n_src * c_dev
    whole = pl.BlockSpec(memory_space=pltpu.VMEM)
    arrays, specs, plan, pairs = [], [], [], 0
    for srcs, parts, before in runs:
        arrays += srcs
        specs += [pl.BlockSpec((1,) + a.shape[1:], lambda g: (g, 0, 0)) for a in srcs]
        others = [rec for rec, _ in parts] + ([] if before is None else [before])
        arrays += others
        specs += [whole] * len(others)
        plan.append((len(srcs), [cut for _, cut in parts], before is not None))
        pairs += len(srcs) * n_src * sum(stop - start for _, (start, stop) in parts)
    others = list(done) + ([ltab] if last else [])
    arrays += others + list(after)
    specs += [whole] * len(others) + [pl.BlockSpec(memory_space=pl.ANY)] * len(after)
    scratch = [pltpu.VMEM((n_list * n_src * n_win, 3 * NB), jnp.float32)]
    if last:
        scratch.append(pltpu.VMEM((rows, 2 * NB), jnp.bfloat16))
    shapes = [
        jax.ShapeDtypeStruct((grid * rows, LAGS), jnp.bfloat16)
        if last
        else jax.ShapeDtypeStruct((grid * rows, 2 * NB), jnp.float32)
    ]
    out_specs = [pl.BlockSpec((rows, shapes[0].shape[1]), lambda g: (g, 0))]
    if done:
        shapes.append(jax.ShapeDtypeStruct((sum(a.shape[0] for a in done), LAGS), jnp.bfloat16))
        out_specs.append(whole)
    return pl.pallas_call(
        functools.partial(cross_kernel, plan, n_src, n_win, c_dev, scale, len(done), len(after), last),
        grid=(grid,),
        out_shape=shapes,
        in_specs=specs,
        out_specs=out_specs,
        scratch_shapes=scratch,
        compiler_params=pltpu.CompilerParams(vmem_limit_bytes=24 << 20),
        cost_estimate=pl.CostEstimate(
            flops=int((0.4 + grid * pairs * 0.008) * 1.15e9), bytes_accessed=1 << 20, transcendentals=0
        ),
        name="cross",
    )(*arrays)


def body(record, offsets, src_idx):
    c_dev = record.shape[0]
    n_win = offsets.shape[0]
    n_src = src_idx.shape[0]
    n_tm = lax.axis_size("tm")
    n_fibre = lax.axis_size("fibre")
    n_group = n_fibre // 2
    fibre = lax.axis_index("fibre")
    tm = lax.axis_index("tm")
    early = n_win * 3 // 4
    scale = 1.0 / math.sqrt(n_win * n_tm * NB)
    tables = [jnp.asarray(t) for t in (half_tables(), taper_table(), smoothing())]
    ltab = jnp.asarray(lag_table())
    direct = n_group == 4 and n_tm == 4

    def trade(array, by):
        return lax.ppermute(array, "fibre", [(i, i ^ by) for i in range(n_fibre)])

    rec_a, src_a, edge, *tables = spectra_call(record, offsets, src_idx, tables, 0, early)
    far_a = trade(rec_a, 1)
    if direct:
        by_2a = trade(src_a, 4)
    halo = lax.ppermute(edge, "tm", [(i, i - 1) for i in range(1, n_tm)])
    rec_b, src_b, src = spectra_call(record, offsets, src_idx, tables, early, n_win - early, (halo, src_a))
    far_b = trade(rec_b, 1)
    cross = functools.partial(cross_call, n_src=n_src, n_win=n_win, c_dev=c_dev, scale=scale)
    head, rest = (0, early), (early, n_win)
    own = [(rec_a, head), (rec_b, rest)]
    if direct:
        by_2 = jnp.concatenate([by_2a, trade(src_b, 4)], axis=0)
        by_1 = trade(src, 2)
        by_3 = trade(by_2, 2)
        srcs = [part[None] for part in (src, by_1, by_2, by_3)]
        split = (srcs[:1], srcs[1:3], srcs[3:])
        near, sums = [], []
        for k, part in enumerate(split):
            after = sums[-1:]
            near += cross([(part, own, None)], ltab=ltab, after=after)
            sums += cross([(part, [(far_a, head)], None)], after=near[-1:])
        runs = [(part, [(far_b, rest)], before) for part, before in zip(split, sums)]
        far, near = cross(runs, ltab=ltab, done=near)
    else:
        ranks = [[2 * j + p for j in range(n_group)] for p in range(2)]
        srcs = [lax.all_gather(src, "fibre", axis=0, axis_index_groups=ranks)]
        near = cross([(srcs, own, None)], ltab=ltab)[0]
        far = cross([(srcs, [(far_a, head), (far_b, rest)], None)], ltab=ltab)[0]
    near, far = (r.reshape(n_group, n_src, c_dev, LAGS) for r in (near, far))

    def piece(lagged, owner):
        if direct:
            return lax.dynamic_index_in_dim(lagged, (fibre // 2) ^ owner, 0, keepdims=True)
        share = n_group // n_tm
        return lax.dynamic_slice_in_dim(lagged, owner * share, share, 0)

    keep = jnp.stack([piece(r, tm ^ k) for r in (near, far) for k in range(0, n_tm, 2)])
    give = jnp.stack([piece(r, tm ^ k) for r in (near, far) for k in range(1, n_tm, 2)])
    got = lax.ppermute(give, "tm", [(i, i ^ 1) for i in range(n_tm)])
    pairs = keep.astype(jnp.float32) + got.astype(jnp.float32)
    totals = []
    for side in range(2):
        total = None
        for k in range(n_tm // 2):
            mine = pairs[side * (n_tm // 2) + k]
            if side or k:
                routes = [
                    (i * n_tm + t, (i ^ side) * n_tm + (t ^ (2 * k)))
                    for i in range(n_fibre)
                    for t in range(n_tm)
                ]
                mine = lax.ppermute(mine.astype(jnp.bfloat16), ("fibre", "tm"), routes)
                mine = mine.astype(jnp.float32)
            total = mine if total is None else total + mine
        totals.append(total)
    even = fibre % 2 == 0
    near, far = totals
    out = jnp.stack([jnp.where(even, near, far), jnp.where(even, far, near)], axis=1)
    return out.reshape(-1, c_dev, LAGS)


def solution(mesh):
    return jax.shard_map(
        body,
        mesh=mesh,
        in_specs=(P("fibre", "tm"), P("tm"), P("fibre")),
        out_specs=P("tm", "fibre", None),
        check_vma=False,
    )
```

```python
import functools
import math

import jax
import jax.numpy as jnp
import numpy as np
from jax import lax
from jax.experimental import pallas as pl
from jax.experimental.pallas import tpu as pltpu
from jax.sharding import PartitionSpec as P

W = 2048
HOP = 1024
NB = 384
B0 = 20
SMOOTH = 64
LAGS = 256
LANE = 128
CUT = W + LANE
FOLD = W // 2
BINS = np.concatenate(
    [np.arange(0, 256, 2), np.arange(1, 256, 2), np.arange(256, NB, 2), np.arange(257, NB, 2)]
)


def taper_table():
    return (0.5 - 0.5 * np.cos(np.arange(W) * (2.0 * math.pi / W))).astype(np.float32)[None, :]


def half_tables():
    samples = np.arange(FOLD, dtype=np.int64)[:, None]

    def waves(bins):
        turns = (samples * (B0 + bins)[None, :] % W) * (2.0 * math.pi / W)
        return np.cos(turns), -np.sin(turns)

    even_cos, even_sin = waves(np.arange(0, NB, 2))
    odd_cos, odd_sin = waves(np.arange(1, NB, 2))
    cut = LANE
    columns = [
        even_cos[:, :cut], even_sin[:, :cut], even_cos[:, cut:], even_sin[:, cut:],
        odd_cos[:, :cut], odd_sin[:, :cut], odd_sin[:, cut:], odd_cos[:, cut:],
    ]
    return np.concatenate(columns, axis=1).astype(np.float32).astype(jnp.bfloat16)


def smoothing():
    rows = BINS[:, None]
    cols = BINS[None, :]
    first = np.clip(cols - SMOOTH // 2, 0, NB - SMOOTH)
    return np.where((rows >= first) & (rows < first + SMOOTH), 1.0 / SMOOTH, 0.0).astype(jnp.bfloat16)


def lag_table():
    shifts = np.arange(LAGS, dtype=np.int64) - LAGS // 2
    turns = ((B0 + BINS)[:, None] * shifts[None, :] % W) * (2.0 * math.pi / W)
    table = np.concatenate([np.cos(turns), -np.sin(turns)], axis=0)
    return table.astype(np.float32).astype(jnp.bfloat16)


def spectra_kernel(first, count, late, c_dev, n_src, *refs):
    if late:
        offs, sources, rec, halo, table_v, taper_v, smooth_v, before_s, out_r, out_s, out_all, *refs = refs
        sums, diffs, held, offs_v, sources_v, sems = refs
    else:
        offs, sources, rec, table, taper, smooth, *refs = refs
        out_r, out_s, out_edge, table_v, taper_v, smooth_v, *refs = refs
        sums, diffs, held, offs_v, sources_v, sems = refs
    width = (count + 2) * HOP
    copies = []

    def fetch(source, target):
        copy = pltpu.make_async_copy(source, target, sems.at[len(copies)])
        copy.start()
        copies.append(copy)

    fetch(offs, offs_v)
    fetch(sources, sources_v)
    inside = width - (W if late else 0)
    for at in range(0, inside, inside // 2):
        fetch(rec.at[:, pl.ds(first * HOP + at, inside // 2)], held.at[:, pl.ds(at, inside // 2)])
    if late:
        held[:, inside:] = halo[...]
        ready = len(copies)
    else:
        fetch(taper, taper_v)
        ready = len(copies)
        rows = FOLD // 4
        for at in range(0, FOLD, rows):
            fetch(table.at[pl.ds(at, rows)], table_v.at[pl.ds(at, rows)])
        fetch(smooth, smooth_v)
        fetch(rec.at[:, pl.ds(0, W)], out_edge)
    for copy in copies[:ready]:
        copy.wait()

    lanes = lax.broadcasted_iota(jnp.int32, (c_dev, LANE), 1)

    def cut(slot):
        start = slot * HOP + offs_v[first + slot]
        rest = start % LANE
        keep = lanes < LANE - rest
        shift = (LANE - rest) % LANE
        chunk = held[:, pl.ds(pl.multiple_of(start // LANE * LANE, LANE), CUT)].astype(jnp.float32)
        turned = [pltpu.roll(chunk[:, i * LANE : (i + 1) * LANE], shift, 1) for i in range(CUT // LANE)]
        row = pl.ds(pl.multiple_of(slot * c_dev, c_dev), c_dev)
        tiles = FOLD // LANE
        for i in range(tiles):
            lo = slice(i * LANE, (i + 1) * LANE)
            hi = slice(FOLD + i * LANE, FOLD + (i + 1) * LANE)
            near = jnp.where(keep, turned[i], turned[i + 1]) * taper_v[:, lo]
            far = jnp.where(keep, turned[tiles + i], turned[tiles + i + 1]) * taper_v[:, hi]
            sums[row, lo] = (near + far).astype(jnp.bfloat16)
            diffs[row, lo] = (near - far).astype(jnp.bfloat16)

    pl.loop(0, count, unroll=4)(cut)
    for copy in copies[ready:]:
        copy.wait()

    split = 3 * LANE
    even = jnp.dot(sums[...], table_v[:, :split], preferred_element_type=jnp.float32)
    odd = jnp.dot(diffs[...], table_v[:, split:], preferred_element_type=jnp.float32)
    left = lax.broadcasted_iota(jnp.int32, (1, LANE), 1) < LANE // 2
    mixed_even, mixed_odd = even[:, 2 * LANE :], odd[:, 2 * LANE :]
    real = [even[:, :LANE], odd[:, :LANE], jnp.where(left, mixed_even, mixed_odd)]
    swapped = pltpu.roll(jnp.where(left, mixed_odd, mixed_even), LANE // 2, 1)
    imag = [even[:, LANE : 2 * LANE], odd[:, LANE : 2 * LANE], swapped]
    power = jnp.concatenate([r * r + i * i for r, i in zip(real, imag)], axis=1).astype(jnp.bfloat16)
    smoothed = jnp.dot(power, smooth_v[...], preferred_element_type=jnp.float32)
    factor = lax.rsqrt(smoothed + 1e-05)
    for i in range(NB // LANE):
        lo = slice(i * LANE, (i + 1) * LANE)
        hi = slice(NB + i * LANE, NB + (i + 1) * LANE)
        out_r[:, lo] = (real[i] * factor[:, lo]).astype(jnp.bfloat16)
        out_r[:, hi] = (imag[i] * factor[:, lo]).astype(jnp.bfloat16)
    rows = lax.broadcasted_iota(jnp.int32, (n_src * count, 1), 0)
    cols = lax.broadcasted_iota(jnp.int32, (n_src * count, count * c_dev), 1)
    wanted = jnp.zeros_like(rows)
    for s in range(n_src):
        wanted = jnp.where(rows // count == s, sources_v[s] % c_dev + (rows % count) * c_dev, wanted)
    picker = jnp.where(cols == wanted, 1.0, 0.0).astype(jnp.bfloat16)
    out_s[...] = jnp.dot(picker, out_r[...], preferred_element_type=jnp.float32).astype(jnp.bfloat16)
    if late:
        at = before_s.shape[0]
        out_all[:at] = before_s[...]
        out_all[at:] = out_s[...]


def spectra_call(record, offsets, src_idx, tables, first, count, late=None):
    c_dev = record.shape[0]
    n_src = src_idx.shape[0]
    vmem = pl.BlockSpec(memory_space=pltpu.VMEM)
    hbm = pl.BlockSpec(memory_space=pltpu.HBM)
    arrays = [offsets, src_idx, record]
    if late is None:
        arrays += tables
    arrays = [pltpu.with_memory_space_constraint(a, pltpu.HBM) for a in arrays]
    specs = [hbm] * len(arrays)
    out_shape = [
        jax.ShapeDtypeStruct((count * c_dev, 2 * NB), jnp.bfloat16),
        jax.ShapeDtypeStruct((n_src * count, 2 * NB), jnp.bfloat16),
    ]
    if late is None:
        out_shape.append(jax.ShapeDtypeStruct((c_dev, W), record.dtype))
        out_shape += [jax.ShapeDtypeStruct(t.shape, t.dtype) for t in tables]
    else:
        halo, earlier = late
        arrays += [halo, *tables, earlier]
        specs += [vmem] * 5
        out_shape.append(jax.ShapeDtypeStruct((earlier.shape[0] + n_src * count, 2 * NB), jnp.bfloat16))
    return pl.pallas_call(
        functools.partial(spectra_kernel, first, count, late is not None, c_dev, n_src),
        out_shape=out_shape,
        in_specs=specs,
        out_specs=[vmem] * len(out_shape),
        scratch_shapes=[
            pltpu.VMEM((count * c_dev, FOLD), jnp.bfloat16),
            pltpu.VMEM((count * c_dev, FOLD), jnp.bfloat16),
            pltpu.VMEM((c_dev, (count + 2) * HOP), jnp.bfloat16),
            pltpu.SMEM(offsets.shape, jnp.int32),
            pltpu.SMEM(src_idx.shape, jnp.int32),
            pltpu.SemaphoreType.DMA((16,)),
        ],
        compiler_params=pltpu.CompilerParams(vmem_limit_bytes=24 << 20),
        cost_estimate=pl.CostEstimate(
            flops=int((1.5 + 0.1 * count) * 0.3e9), bytes_accessed=1 << 20, transcendentals=0
        ),
        name="spectra",
    )(*arrays)


def cross_kernel(plan, n_src, n_win, c_dev, scale, n_done, n_after, last, *refs):
    runs = []
    for n_group, parts, has_before in plan:
        srcs, refs = refs[:n_group], refs[n_group:]
        recs, refs = refs[: len(parts)], refs[len(parts) :]
        before, refs = refs[: int(has_before)], refs[int(has_before) :]
        runs.append((srcs, list(zip(recs, parts)), before))
    done, refs = refs[:n_done], refs[n_done:]
    if last:
        ltab, refs = refs[0], refs[1:]
    refs = refs[n_after:]
    if last:
        out, *assembled, wide, cross = refs
    else:
        out, wide = refs
        cross = out
    at = 0
    for srcs, _, _ in runs:
        for src in srcs:
            rows = slice(at, at + src.shape[1])
            real = src[0, :, :NB].astype(jnp.float32)
            imag = src[0, :, NB:].astype(jnp.float32)
            wide[rows, :NB] = real
            wide[rows, NB : 2 * NB] = real + imag
            wide[rows, 2 * NB :] = real - imag
            at += src.shape[1]
    tiles = NB // LANE

    def run(step, first, groups, recs, before):
        block = groups * n_src
        local = step // tiles * groups
        lo, hi, top = (
            pl.ds(pl.multiple_of(step % tiles * LANE + i * NB, LANE), LANE) for i in range(3)
        )
        base = pl.multiple_of((first + local) * (n_src * n_win), 8)
        src = wide.at[pl.ds(base, block * n_win)]

        def place(group, s):
            return pl.ds(pl.multiple_of((group * n_src + s) * c_dev, c_dev), c_dev)

        sums = [[jnp.zeros((c_dev, LANE), jnp.float32)] * 3 for _ in range(block)]
        for rec, (start, stop) in recs:
            for w in range(stop - start):
                row = slice(w * c_dev, (w + 1) * c_dev)
                rec_real = rec[row, lo].astype(jnp.float32)
                rec_imag = rec[row, hi].astype(jnp.float32)
                rec_both = rec_real + rec_imag
                for s in range(block):
                    at = s // n_src * n_src * n_win
                    at += start * n_src + s % n_src * (stop - start) + w
                    row = slice(at, at + 1)
                    both, plus, minus = sums[s]
                    sums[s] = [
                        both + src[row, lo] * rec_both,
                        plus + src[row, hi] * rec_real,
                        minus + src[row, top] * rec_imag,
                    ]
        for s in range(block):
            both, plus, minus = sums[s]
            real, imag = both - minus, both - plus
            for earlier in before:
                real += earlier[place(local, s), lo]
                imag += earlier[place(local, s), hi]
            cross[place(first + local, s), lo] = real.astype(cross.dtype)
            cross[place(first + local, s), hi] = imag.astype(cross.dtype)

    first = 0
    for srcs, recs, before in runs:
        groups = 8 // n_src if len(srcs) * n_src % 8 == 0 and 8 % n_src == 0 else 1
        pl.loop(0, len(srcs) // groups * tiles)(
            functools.partial(run, first=first, groups=groups, recs=recs, before=before)
        )
        first += len(srcs)

    if last:
        lagged = jnp.dot(cross[...], ltab[...], preferred_element_type=jnp.float32)
        out[...] = (lagged * scale).astype(jnp.bfloat16)
    at = 0
    for part in done:
        assembled[0][at : at + part.shape[0], :] = part[...]
        at += part.shape[0]


def cross_call(runs, n_src, n_win, c_dev, scale, ltab=None, done=(), after=()):
    grid = runs[0][0][0].shape[0]
    last = ltab is not None
    n_list = sum(len(srcs) for srcs, _, _ in runs)
    rows = n_list * n_src * c_dev
    whole = pl.BlockSpec(memory_space=pltpu.VMEM)
    arrays, specs, plan, pairs = [], [], [], 0
    for srcs, parts, before in runs:
        arrays += srcs
        if grid == 1:
            specs += [whole] * len(srcs)
        else:
            specs += [pl.BlockSpec((1,) + a.shape[1:], lambda g: (g, 0, 0)) for a in srcs]
        others = [rec for rec, _ in parts] + ([] if before is None else [before])
        arrays += others
        specs += [whole] * len(others)
        plan.append((len(srcs), [cut for _, cut in parts], before is not None))
        pairs += len(srcs) * n_src * sum(stop - start for _, (start, stop) in parts)
    others = list(done) + ([ltab] if last else [])
    arrays += others + list(after)
    specs += [whole] * len(others) + [pl.BlockSpec(memory_space=pl.ANY)] * len(after)
    scratch = [pltpu.VMEM((n_list * n_src * n_win, 3 * NB), jnp.float32)]
    if last:
        scratch.append(pltpu.VMEM((rows, 2 * NB), jnp.bfloat16))
    shapes = [
        jax.ShapeDtypeStruct((grid * rows, LAGS), jnp.bfloat16)
        if last
        else jax.ShapeDtypeStruct((grid * rows, 2 * NB), jnp.float32)
    ]
    out_specs = [whole if grid == 1 else pl.BlockSpec((rows, shapes[0].shape[1]), lambda g: (g, 0))]
    if done:
        shapes.append(jax.ShapeDtypeStruct((sum(a.shape[0] for a in done), LAGS), jnp.bfloat16))
        out_specs.append(whole)
    return pl.pallas_call(
        functools.partial(cross_kernel, plan, n_src, n_win, c_dev, scale, len(done), len(after), last),
        grid=() if grid == 1 else (grid,),
        out_shape=shapes,
        in_specs=specs,
        out_specs=out_specs,
        scratch_shapes=scratch,
        compiler_params=pltpu.CompilerParams(vmem_limit_bytes=24 << 20),
        cost_estimate=pl.CostEstimate(
            flops=int((0.4 + grid * pairs * 0.008) * 1.15e9), bytes_accessed=1 << 20, transcendentals=0
        ),
        name="cross",
    )(*arrays)


def body(record, offsets, src_idx):
    c_dev = record.shape[0]
    n_win = offsets.shape[0]
    n_src = src_idx.shape[0]
    n_tm = lax.axis_size("tm")
    n_fibre = lax.axis_size("fibre")
    n_group = n_fibre // 2
    fibre = lax.axis_index("fibre")
    tm = lax.axis_index("tm")
    early = n_win * 3 // 4
    scale = 1.0 / math.sqrt(n_win * n_tm * NB)
    tables = [jnp.asarray(t) for t in (half_tables(), taper_table(), smoothing())]
    ltab = jnp.asarray(lag_table())
    direct = n_group == 4 and n_tm == 4

    def trade(array, by):
        return lax.ppermute(array, "fibre", [(i, i ^ by) for i in range(n_fibre)])

    rec_a, src_a, edge, *tables = spectra_call(record, offsets, src_idx, tables, 0, early)
    far_a = trade(rec_a, 1)
    if direct:
        by_2a = trade(src_a, 4)
    halo = lax.ppermute(edge, "tm", [(i, i - 1) for i in range(1, n_tm)])
    rec_b, src_b, src = spectra_call(record, offsets, src_idx, tables, early, n_win - early, (halo, src_a))
    far_b = trade(rec_b, 1)
    cross = functools.partial(cross_call, n_src=n_src, n_win=n_win, c_dev=c_dev, scale=scale)
    head, rest = (0, early), (early, n_win)
    own = [(rec_a, head), (rec_b, rest)]
    if direct:
        by_2 = jnp.concatenate([by_2a, trade(src_b, 4)], axis=0)
        by_1 = trade(src, 2)
        by_3 = trade(by_2, 2)
        srcs = [part[None] for part in (src, by_1, by_2, by_3)]
        split = (srcs[:1], srcs[1:3], srcs[3:])
        near, sums = [], []
        for k, part in enumerate(split):
            after = sums[-1:]
            near += cross([(part, own, None)], ltab=ltab, after=after)
            sums += cross([(part, [(far_a, head)], None)], after=near[-1:])
        runs = [(part, [(far_b, rest)], before) for part, before in zip(split, sums)]
        far, near = cross(runs, ltab=ltab, done=near)
    else:
        ranks = [[2 * j + p for j in range(n_group)] for p in range(2)]
        srcs = [lax.all_gather(src, "fibre", axis=0, axis_index_groups=ranks)]
        near = cross([(srcs, own, None)], ltab=ltab)[0]
        far = cross([(srcs, [(far_a, head), (far_b, rest)], None)], ltab=ltab)[0]
    near, far = (r.reshape(n_group, n_src, c_dev, LAGS) for r in (near, far))

    def piece(lagged, owner):
        if direct:
            return lax.dynamic_index_in_dim(lagged, (fibre // 2) ^ owner, 0, keepdims=True)
        share = n_group // n_tm
        return lax.dynamic_slice_in_dim(lagged, owner * share, share, 0)

    keep = jnp.stack([piece(r, tm ^ k) for r in (near, far) for k in range(0, n_tm, 2)])
    give = jnp.stack([piece(r, tm ^ k) for r in (near, far) for k in range(1, n_tm, 2)])
    got = lax.ppermute(give, "tm", [(i, i ^ 1) for i in range(n_tm)])
    pairs = keep.astype(jnp.float32) + got.astype(jnp.float32)
    totals = []
    for side in range(2):
        total = None
        for k in range(n_tm // 2):
            mine = pairs[side * (n_tm // 2) + k]
            if side or k:
                routes = [
                    (i * n_tm + t, (i ^ side) * n_tm + (t ^ (2 * k)))
                    for i in range(n_fibre)
                    for t in range(n_tm)
                ]
                mine = lax.ppermute(mine.astype(jnp.bfloat16), ("fibre", "tm"), routes)
                mine = mine.astype(jnp.float32)
            total = mine if total is None else total + mine
        totals.append(total)
    even = fibre % 2 == 0
    near, far = totals
    out = jnp.stack([jnp.where(even, near, far), jnp.where(even, far, near)], axis=1)
    return out.reshape(-1, c_dev, LAGS)


def solution(mesh):
    return jax.shard_map(
        body,
        mesh=mesh,
        in_specs=(P("fibre", "tm"), P("tm"), P("fibre")),
        out_specs=P("tm", "fibre", None),
        check_vma=False,
    )
```

```python
import functools
import math

import jax
import jax.numpy as jnp
import numpy as np
from jax import lax
from jax.experimental import pallas as pl
from jax.experimental.pallas import tpu as pltpu
from jax.sharding import PartitionSpec as P

W = 2048
HOP = 1024
NB = 384
B0 = 20
SMOOTH = 64
LAGS = 256
LANE = 128
CUT = W + LANE
FOLD = W // 2
BINS = np.concatenate(
    [np.arange(0, 256, 2), np.arange(1, 256, 2), np.arange(256, NB, 2), np.arange(257, NB, 2)]
)


def taper_table():
    return (0.5 - 0.5 * np.cos(np.arange(W) * (2.0 * math.pi / W))).astype(np.float32)[None, :]


def half_tables():
    samples = np.arange(FOLD, dtype=np.int64)[:, None]

    def waves(bins):
        turns = (samples * (B0 + bins)[None, :] % W) * (2.0 * math.pi / W)
        return np.cos(turns), -np.sin(turns)

    even_cos, even_sin = waves(np.arange(0, NB, 2))
    odd_cos, odd_sin = waves(np.arange(1, NB, 2))
    cut = LANE
    columns = [
        even_cos[:, :cut], even_sin[:, :cut], even_cos[:, cut:], even_sin[:, cut:],
        odd_cos[:, :cut], odd_sin[:, :cut], odd_sin[:, cut:], odd_cos[:, cut:],
    ]
    return np.concatenate(columns, axis=1).astype(np.float32).astype(jnp.bfloat16)


def smoothing():
    rows = BINS[:, None]
    cols = BINS[None, :]
    first = np.clip(cols - SMOOTH // 2, 0, NB - SMOOTH)
    return np.where((rows >= first) & (rows < first + SMOOTH), 1.0 / SMOOTH, 0.0).astype(jnp.bfloat16)


def lag_table():
    shifts = np.arange(LAGS, dtype=np.int64) - LAGS // 2
    turns = ((B0 + BINS)[:, None] * shifts[None, :] % W) * (2.0 * math.pi / W)
    table = np.concatenate([np.cos(turns), -np.sin(turns)], axis=0)
    return table.astype(np.float32).astype(jnp.bfloat16)


def spectra_kernel(first, count, late, c_dev, n_src, *refs):
    if late:
        offs, sources, rec, halo, table_v, taper_v, smooth_v, before_r, before_s, *refs = refs
        out_r, out_s, out_all, *refs = refs
        sums, diffs, held, offs_v, sources_v, sems = refs
    else:
        offs, sources, rec, table, taper, smooth, *refs = refs
        out_r, out_mid, out_s, out_edge, table_v, taper_v, smooth_v, *refs = refs
        sums, diffs, held, offs_v, sources_v, sems = refs
    width = (count + 2) * HOP
    copies = []

    def fetch(source, target):
        copy = pltpu.make_async_copy(source, target, sems.at[len(copies)])
        copy.start()
        copies.append(copy)

    fetch(offs, offs_v)
    fetch(sources, sources_v)
    inside = width - (W if late else 0)
    for at in range(0, inside, inside // 2):
        fetch(rec.at[:, pl.ds(first * HOP + at, inside // 2)], held.at[:, pl.ds(at, inside // 2)])
    if late:
        held[:, inside:] = halo[...]
        ready = len(copies)
    else:
        fetch(taper, taper_v)
        ready = len(copies)
        rows = FOLD // 4
        for at in range(0, FOLD, rows):
            fetch(table.at[pl.ds(at, rows)], table_v.at[pl.ds(at, rows)])
        fetch(smooth, smooth_v)
        fetch(rec.at[:, pl.ds(0, W)], out_edge)
    for copy in copies[:ready]:
        copy.wait()

    lanes = lax.broadcasted_iota(jnp.int32, (c_dev, LANE), 1)

    def cut(slot):
        start = slot * HOP + offs_v[first + slot]
        rest = start % LANE
        keep = lanes < LANE - rest
        shift = (LANE - rest) % LANE
        chunk = held[:, pl.ds(pl.multiple_of(start // LANE * LANE, LANE), CUT)].astype(jnp.float32)
        turned = [pltpu.roll(chunk[:, i * LANE : (i + 1) * LANE], shift, 1) for i in range(CUT // LANE)]
        row = pl.ds(pl.multiple_of(slot * c_dev, c_dev), c_dev)
        tiles = FOLD // LANE
        for i in range(tiles):
            lo = slice(i * LANE, (i + 1) * LANE)
            hi = slice(FOLD + i * LANE, FOLD + (i + 1) * LANE)
            near = jnp.where(keep, turned[i], turned[i + 1]) * taper_v[:, lo]
            far = jnp.where(keep, turned[tiles + i], turned[tiles + i + 1]) * taper_v[:, hi]
            sums[row, lo] = (near + far).astype(jnp.bfloat16)
            diffs[row, lo] = (near - far).astype(jnp.bfloat16)

    pl.loop(0, count, unroll=4)(cut)
    for copy in copies[ready:]:
        copy.wait()

    split = 3 * LANE
    even = jnp.dot(sums[...], table_v[:, :split], preferred_element_type=jnp.float32)
    odd = jnp.dot(diffs[...], table_v[:, split:], preferred_element_type=jnp.float32)
    left = lax.broadcasted_iota(jnp.int32, (1, LANE), 1) < LANE // 2
    mixed_even, mixed_odd = even[:, 2 * LANE :], odd[:, 2 * LANE :]
    real = [even[:, :LANE], odd[:, :LANE], jnp.where(left, mixed_even, mixed_odd)]
    swapped = pltpu.roll(jnp.where(left, mixed_odd, mixed_even), LANE // 2, 1)
    imag = [even[:, LANE : 2 * LANE], odd[:, LANE : 2 * LANE], swapped]
    power = jnp.concatenate([r * r + i * i for r, i in zip(real, imag)], axis=1).astype(jnp.bfloat16)
    smoothed = jnp.dot(power, smooth_v[...], preferred_element_type=jnp.float32)
    factor = lax.rsqrt(smoothed + 1e-05)
    parts = [value * factor[:, i % 3 * LANE : (i % 3 + 1) * LANE] for i, value in enumerate(real + imag)]
    white = jnp.concatenate([part.astype(jnp.bfloat16) for part in parts], axis=1)
    if late:
        at = before_r.shape[0]
        out_r[:at] = before_r[...]
        out_r[at:] = white
    else:
        at = out_r.shape[0]
        out_r[...] = white[:at]
        out_mid[...] = white[at:]
    rows = lax.broadcasted_iota(jnp.int32, (n_src * count, 1), 0)
    cols = lax.broadcasted_iota(jnp.int32, (n_src * count, count * c_dev), 1)
    wanted = jnp.zeros_like(rows)
    for s in range(n_src):
        wanted = jnp.where(rows // count == s, sources_v[s] % c_dev + (rows % count) * c_dev, wanted)
    picker = jnp.where(cols == wanted, 1.0, 0.0).astype(jnp.bfloat16)
    out_s[...] = jnp.dot(picker, white, preferred_element_type=jnp.float32).astype(jnp.bfloat16)
    if late:
        at = before_s.shape[0]
        out_all[:at] = before_s[...]
        out_all[at:] = out_s[...]


def spectra_call(record, offsets, src_idx, tables, first, count, head=None, late=None):
    c_dev = record.shape[0]
    n_src = src_idx.shape[0]
    vmem = pl.BlockSpec(memory_space=pltpu.VMEM)
    hbm = pl.BlockSpec(memory_space=pltpu.HBM)
    arrays = [offsets, src_idx, record]
    if late is None:
        arrays += tables
    arrays = [pltpu.with_memory_space_constraint(a, pltpu.HBM) for a in arrays]
    specs = [hbm] * len(arrays)
    rows = [head, count - head] if late is None else [count + late[1].shape[0] // c_dev]
    out_shape = [jax.ShapeDtypeStruct((n * c_dev, 2 * NB), jnp.bfloat16) for n in rows]
    out_shape.append(jax.ShapeDtypeStruct((n_src * count, 2 * NB), jnp.bfloat16))
    if late is None:
        out_shape.append(jax.ShapeDtypeStruct((c_dev, W), record.dtype))
        out_shape += [jax.ShapeDtypeStruct(t.shape, t.dtype) for t in tables]
    else:
        halo, middle, sources = late
        arrays += [halo, *tables, middle, sources]
        specs += [vmem] * 6
        out_shape.append(jax.ShapeDtypeStruct((sources.shape[0] + n_src * count, 2 * NB), jnp.bfloat16))
    return pl.pallas_call(
        functools.partial(spectra_kernel, first, count, late is not None, c_dev, n_src),
        out_shape=out_shape,
        in_specs=specs,
        out_specs=[vmem] * len(out_shape),
        scratch_shapes=[
            pltpu.VMEM((count * c_dev, FOLD), jnp.bfloat16),
            pltpu.VMEM((count * c_dev, FOLD), jnp.bfloat16),
            pltpu.VMEM((c_dev, (count + 2) * HOP), jnp.bfloat16),
            pltpu.SMEM(offsets.shape, jnp.int32),
            pltpu.SMEM(src_idx.shape, jnp.int32),
            pltpu.SemaphoreType.DMA((16,)),
        ],
        compiler_params=pltpu.CompilerParams(vmem_limit_bytes=24 << 20),
        cost_estimate=pl.CostEstimate(
            flops=int((1.5 + 0.1 * count) * 0.01e9), bytes_accessed=1 << 20, transcendentals=0
        ),
        name="spectra",
    )(*arrays)


def cross_kernel(plan, n_src, n_win, early, c_dev, scale, n_done, n_after, last, *refs):
    runs = []
    for n_group, parts, has_before in plan:
        srcs, refs = refs[:n_group], refs[n_group:]
        recs, refs = refs[: len(parts)], refs[len(parts) :]
        before, refs = refs[: int(has_before)], refs[int(has_before) :]
        runs.append((srcs, list(zip(recs, parts)), before))
    done, refs = refs[:n_done], refs[n_done:]
    if last:
        ltab, refs = refs[0], refs[1:]
    refs = refs[n_after:]
    if last:
        out, *assembled, wide, cross = refs
    else:
        out, wide = refs
        cross = out
    at = 0
    for srcs, _, _ in runs:
        for src in srcs:
            rows = slice(at, at + src.shape[1])
            real = src[0, :, :NB].astype(jnp.float32)
            imag = src[0, :, NB:].astype(jnp.float32)
            wide[rows, :NB] = real
            wide[rows, NB : 2 * NB] = real + imag
            wide[rows, 2 * NB :] = real - imag
            at += src.shape[1]
    tiles = NB // LANE

    def run(step, first, groups, recs, before):
        block = groups * n_src
        local = step // tiles * groups
        lo, hi, top = (
            pl.ds(pl.multiple_of(step % tiles * LANE + i * NB, LANE), LANE) for i in range(3)
        )
        base = pl.multiple_of((first + local) * (n_src * n_win), 8)
        src = wide.at[pl.ds(base, block * n_win)]

        def place(group, s):
            return pl.ds(pl.multiple_of((group * n_src + s) * c_dev, c_dev), c_dev)

        sums = [[jnp.zeros((c_dev, LANE), jnp.float32)] * 3 for _ in range(block)]
        for rec, (start, stop) in recs:
            for w in range(stop - start):
                row = slice(w * c_dev, (w + 1) * c_dev)
                rec_real = rec[row, lo].astype(jnp.float32)
                rec_imag = rec[row, hi].astype(jnp.float32)
                rec_both = rec_real + rec_imag
                for s in range(block):
                    at = s // n_src * n_src * n_win
                    if start + w < early:
                        at += s % n_src * early + start + w
                    else:
                        at += n_src * early + s % n_src * (n_win - early) + start + w - early
                    row = slice(at, at + 1)
                    both, plus, minus = sums[s]
                    sums[s] = [
                        both + src[row, lo] * rec_both,
                        plus + src[row, hi] * rec_real,
                        minus + src[row, top] * rec_imag,
                    ]
        for s in range(block):
            both, plus, minus = sums[s]
            real, imag = both - minus, both - plus
            for earlier in before:
                real += earlier[place(local, s), lo]
                imag += earlier[place(local, s), hi]
            cross[place(first + local, s), lo] = real.astype(cross.dtype)
            cross[place(first + local, s), hi] = imag.astype(cross.dtype)

    first = 0
    for srcs, recs, before in runs:
        groups = 8 // n_src if len(srcs) * n_src % 8 == 0 and 8 % n_src == 0 else 1
        pl.loop(0, len(srcs) // groups * tiles)(
            functools.partial(run, first=first, groups=groups, recs=recs, before=before)
        )
        first += len(srcs)

    if last:
        lagged = jnp.dot(cross[...], ltab[...], preferred_element_type=jnp.float32)
        out[...] = (lagged * scale).astype(jnp.bfloat16)
    at = 0
    for part in done:
        assembled[0][at : at + part.shape[0], :] = part[...]
        at += part.shape[0]


def cross_call(runs, n_src, n_win, early, c_dev, scale, ltab=None, done=(), after=()):
    grid = runs[0][0][0].shape[0]
    last = ltab is not None
    n_list = sum(len(srcs) for srcs, _, _ in runs)
    rows = n_list * n_src * c_dev
    whole = pl.BlockSpec(memory_space=pltpu.VMEM)
    arrays, specs, plan, pairs = [], [], [], 0
    for srcs, parts, before in runs:
        arrays += srcs
        if grid == 1:
            specs += [whole] * len(srcs)
        else:
            specs += [pl.BlockSpec((1,) + a.shape[1:], lambda g: (g, 0, 0)) for a in srcs]
        others = [rec for rec, _ in parts] + ([] if before is None else [before])
        arrays += others
        specs += [whole] * len(others)
        plan.append((len(srcs), [cut for _, cut in parts], before is not None))
        pairs += len(srcs) * n_src * sum(stop - start for _, (start, stop) in parts)
    others = list(done) + ([ltab] if last else [])
    arrays += others + list(after)
    specs += [whole] * len(others) + [pl.BlockSpec(memory_space=pl.ANY)] * len(after)
    scratch = [pltpu.VMEM((n_list * n_src * n_win, 3 * NB), jnp.float32)]
    if last:
        scratch.append(pltpu.VMEM((rows, 2 * NB), jnp.bfloat16))
    shapes = [
        jax.ShapeDtypeStruct((grid * rows, LAGS), jnp.bfloat16)
        if last
        else jax.ShapeDtypeStruct((grid * rows, 2 * NB), jnp.float32)
    ]
    out_specs = [whole if grid == 1 else pl.BlockSpec((rows, shapes[0].shape[1]), lambda g: (g, 0))]
    if done:
        shapes.append(jax.ShapeDtypeStruct((sum(a.shape[0] for a in done), LAGS), jnp.bfloat16))
        out_specs.append(whole)
    return pl.pallas_call(
        functools.partial(cross_kernel, plan, n_src, n_win, early, c_dev, scale, len(done), len(after), last),
        grid=() if grid == 1 else (grid,),
        out_shape=shapes,
        in_specs=specs,
        out_specs=out_specs,
        scratch_shapes=scratch,
        compiler_params=pltpu.CompilerParams(vmem_limit_bytes=24 << 20),
        cost_estimate=pl.CostEstimate(
            flops=int((0.4 + grid * pairs * 0.008) * 0.6e9), bytes_accessed=1 << 20, transcendentals=0
        ),
        name="cross",
    )(*arrays)


def body(record, offsets, src_idx):
    c_dev = record.shape[0]
    n_win = offsets.shape[0]
    n_src = src_idx.shape[0]
    n_tm = lax.axis_size("tm")
    n_fibre = lax.axis_size("fibre")
    n_group = n_fibre // 2
    fibre = lax.axis_index("fibre")
    tm = lax.axis_index("tm")
    head, early = n_win * 3 // 4, n_win * 7 // 8
    scale = 1.0 / math.sqrt(n_win * n_tm * NB)
    tables = [jnp.asarray(t) for t in (half_tables(), taper_table(), smoothing())]
    ltab = jnp.asarray(lag_table())
    direct = n_group == 4 and n_tm == 4

    def trade(array, by):
        return lax.ppermute(array, "fibre", [(i, i ^ by) for i in range(n_fibre)])

    rec_a, middle, src_a, edge, *tables = spectra_call(record, offsets, src_idx, tables, 0, early, head)
    far_a = trade(rec_a, 1)
    if direct:
        by_2a = trade(src_a, 4)
    halo = lax.ppermute(edge, "tm", [(i, i - 1) for i in range(1, n_tm)])
    late = (halo, middle, src_a)
    rec_b, src_b, src = spectra_call(record, offsets, src_idx, tables, early, n_win - early, late=late)
    far_b = trade(rec_b, 1)
    cross = functools.partial(cross_call, n_src=n_src, n_win=n_win, early=early, c_dev=c_dev, scale=scale)
    head, rest = (0, head), (head, n_win)
    own = [(rec_a, head), (rec_b, rest)]
    if direct:
        by_2 = jnp.concatenate([by_2a, trade(src_b, 4)], axis=0)
        by_1 = trade(src, 2)
        by_3 = trade(by_2, 2)
        srcs = [part[None] for part in (src, by_1, by_2, by_3)]
        split = (srcs[:1], srcs[1:3], srcs[3:])
        near, sums = [], []
        for k, part in enumerate(split):
            after = sums[-1:]
            near += cross([(part, own, None)], ltab=ltab, after=after)
            sums += cross([(part, [(far_a, head)], None)], after=near[-1:])
        runs = [(part, [(far_b, rest)], before) for part, before in zip(split, sums)]
        far, near = cross(runs, ltab=ltab, done=near)
    else:
        ranks = [[2 * j + p for j in range(n_group)] for p in range(2)]
        srcs = [lax.all_gather(src, "fibre", axis=0, axis_index_groups=ranks)]
        near = cross([(srcs, own, None)], ltab=ltab)[0]
        far = cross([(srcs, [(far_a, head), (far_b, rest)], None)], ltab=ltab)[0]
    near, far = (r.reshape(n_group, n_src, c_dev, LAGS) for r in (near, far))

    def piece(lagged, owner):
        if direct:
            return lax.dynamic_index_in_dim(lagged, (fibre // 2) ^ owner, 0, keepdims=True)
        share = n_group // n_tm
        return lax.dynamic_slice_in_dim(lagged, owner * share, share, 0)

    keep = jnp.stack([piece(r, tm ^ k) for r in (near, far) for k in range(0, n_tm, 2)])
    give = jnp.stack([piece(r, tm ^ k) for r in (near, far) for k in range(1, n_tm, 2)])
    got = lax.ppermute(give, "tm", [(i, i ^ 1) for i in range(n_tm)])
    pairs = keep.astype(jnp.float32) + got.astype(jnp.float32)
    totals = []
    for side in range(2):
        total = None
        for k in range(n_tm // 2):
            mine = pairs[side * (n_tm // 2) + k]
            if side or k:
                routes = [
                    (i * n_tm + t, (i ^ side) * n_tm + (t ^ (2 * k)))
                    for i in range(n_fibre)
                    for t in range(n_tm)
                ]
                mine = lax.ppermute(mine.astype(jnp.bfloat16), ("fibre", "tm"), routes)
                mine = mine.astype(jnp.float32)
            total = mine if total is None else total + mine
        totals.append(total)
    even = fibre % 2 == 0
    near, far = totals
    out = jnp.stack([jnp.where(even, near, far), jnp.where(even, far, near)], axis=1)
    return out.reshape(-1, c_dev, LAGS)


def solution(mesh):
    return jax.shard_map(
        body,
        mesh=mesh,
        in_specs=(P("fibre", "tm"), P("tm"), P("fibre")),
        out_specs=P("tm", "fibre", None),
        check_vma=False,
    )
```

```python
import functools
import math

import jax
import jax.numpy as jnp
import numpy as np
from jax import lax
from jax.experimental import pallas as pl
from jax.experimental.pallas import tpu as pltpu
from jax.sharding import PartitionSpec as P

W = 2048
HOP = 1024
NB = 384
B0 = 20
SMOOTH = 64
LAGS = 256
LANE = 128
CUT = W + LANE
FOLD = W // 2
BINS = np.concatenate(
    [np.arange(0, 256, 2), np.arange(1, 256, 2), np.arange(256, NB, 2), np.arange(257, NB, 2)]
)


def taper_table():
    return (0.5 - 0.5 * np.cos(np.arange(W) * (2.0 * math.pi / W))).astype(np.float32)[None, :]


def half_tables():
    samples = np.arange(FOLD, dtype=np.int64)[:, None]

    def waves(bins):
        turns = (samples * (B0 + bins)[None, :] % W) * (2.0 * math.pi / W)
        return np.cos(turns), -np.sin(turns)

    even_cos, even_sin = waves(np.arange(0, NB, 2))
    odd_cos, odd_sin = waves(np.arange(1, NB, 2))
    cut = LANE
    columns = [
        even_cos[:, :cut], even_sin[:, :cut], even_cos[:, cut:], even_sin[:, cut:],
        odd_cos[:, :cut], odd_sin[:, :cut], odd_sin[:, cut:], odd_cos[:, cut:],
    ]
    return np.concatenate(columns, axis=1).astype(np.float32).astype(jnp.bfloat16)


def smoothing():
    rows = BINS[:, None]
    cols = BINS[None, :]
    first = np.clip(cols - SMOOTH // 2, 0, NB - SMOOTH)
    return np.where((rows >= first) & (rows < first + SMOOTH), 1.0 / SMOOTH, 0.0).astype(jnp.bfloat16)


def lag_table():
    shifts = np.arange(LAGS, dtype=np.int64) - LAGS // 2
    turns = ((B0 + BINS)[:, None] * shifts[None, :] % W) * (2.0 * math.pi / W)
    table = np.concatenate([np.cos(turns), -np.sin(turns)], axis=0)
    return table.astype(np.float32).astype(jnp.bfloat16)


def spectra_kernel(first, count, late, c_dev, n_src, n_after, *refs):
    if late:
        offs, sources, rec, halo, table_v, taper_v, smooth_v, before_r, before_s, *refs = refs
        out_r, out_s, out_all, *refs = refs[n_after:]
        sums, diffs, held, offs_v, sources_v, sems = refs
    else:
        offs, sources, rec, table, taper, smooth, *refs = refs
        out_r, out_mid, out_s, out_edge, table_v, taper_v, smooth_v, *refs = refs
        sums, diffs, held, offs_v, sources_v, sems = refs
    width = (count + 2) * HOP
    copies = []

    def fetch(source, target):
        copy = pltpu.make_async_copy(source, target, sems.at[len(copies)])
        copy.start()
        copies.append(copy)

    fetch(offs, offs_v)
    fetch(sources, sources_v)
    inside = width - (W if late else 0)
    for at in range(0, inside, inside // 2):
        fetch(rec.at[:, pl.ds(first * HOP + at, inside // 2)], held.at[:, pl.ds(at, inside // 2)])
    if late:
        held[:, inside:] = halo[...]
        ready = len(copies)
    else:
        fetch(taper, taper_v)
        ready = len(copies)
        rows = FOLD // 4
        for at in range(0, FOLD, rows):
            fetch(table.at[pl.ds(at, rows)], table_v.at[pl.ds(at, rows)])
        fetch(smooth, smooth_v)
        fetch(rec.at[:, pl.ds(0, W)], out_edge)
    for copy in copies[:ready]:
        copy.wait()

    lanes = lax.broadcasted_iota(jnp.int32, (c_dev, LANE), 1)

    def cut(slot):
        start = slot * HOP + offs_v[first + slot]
        rest = start % LANE
        keep = lanes < LANE - rest
        shift = (LANE - rest) % LANE
        chunk = held[:, pl.ds(pl.multiple_of(start // LANE * LANE, LANE), CUT)].astype(jnp.float32)
        turned = [pltpu.roll(chunk[:, i * LANE : (i + 1) * LANE], shift, 1) for i in range(CUT // LANE)]
        row = pl.ds(pl.multiple_of(slot * c_dev, c_dev), c_dev)
        tiles = FOLD // LANE
        for i in range(tiles):
            lo = slice(i * LANE, (i + 1) * LANE)
            hi = slice(FOLD + i * LANE, FOLD + (i + 1) * LANE)
            near = jnp.where(keep, turned[i], turned[i + 1]) * taper_v[:, lo]
            far = jnp.where(keep, turned[tiles + i], turned[tiles + i + 1]) * taper_v[:, hi]
            sums[row, lo] = (near + far).astype(jnp.bfloat16)
            diffs[row, lo] = (near - far).astype(jnp.bfloat16)

    pl.loop(0, count, unroll=4)(cut)
    for copy in copies[ready:]:
        copy.wait()

    split = 3 * LANE
    even = jnp.dot(sums[...], table_v[:, :split], preferred_element_type=jnp.float32)
    odd = jnp.dot(diffs[...], table_v[:, split:], preferred_element_type=jnp.float32)
    left = lax.broadcasted_iota(jnp.int32, (1, LANE), 1) < LANE // 2
    mixed_even, mixed_odd = even[:, 2 * LANE :], odd[:, 2 * LANE :]
    real = [even[:, :LANE], odd[:, :LANE], jnp.where(left, mixed_even, mixed_odd)]
    swapped = pltpu.roll(jnp.where(left, mixed_odd, mixed_even), LANE // 2, 1)
    imag = [even[:, LANE : 2 * LANE], odd[:, LANE : 2 * LANE], swapped]
    power = jnp.concatenate([r * r + i * i for r, i in zip(real, imag)], axis=1).astype(jnp.bfloat16)
    smoothed = jnp.dot(power, smooth_v[...], preferred_element_type=jnp.float32)
    factor = lax.rsqrt(smoothed + 1e-05)
    parts = [value * factor[:, i % 3 * LANE : (i % 3 + 1) * LANE] for i, value in enumerate(real + imag)]
    white = jnp.concatenate([part.astype(jnp.bfloat16) for part in parts], axis=1)
    if late:
        at = before_r.shape[0]
        out_r[:at] = before_r[...]
        out_r[at:] = white
    else:
        at = out_r.shape[0]
        out_r[...] = white[:at]
        out_mid[...] = white[at:]
    rows = lax.broadcasted_iota(jnp.int32, (n_src * count, 1), 0)
    cols = lax.broadcasted_iota(jnp.int32, (n_src * count, count * c_dev), 1)
    wanted = jnp.zeros_like(rows)
    for s in range(n_src):
        wanted = jnp.where(rows // count == s, sources_v[s] % c_dev + (rows % count) * c_dev, wanted)
    picker = jnp.where(cols == wanted, 1.0, 0.0).astype(jnp.bfloat16)
    out_s[...] = jnp.dot(picker, white, preferred_element_type=jnp.float32).astype(jnp.bfloat16)
    if late:
        at = before_s.shape[0]
        out_all[:at] = before_s[...]
        out_all[at:] = out_s[...]


def spectra_call(record, offsets, src_idx, tables, first, count, head=None, late=None, after=()):
    c_dev = record.shape[0]
    n_src = src_idx.shape[0]
    vmem = pl.BlockSpec(memory_space=pltpu.VMEM)
    hbm = pl.BlockSpec(memory_space=pltpu.HBM)
    arrays = [offsets, src_idx, record]
    if late is None:
        arrays += tables
    arrays = [pltpu.with_memory_space_constraint(a, pltpu.HBM) for a in arrays]
    specs = [hbm] * len(arrays)
    rows = [head, count - head] if late is None else [count + late[1].shape[0] // c_dev]
    out_shape = [jax.ShapeDtypeStruct((n * c_dev, 2 * NB), jnp.bfloat16) for n in rows]
    out_shape.append(jax.ShapeDtypeStruct((n_src * count, 2 * NB), jnp.bfloat16))
    if late is None:
        out_shape.append(jax.ShapeDtypeStruct((c_dev, W), record.dtype))
        out_shape += [jax.ShapeDtypeStruct(t.shape, t.dtype) for t in tables]
    else:
        halo, middle, sources = late
        arrays += [halo, *tables, middle, sources, *after]
        specs += [vmem] * 6 + [pl.BlockSpec(memory_space=pl.ANY)] * len(after)
        out_shape.append(jax.ShapeDtypeStruct((sources.shape[0] + n_src * count, 2 * NB), jnp.bfloat16))
    return pl.pallas_call(
        functools.partial(spectra_kernel, first, count, late is not None, c_dev, n_src, len(after)),
        out_shape=out_shape,
        in_specs=specs,
        out_specs=[vmem] * len(out_shape),
        scratch_shapes=[
            pltpu.VMEM((count * c_dev, FOLD), jnp.bfloat16),
            pltpu.VMEM((count * c_dev, FOLD), jnp.bfloat16),
            pltpu.VMEM((c_dev, (count + 2) * HOP), jnp.bfloat16),
            pltpu.SMEM(offsets.shape, jnp.int32),
            pltpu.SMEM(src_idx.shape, jnp.int32),
            pltpu.SemaphoreType.DMA((16,)),
        ],
        compiler_params=pltpu.CompilerParams(vmem_limit_bytes=24 << 20),
        cost_estimate=pl.CostEstimate(
            flops=int((1.5 + 0.1 * count) * 0.01e9), bytes_accessed=1 << 20, transcendentals=0
        ),
        name="spectra",
    )(*arrays)


def cross_kernel(runs, outs, counts, n_src, n_win, early, c_dev, scale, *refs):
    groups = []
    for count in counts:
        groups.append(refs[:count])
        refs = refs[count:]
    srcs, recs, befores, done, tables, _ = groups
    outputs, refs = refs[: len(outs)], refs[len(outs) :]
    wide = refs[0]
    span = n_src * n_win
    for k, src in enumerate(srcs):
        rows = slice(k * span, k * span + src.shape[1])
        real = src[0, :, :NB].astype(jnp.float32)
        imag = src[0, :, NB:].astype(jnp.float32)
        wide[rows, :NB] = real
        wide[rows, NB : 2 * NB] = real + imag
        wide[rows, 2 * NB :] = real - imag
    tiles = NB // LANE

    def run(step, first, wave, parts, before, target, offset):
        block = wave * n_src
        local = step // tiles * wave
        lo, hi, top = (
            pl.ds(pl.multiple_of(step % tiles * LANE + i * NB, LANE), LANE) for i in range(3)
        )
        src = wide.at[pl.ds(pl.multiple_of((first + local) * span, 8), wave * span)]

        def place(start, s):
            return pl.ds(pl.multiple_of(((start + local) * n_src + s) * c_dev, c_dev), c_dev)

        sums = [[jnp.zeros((c_dev, LANE), jnp.float32)] * 3 for _ in range(block)]
        for index, base, start, stop in parts:
            for w in range(start, stop):
                row = slice((w - base) * c_dev, (w - base + 1) * c_dev)
                rec_real = recs[index][row, lo].astype(jnp.float32)
                rec_imag = recs[index][row, hi].astype(jnp.float32)
                rec_both = rec_real + rec_imag
                for s in range(block):
                    at = s // n_src * span
                    if w < early:
                        at += s % n_src * early + w
                    else:
                        at += n_src * early + s % n_src * (n_win - early) + w - early
                    row = slice(at, at + 1)
                    both, plus, minus = sums[s]
                    sums[s] = [
                        both + src[row, lo] * rec_both,
                        plus + src[row, hi] * rec_real,
                        minus + src[row, top] * rec_imag,
                    ]
        for s in range(block):
            both, plus, minus = sums[s]
            real, imag = both - minus, both - plus
            if before is not None:
                real += befores[before[0]][place(before[1], s), lo]
                imag += befores[before[0]][place(before[1], s), hi]
            target[place(offset, s), lo] = real.astype(target.dtype)
            target[place(offset, s), hi] = imag.astype(target.dtype)

    lagged = 0
    for first, n_group, parts, before, place in runs:
        if place is None:
            target, offset = refs[1], lagged
            lagged += n_group
        else:
            target, offset = outputs[place[0]], place[1]
        wave = 8 // n_src if n_group * n_src % 8 == 0 and 8 % n_src == 0 else 1
        pl.loop(0, n_group // wave * tiles)(
            functools.partial(
                run, first=first, wave=wave, parts=parts, before=before, target=target, offset=offset
            )
        )

    if lagged:
        lags = jnp.dot(refs[1][...], tables[0][...], preferred_element_type=jnp.float32)
        lags = (lags * scale).astype(jnp.bfloat16)
        unit = n_src * c_dev
        start = 0
        for out, pieces in zip(outputs, outs):
            at = 0
            for piece in pieces or ():
                if isinstance(piece, str):
                    part = done[0][...]
                else:
                    part = lags[start * unit : (start + piece) * unit]
                    start += piece
                out[at : at + part.shape[0], :] = part
                at += part.shape[0]


def cross_call(srcs, recs, runs, outs, n_src, n_win, early, c_dev, scale, befores=(), done=(), ltab=None, after=()):
    grid = srcs[0].shape[0]
    unit = n_src * c_dev
    whole = pl.BlockSpec(memory_space=pltpu.VMEM)
    lists = [srcs, recs, befores, done, () if ltab is None else (ltab,), after]
    arrays = [a for some in lists for a in some]
    specs = [whole] * (len(arrays) - len(after)) + [pl.BlockSpec(memory_space=pl.ANY)] * len(after)
    shapes = []
    for out in outs:
        if isinstance(out, int):
            shapes.append(jax.ShapeDtypeStruct((out * unit, 2 * NB), jnp.float32))
        else:
            rows = sum(done[0].shape[0] if isinstance(p, str) else p * unit for p in out)
            shapes.append(jax.ShapeDtypeStruct((grid * rows, LAGS), jnp.bfloat16))
    out_specs = [whole] * len(shapes)
    if grid > 1:
        specs[: len(srcs)] = [pl.BlockSpec((1,) + a.shape[1:], lambda g: (g, 0, 0)) for a in srcs]
        out_specs = [pl.BlockSpec((s.shape[0] // grid, s.shape[1]), lambda g: (g, 0)) for s in shapes]
    scratch = [pltpu.VMEM((len(srcs) * n_src * n_win, 3 * NB), jnp.float32)]
    lagged = sum(n for _, n, _, _, place in runs if place is None)
    if lagged:
        scratch.append(pltpu.VMEM((lagged * unit, 2 * NB), jnp.bfloat16))
    pairs = sum(n * n_src * sum(p[3] - p[2] for p in parts) for _, n, parts, _, _ in runs)
    kept = [None if isinstance(out, int) else out for out in outs]
    return pl.pallas_call(
        functools.partial(
            cross_kernel, runs, kept, [len(some) for some in lists], n_src, n_win, early, c_dev, scale
        ),
        grid=() if grid == 1 else (grid,),
        out_shape=shapes,
        in_specs=specs,
        out_specs=out_specs,
        scratch_shapes=scratch,
        compiler_params=pltpu.CompilerParams(vmem_limit_bytes=24 << 20),
        cost_estimate=pl.CostEstimate(
            flops=int((0.4 + grid * pairs * 0.008) * 0.02e9), bytes_accessed=1 << 20, transcendentals=0
        ),
        name="cross",
    )(*arrays)


def join_kernel(*refs):
    *parts, out = refs
    at = 0
    for part in parts:
        out[at : at + part.shape[0]] = part[...]
        at += part.shape[0]


def join_call(*parts):
    rows = sum(part.shape[0] for part in parts)
    vmem = pl.BlockSpec(memory_space=pltpu.VMEM)
    return pl.pallas_call(
        join_kernel,
        out_shape=jax.ShapeDtypeStruct((rows, parts[0].shape[1]), parts[0].dtype),
        in_specs=[vmem] * len(parts),
        out_specs=vmem,
        cost_estimate=pl.CostEstimate(flops=1 << 20, bytes_accessed=1 << 19, transcendentals=0),
        name="join",
    )(*parts)


def body(record, offsets, src_idx):
    c_dev = record.shape[0]
    n_win = offsets.shape[0]
    n_src = src_idx.shape[0]
    n_tm = lax.axis_size("tm")
    n_fibre = lax.axis_size("fibre")
    n_group = n_fibre // 2
    fibre = lax.axis_index("fibre")
    tm = lax.axis_index("tm")
    head, early = n_win * 3 // 4, n_win * 7 // 8
    scale = 1.0 / math.sqrt(n_win * n_tm * NB)
    tables = [jnp.asarray(t) for t in (half_tables(), taper_table(), smoothing())]
    ltab = jnp.asarray(lag_table())
    direct = n_group == 4 and n_tm == 4

    def trade(array, by):
        return lax.ppermute(array, "fibre", [(i, i ^ by) for i in range(n_fibre)])

    rec_a, middle, src_a, edge, *tables = spectra_call(record, offsets, src_idx, tables, 0, early, head)
    far_a = trade(rec_a, 1)
    if direct:
        by_2a = trade(src_a, 4)
    halo = lax.ppermute(edge, "tm", [(i, i - 1) for i in range(1, n_tm)])
    cross = functools.partial(
        cross_call, n_src=n_src, n_win=n_win, early=early, c_dev=c_dev, scale=scale
    )
    late = (halo, middle, src_a)
    begun = []
    if direct:
        parts = [(0, 0, 0, head), (1, head, head, early)]
        begun = cross([src_a[None]], [rec_a, middle], [(0, 1, parts, None, (0, 0))], [1])
    rec_b, src_b, src = spectra_call(
        record, offsets, src_idx, tables, early, n_win - early, late=late, after=begun
    )
    far_b = trade(rec_b, 1)
    own = [(0, 0, 0, head), (1, head, head, n_win)]
    if direct:
        by_2 = join_call(by_2a, trade(src_b, 4))
        by_1 = trade(src, 2)
        by_3 = trade(by_2, 2)
        srcs = [part[None] for part in (src, by_1, by_2, by_3)]
        swapped = [(2, 0, 0, head)]
        runs = [
            (0, 1, [(1, head, early, n_win)], (0, 0), None),
            (1, 2, own, None, None),
            (0, 1, swapped, None, (1, 0)),
            (1, 2, swapped, None, (1, 1)),
        ]
        near, sums = cross(srcs[:3], [rec_a, rec_b, far_a], runs, [[1, 2], 3], befores=begun, ltab=ltab)
        swapped = [(3, head, head, n_win)]
        runs = [
            (0, 1, swapped, (0, 0), None),
            (1, 2, swapped, (0, 1), None),
            (3, 1, [(2, 0, 0, head)] + swapped, None, None),
            (3, 1, own, None, None),
        ]
        far, near = cross(
            srcs, [rec_a, rec_b, far_a, far_b], runs, [[1, 2, 1], ["done", 1]],
            befores=[sums], done=[near], ltab=ltab,
        )
    else:
        ranks = [[2 * j + p for j in range(n_group)] for p in range(2)]
        srcs = [lax.all_gather(src, "fibre", axis=0, axis_index_groups=ranks)]
        runs = [(0, 1, own, None, None)]
        near = cross(srcs, [rec_a, rec_b], runs, [[1]], ltab=ltab)[0]
        far = cross(srcs, [far_a, far_b], runs, [[1]], ltab=ltab)[0]
    near, far = (r.reshape(n_group, n_src, c_dev, LAGS) for r in (near, far))

    def piece(lagged, owner):
        if direct:
            return lax.dynamic_index_in_dim(lagged, (fibre // 2) ^ owner, 0, keepdims=True)
        share = n_group // n_tm
        return lax.dynamic_slice_in_dim(lagged, owner * share, share, 0)

    keep = jnp.stack([piece(r, tm ^ k) for r in (near, far) for k in range(0, n_tm, 2)])
    give = jnp.stack([piece(r, tm ^ k) for r in (near, far) for k in range(1, n_tm, 2)])
    got = lax.ppermute(give, "tm", [(i, i ^ 1) for i in range(n_tm)])
    pairs = keep.astype(jnp.float32) + got.astype(jnp.float32)
    totals = []
    for side in range(2):
        total = None
        for k in range(n_tm // 2):
            mine = pairs[side * (n_tm // 2) + k]
            if side or k:
                routes = [
                    (i * n_tm + t, (i ^ side) * n_tm + (t ^ (2 * k)))
                    for i in range(n_fibre)
                    for t in range(n_tm)
                ]
                mine = lax.ppermute(mine.astype(jnp.bfloat16), ("fibre", "tm"), routes)
                mine = mine.astype(jnp.float32)
            total = mine if total is None else total + mine
        totals.append(total)
    even = fibre % 2 == 0
    near, far = totals
    out = jnp.stack([jnp.where(even, near, far), jnp.where(even, far, near)], axis=1)
    return out.reshape(-1, c_dev, LAGS)


def solution(mesh):
    return jax.shard_map(
        body,
        mesh=mesh,
        in_specs=(P("fibre", "tm"), P("tm"), P("fibre")),
        out_specs=P("tm", "fibre", None),
        check_vma=False,
    )
```

```python
import functools
import math

import jax
import jax.numpy as jnp
import numpy as np
from jax import lax
from jax.experimental import pallas as pl
from jax.experimental.pallas import tpu as pltpu
from jax.sharding import PartitionSpec as P

W = 2048
HOP = 1024
NB = 384
B0 = 20
SMOOTH = 64
LAGS = 256
LANE = 128
CUT = W + LANE
FOLD = W // 2
BINS = np.concatenate(
    [np.arange(0, 256, 2), np.arange(1, 256, 2), np.arange(256, NB, 2), np.arange(257, NB, 2)]
)


def taper_table():
    return (0.5 - 0.5 * np.cos(np.arange(W) * (2.0 * math.pi / W))).astype(np.float32)[None, :]


def half_tables():
    samples = np.arange(FOLD, dtype=np.int64)[:, None]

    def waves(bins):
        turns = (samples * (B0 + bins)[None, :] % W) * (2.0 * math.pi / W)
        return np.cos(turns), -np.sin(turns)

    even_cos, even_sin = waves(np.arange(0, NB, 2))
    odd_cos, odd_sin = waves(np.arange(1, NB, 2))
    cut = LANE
    columns = [
        even_cos[:, :cut], even_sin[:, :cut], even_cos[:, cut:], even_sin[:, cut:],
        odd_cos[:, :cut], odd_sin[:, :cut], odd_sin[:, cut:], odd_cos[:, cut:],
    ]
    return np.concatenate(columns, axis=1).astype(np.float32).astype(jnp.bfloat16)


def smoothing():
    rows = BINS[:, None]
    cols = BINS[None, :]
    first = np.clip(cols - SMOOTH // 2, 0, NB - SMOOTH)
    return np.where((rows >= first) & (rows < first + SMOOTH), 1.0 / SMOOTH, 0.0).astype(jnp.bfloat16)


def lag_table():
    shifts = np.arange(LAGS, dtype=np.int64) - LAGS // 2
    turns = ((B0 + BINS)[:, None] * shifts[None, :] % W) * (2.0 * math.pi / W)
    table = np.concatenate([np.cos(turns), -np.sin(turns)], axis=0)
    return table.astype(np.float32).astype(jnp.bfloat16)


def spectra_kernel(first, count, late, c_dev, n_src, n_after, *refs):
    if late:
        offs, sources, rec, halo, table_v, taper_v, smooth_v, before_r, before_s, *refs = refs
        out_r, out_s, out_all, *refs = refs[n_after:]
        sums, diffs, held, offs_v, sources_v, sems = refs
    else:
        offs, sources, rec, table, taper, smooth, *refs = refs
        out_r, out_mid, out_s, out_edge, table_v, taper_v, smooth_v, *refs = refs
        sums, diffs, held, offs_v, sources_v, sems = refs
    width = (count + 2) * HOP
    copies = []

    def fetch(source, target):
        copy = pltpu.make_async_copy(source, target, sems.at[len(copies)])
        copy.start()
        copies.append(copy)

    fetch(offs, offs_v)
    fetch(sources, sources_v)
    inside = width - (W if late else 0)
    for at in range(0, inside, inside // 2):
        fetch(rec.at[:, pl.ds(first * HOP + at, inside // 2)], held.at[:, pl.ds(at, inside // 2)])
    if late:
        held[:, inside:] = halo[...]
        ready = len(copies)
    else:
        fetch(taper, taper_v)
        ready = len(copies)
        rows = FOLD // 4
        for at in range(0, FOLD, rows):
            fetch(table.at[pl.ds(at, rows)], table_v.at[pl.ds(at, rows)])
        fetch(smooth, smooth_v)
        fetch(rec.at[:, pl.ds(0, W)], out_edge)
    for copy in copies[:ready]:
        copy.wait()

    lanes = lax.broadcasted_iota(jnp.int32, (c_dev, LANE), 1)

    def cut(slot):
        start = slot * HOP + offs_v[first + slot]
        rest = start % LANE
        keep = lanes < LANE - rest
        shift = (LANE - rest) % LANE
        chunk = held[:, pl.ds(pl.multiple_of(start // LANE * LANE, LANE), CUT)].astype(jnp.float32)
        turned = [pltpu.roll(chunk[:, i * LANE : (i + 1) * LANE], shift, 1) for i in range(CUT // LANE)]
        row = pl.ds(pl.multiple_of(slot * c_dev, c_dev), c_dev)
        tiles = FOLD // LANE
        for i in range(tiles):
            lo = slice(i * LANE, (i + 1) * LANE)
            hi = slice(FOLD + i * LANE, FOLD + (i + 1) * LANE)
            near = jnp.where(keep, turned[i], turned[i + 1]) * taper_v[:, lo]
            far = jnp.where(keep, turned[tiles + i], turned[tiles + i + 1]) * taper_v[:, hi]
            sums[row, lo] = (near + far).astype(jnp.bfloat16)
            diffs[row, lo] = (near - far).astype(jnp.bfloat16)

    pl.loop(0, count, unroll=4)(cut)
    for copy in copies[ready:]:
        copy.wait()

    split = 3 * LANE
    even = jnp.dot(sums[...], table_v[:, :split], preferred_element_type=jnp.float32)
    odd = jnp.dot(diffs[...], table_v[:, split:], preferred_element_type=jnp.float32)
    left = lax.broadcasted_iota(jnp.int32, (1, LANE), 1) < LANE // 2
    mixed_even, mixed_odd = even[:, 2 * LANE :], odd[:, 2 * LANE :]
    real = [even[:, :LANE], odd[:, :LANE], jnp.where(left, mixed_even, mixed_odd)]
    swapped = pltpu.roll(jnp.where(left, mixed_odd, mixed_even), LANE // 2, 1)
    imag = [even[:, LANE : 2 * LANE], odd[:, LANE : 2 * LANE], swapped]
    power = jnp.concatenate([r * r + i * i for r, i in zip(real, imag)], axis=1).astype(jnp.bfloat16)
    smoothed = jnp.dot(power, smooth_v[...], preferred_element_type=jnp.float32)
    factor = lax.rsqrt(smoothed + 1e-05)
    parts = [value * factor[:, i % 3 * LANE : (i % 3 + 1) * LANE] for i, value in enumerate(real + imag)]
    white = jnp.concatenate([part.astype(jnp.bfloat16) for part in parts], axis=1)
    if late:
        at = before_r.shape[0]
        out_r[:at] = before_r[...]
        out_r[at:] = white
    else:
        at = out_r.shape[0]
        out_r[...] = white[:at]
        out_mid[...] = white[at:]
    rows = lax.broadcasted_iota(jnp.int32, (n_src * count, 1), 0)
    cols = lax.broadcasted_iota(jnp.int32, (n_src * count, count * c_dev), 1)
    wanted = jnp.zeros_like(rows)
    for s in range(n_src):
        wanted = jnp.where(rows // count == s, sources_v[s] % c_dev + (rows % count) * c_dev, wanted)
    picker = jnp.where(cols == wanted, 1.0, 0.0).astype(jnp.bfloat16)
    out_s[...] = jnp.dot(picker, white, preferred_element_type=jnp.float32).astype(jnp.bfloat16)
    if late:
        at = before_s.shape[0]
        out_all[:at] = before_s[...]
        out_all[at:] = out_s[...]


def spectra_call(record, offsets, src_idx, tables, first, count, head=None, late=None, after=()):
    c_dev = record.shape[0]
    n_src = src_idx.shape[0]
    vmem = pl.BlockSpec(memory_space=pltpu.VMEM)
    hbm = pl.BlockSpec(memory_space=pltpu.HBM)
    arrays = [offsets, src_idx, record]
    if late is None:
        arrays += tables
    arrays = [pltpu.with_memory_space_constraint(a, pltpu.HBM) for a in arrays]
    specs = [hbm] * len(arrays)
    rows = [head, count - head] if late is None else [count + late[1].shape[0] // c_dev]
    out_shape = [jax.ShapeDtypeStruct((n * c_dev, 2 * NB), jnp.bfloat16) for n in rows]
    out_shape.append(jax.ShapeDtypeStruct((n_src * count, 2 * NB), jnp.bfloat16))
    if late is None:
        out_shape.append(jax.ShapeDtypeStruct((c_dev, W), record.dtype))
        out_shape += [jax.ShapeDtypeStruct(t.shape, t.dtype) for t in tables]
    else:
        halo, middle, sources = late
        arrays += [halo, *tables, middle, sources, *after]
        specs += [vmem] * 6 + [pl.BlockSpec(memory_space=pl.ANY)] * len(after)
        out_shape.append(jax.ShapeDtypeStruct((sources.shape[0] + n_src * count, 2 * NB), jnp.bfloat16))
    return pl.pallas_call(
        functools.partial(spectra_kernel, first, count, late is not None, c_dev, n_src, len(after)),
        out_shape=out_shape,
        in_specs=specs,
        out_specs=[vmem] * len(out_shape),
        scratch_shapes=[
            pltpu.VMEM((count * c_dev, FOLD), jnp.bfloat16),
            pltpu.VMEM((count * c_dev, FOLD), jnp.bfloat16),
            pltpu.VMEM((c_dev, (count + 2) * HOP), jnp.bfloat16),
            pltpu.SMEM(offsets.shape, jnp.int32),
            pltpu.SMEM(src_idx.shape, jnp.int32),
            pltpu.SemaphoreType.DMA((16,)),
        ],
        compiler_params=pltpu.CompilerParams(vmem_limit_bytes=24 << 20),
        cost_estimate=pl.CostEstimate(
            flops=int((1.5 + 0.1 * count) * 0.01e9), bytes_accessed=1 << 20, transcendentals=0
        ),
        name="spectra",
    )(*arrays)


def cross_kernel(runs, outs, counts, n_src, n_win, early, c_dev, scale, *refs):
    groups = []
    for count in counts:
        groups.append(refs[:count])
        refs = refs[count:]
    srcs, recs, befores, done, tables, _ = groups
    outputs, refs = refs[: len(outs)], refs[len(outs) :]
    wide = refs[0]
    span = n_src * n_win
    for k, src in enumerate(srcs):
        rows = slice(k * span, k * span + src.shape[1])
        real = src[0, :, :NB].astype(jnp.float32)
        imag = src[0, :, NB:].astype(jnp.float32)
        wide[rows, :NB] = real
        wide[rows, NB : 2 * NB] = real + imag
        wide[rows, 2 * NB :] = real - imag
    tiles = NB // LANE

    def run(step, first, wave, parts, before, target, offset):
        block = wave * n_src
        local = step // tiles * wave
        lo, hi, top = (
            pl.ds(pl.multiple_of(step % tiles * LANE + i * NB, LANE), LANE) for i in range(3)
        )
        src = wide.at[pl.ds(pl.multiple_of((first + local) * span, 8), wave * span)]

        def place(start, s):
            return pl.ds(pl.multiple_of(((start + local) * n_src + s) * c_dev, c_dev), c_dev)

        sums = [[jnp.zeros((c_dev, LANE), jnp.float32)] * 3 for _ in range(block)]
        for index, base, start, stop in parts:
            for w in range(start, stop):
                row = slice((w - base) * c_dev, (w - base + 1) * c_dev)
                rec_real = recs[index][row, lo].astype(jnp.float32)
                rec_imag = recs[index][row, hi].astype(jnp.float32)
                rec_both = rec_real + rec_imag
                for s in range(block):
                    at = s // n_src * span
                    if w < early:
                        at += s % n_src * early + w
                    else:
                        at += n_src * early + s % n_src * (n_win - early) + w - early
                    row = slice(at, at + 1)
                    both, plus, minus = sums[s]
                    sums[s] = [
                        both + src[row, lo] * rec_both,
                        plus + src[row, hi] * rec_real,
                        minus + src[row, top] * rec_imag,
                    ]
        for s in range(block):
            both, plus, minus = sums[s]
            real, imag = both - minus, both - plus
            if before is not None:
                real += befores[before[0]][place(before[1], s), lo]
                imag += befores[before[0]][place(before[1], s), hi]
            target[place(offset, s), lo] = real.astype(target.dtype)
            target[place(offset, s), hi] = imag.astype(target.dtype)

    lagged = 0
    for first, n_group, parts, before, place in runs:
        if place is None:
            target, offset = refs[1], lagged
            lagged += n_group
        else:
            target, offset = outputs[place[0]], place[1]
        wave = 8 // n_src if n_group * n_src % 8 == 0 and 8 % n_src == 0 else 1
        pl.loop(0, n_group // wave * tiles)(
            functools.partial(
                run, first=first, wave=wave, parts=parts, before=before, target=target, offset=offset
            )
        )

    if lagged:
        lags = jnp.dot(refs[1][...], tables[0][...], preferred_element_type=jnp.float32)
        lags = (lags * scale).astype(jnp.bfloat16)
        unit = n_src * c_dev
        start = 0
        for out, pieces in zip(outputs, outs):
            at = 0
            for piece in pieces or ():
                if isinstance(piece, str):
                    part = done[0][...]
                else:
                    part = lags[start * unit : (start + piece) * unit]
                    start += piece
                out[at : at + part.shape[0], :] = part
                at += part.shape[0]


def cross_call(srcs, recs, runs, outs, n_src, n_win, early, c_dev, scale, befores=(), done=(), ltab=None, after=()):
    grid = srcs[0].shape[0]
    unit = n_src * c_dev
    whole = pl.BlockSpec(memory_space=pltpu.VMEM)
    lists = [srcs, recs, befores, done, () if ltab is None else (ltab,), after]
    arrays = [a for some in lists for a in some]
    specs = [whole] * (len(arrays) - len(after)) + [pl.BlockSpec(memory_space=pl.ANY)] * len(after)
    shapes = []
    for out in outs:
        if isinstance(out, int):
            shapes.append(jax.ShapeDtypeStruct((out * unit, 2 * NB), jnp.float32))
        else:
            rows = sum(done[0].shape[0] if isinstance(p, str) else p * unit for p in out)
            shapes.append(jax.ShapeDtypeStruct((grid * rows, LAGS), jnp.bfloat16))
    out_specs = [whole] * len(shapes)
    if grid > 1:
        specs[: len(srcs)] = [pl.BlockSpec((1,) + a.shape[1:], lambda g: (g, 0, 0)) for a in srcs]
        out_specs = [pl.BlockSpec((s.shape[0] // grid, s.shape[1]), lambda g: (g, 0)) for s in shapes]
    scratch = [pltpu.VMEM((len(srcs) * n_src * n_win, 3 * NB), jnp.float32)]
    lagged = sum(n for _, n, _, _, place in runs if place is None)
    if lagged:
        scratch.append(pltpu.VMEM((lagged * unit, 2 * NB), jnp.bfloat16))
    pairs = sum(n * n_src * sum(p[3] - p[2] for p in parts) for _, n, parts, _, _ in runs)
    kept = [None if isinstance(out, int) else out for out in outs]
    return pl.pallas_call(
        functools.partial(
            cross_kernel, runs, kept, [len(some) for some in lists], n_src, n_win, early, c_dev, scale
        ),
        grid=() if grid == 1 else (grid,),
        out_shape=shapes,
        in_specs=specs,
        out_specs=out_specs,
        scratch_shapes=scratch,
        compiler_params=pltpu.CompilerParams(vmem_limit_bytes=24 << 20),
        cost_estimate=pl.CostEstimate(
            flops=int((0.4 + grid * pairs * 0.008) * 0.02e9), bytes_accessed=1 << 20, transcendentals=0
        ),
        name="cross",
    )(*arrays)


def join_kernel(*refs):
    *parts, out = refs
    at = 0
    for part in parts:
        out[at : at + part.shape[0]] = part[...]
        at += part.shape[0]


def join_call(*parts):
    rows = sum(part.shape[0] for part in parts)
    vmem = pl.BlockSpec(memory_space=pltpu.VMEM)
    return pl.pallas_call(
        join_kernel,
        out_shape=jax.ShapeDtypeStruct((rows, parts[0].shape[1]), parts[0].dtype),
        in_specs=[vmem] * len(parts),
        out_specs=vmem,
        compiler_params=pltpu.CompilerParams(vmem_limit_bytes=4 << 20),
        cost_estimate=pl.CostEstimate(flops=1 << 20, bytes_accessed=1 << 19, transcendentals=0),
        name="join",
    )(*parts)


def body(record, offsets, src_idx):
    c_dev = record.shape[0]
    n_win = offsets.shape[0]
    n_src = src_idx.shape[0]
    n_tm = lax.axis_size("tm")
    n_fibre = lax.axis_size("fibre")
    n_group = n_fibre // 2
    fibre = lax.axis_index("fibre")
    tm = lax.axis_index("tm")
    head, early = n_win * 3 // 4, n_win * 7 // 8
    scale = 1.0 / math.sqrt(n_win * n_tm * NB)
    tables = [jnp.asarray(t) for t in (half_tables(), taper_table(), smoothing())]
    ltab = jnp.asarray(lag_table())
    direct = n_group == 4 and n_tm == 4

    def trade(array, by):
        return lax.ppermute(array, "fibre", [(i, i ^ by) for i in range(n_fibre)])

    rec_a, middle, src_a, edge, *tables = spectra_call(record, offsets, src_idx, tables, 0, early, head)
    far_a = trade(rec_a, 1)
    if direct:
        by_2a = trade(src_a, 4)
    halo = lax.ppermute(edge, "tm", [(i, i - 1) for i in range(1, n_tm)])
    cross = functools.partial(
        cross_call, n_src=n_src, n_win=n_win, early=early, c_dev=c_dev, scale=scale
    )
    late = (halo, middle, src_a)
    begun = []
    if direct:
        parts = [(0, 0, 0, head), (1, head, head, early)]
        begun = cross([src_a[None]], [rec_a, middle], [(0, 1, parts, None, (0, 0))], [1])
    rec_b, src_b, src = spectra_call(
        record, offsets, src_idx, tables, early, n_win - early, late=late, after=begun
    )
    far_b = trade(rec_b, 1)
    own = [(0, 0, 0, head), (1, head, head, n_win)]
    if direct:
        by_2 = join_call(by_2a, trade(src_b, 4))
        by_1 = trade(src, 2)
        by_3 = trade(by_2, 2)
        srcs = [part[None] for part in (src, by_1, by_2, by_3)]
        swapped = [(2, 0, 0, head)]
        runs = [
            (0, 1, [(1, head, early, n_win)], (0, 0), None),
            (1, 2, own, None, None),
            (0, 1, swapped, None, (1, 0)),
            (1, 2, swapped, None, (1, 1)),
        ]
        near, sums = cross(srcs[:3], [rec_a, rec_b, far_a], runs, [[1, 2], 3], befores=begun, ltab=ltab)
        swapped = [(3, head, head, n_win)]
        runs = [
            (0, 1, swapped, (0, 0), None),
            (1, 2, swapped, (0, 1), None),
            (3, 1, [(2, 0, 0, head)] + swapped, None, None),
            (3, 1, own, None, None),
        ]
        far, near = cross(
            srcs, [rec_a, rec_b, far_a, far_b], runs, [[1, 2, 1], ["done", 1]],
            befores=[sums], done=[near], ltab=ltab,
        )
    else:
        ranks = [[2 * j + p for j in range(n_group)] for p in range(2)]
        srcs = [lax.all_gather(src, "fibre", axis=0, axis_index_groups=ranks)]
        runs = [(0, 1, own, None, None)]
        near = cross(srcs, [rec_a, rec_b], runs, [[1]], ltab=ltab)[0]
        far = cross(srcs, [far_a, far_b], runs, [[1]], ltab=ltab)[0]
    near, far = (r.reshape(n_group, n_src, c_dev, LAGS) for r in (near, far))

    def piece(lagged, owner):
        if direct:
            return lax.dynamic_index_in_dim(lagged, (fibre // 2) ^ owner, 0, keepdims=True)
        share = n_group // n_tm
        return lax.dynamic_slice_in_dim(lagged, owner * share, share, 0)

    keep = jnp.stack([piece(r, tm ^ k) for r in (near, far) for k in range(0, n_tm, 2)])
    give = jnp.stack([piece(r, tm ^ k) for r in (near, far) for k in range(1, n_tm, 2)])
    got = lax.ppermute(give, "tm", [(i, i ^ 1) for i in range(n_tm)])
    pairs = keep.astype(jnp.float32) + got.astype(jnp.float32)
    totals = []
    for side in range(2):
        total = None
        for k in range(n_tm // 2):
            mine = pairs[side * (n_tm // 2) + k]
            if side or k:
                routes = [
                    (i * n_tm + t, (i ^ side) * n_tm + (t ^ (2 * k)))
                    for i in range(n_fibre)
                    for t in range(n_tm)
                ]
                mine = lax.ppermute(mine.astype(jnp.bfloat16), ("fibre", "tm"), routes)
                mine = mine.astype(jnp.float32)
            total = mine if total is None else total + mine
        totals.append(total)
    even = fibre % 2 == 0
    near, far = totals
    out = jnp.stack([jnp.where(even, near, far), jnp.where(even, far, near)], axis=1)
    return out.reshape(-1, c_dev, LAGS)


def solution(mesh):
    return jax.shard_map(
        body,
        mesh=mesh,
        in_specs=(P("fibre", "tm"), P("tm"), P("fibre")),
        out_specs=P("tm", "fibre", None),
        check_vma=False,
    )
```

```python
import functools
import math

import jax
import jax.numpy as jnp
import numpy as np
from jax import lax
from jax.experimental import pallas as pl
from jax.experimental.pallas import tpu as pltpu
from jax.sharding import PartitionSpec as P

W = 2048
HOP = 1024
NB = 384
B0 = 20
SMOOTH = 64
LAGS = 256
LANE = 128
CUT = W + LANE
FOLD = W // 2
BINS = np.concatenate(
    [np.arange(0, 256, 2), np.arange(1, 256, 2), np.arange(256, NB, 2), np.arange(257, NB, 2)]
)


def taper_table():
    return (0.5 - 0.5 * np.cos(np.arange(W) * (2.0 * math.pi / W))).astype(np.float32)[None, :]


def half_tables():
    samples = np.arange(FOLD, dtype=np.int64)[:, None]

    def waves(bins):
        turns = (samples * (B0 + bins)[None, :] % W) * (2.0 * math.pi / W)
        return np.cos(turns), -np.sin(turns)

    even_cos, even_sin = waves(np.arange(0, NB, 2))
    odd_cos, odd_sin = waves(np.arange(1, NB, 2))
    cut = LANE
    columns = [
        even_cos[:, :cut], even_sin[:, :cut], even_cos[:, cut:], even_sin[:, cut:],
        odd_cos[:, :cut], odd_sin[:, :cut], odd_sin[:, cut:], odd_cos[:, cut:],
    ]
    return np.concatenate(columns, axis=1).astype(np.float32).astype(jnp.bfloat16)


def smoothing():
    rows = BINS[:, None]
    cols = BINS[None, :]
    first = np.clip(cols - SMOOTH // 2, 0, NB - SMOOTH)
    return np.where((rows >= first) & (rows < first + SMOOTH), 1.0 / SMOOTH, 0.0).astype(jnp.bfloat16)


def lag_table():
    shifts = np.arange(LAGS, dtype=np.int64) - LAGS // 2
    turns = ((B0 + BINS)[:, None] * shifts[None, :] % W) * (2.0 * math.pi / W)
    table = np.concatenate([np.cos(turns), -np.sin(turns)], axis=0)
    return table.astype(np.float32).astype(jnp.bfloat16)


def spectra_kernel(first, count, late, c_dev, n_src, n_after, *refs):
    if late:
        offs, sources, rec, halo, table_v, taper_v, smooth_v, before_r, before_s, *refs = refs
        out_r, out_s, out_all, *refs = refs[n_after:]
        sums, diffs, held, offs_v, sources_v, sems = refs
    else:
        offs, sources, rec, table, taper, smooth, *refs = refs
        out_r, out_mid, out_s, out_edge, table_v, taper_v, smooth_v, *refs = refs
        sums, diffs, held, offs_v, sources_v, sems = refs
    width = (count + 2) * HOP
    copies = []

    def fetch(source, target):
        copy = pltpu.make_async_copy(source, target, sems.at[len(copies)])
        copy.start()
        copies.append(copy)

    fetch(offs, offs_v)
    fetch(sources, sources_v)
    inside = width - (W if late else 0)
    for at in range(0, inside, inside // 2):
        fetch(rec.at[:, pl.ds(first * HOP + at, inside // 2)], held.at[:, pl.ds(at, inside // 2)])
    if late:
        held[:, inside:] = halo[...]
        ready = len(copies)
    else:
        fetch(taper, taper_v)
        ready = len(copies)
        rows = FOLD // 4
        for at in range(0, FOLD, rows):
            fetch(table.at[pl.ds(at, rows)], table_v.at[pl.ds(at, rows)])
        fetch(smooth, smooth_v)
        fetch(rec.at[:, pl.ds(0, W)], out_edge)
    for copy in copies[:ready]:
        copy.wait()

    lanes = lax.broadcasted_iota(jnp.int32, (c_dev, LANE), 1)

    def cut(slot):
        start = slot * HOP + offs_v[first + slot]
        rest = start % LANE
        keep = lanes < LANE - rest
        shift = (LANE - rest) % LANE
        chunk = held[:, pl.ds(pl.multiple_of(start // LANE * LANE, LANE), CUT)].astype(jnp.float32)
        turned = [pltpu.roll(chunk[:, i * LANE : (i + 1) * LANE], shift, 1) for i in range(CUT // LANE)]
        row = pl.ds(pl.multiple_of(slot * c_dev, c_dev), c_dev)
        tiles = FOLD // LANE
        for i in range(tiles):
            lo = slice(i * LANE, (i + 1) * LANE)
            hi = slice(FOLD + i * LANE, FOLD + (i + 1) * LANE)
            near = jnp.where(keep, turned[i], turned[i + 1]) * taper_v[:, lo]
            far = jnp.where(keep, turned[tiles + i], turned[tiles + i + 1]) * taper_v[:, hi]
            sums[row, lo] = (near + far).astype(jnp.bfloat16)
            diffs[row, lo] = (near - far).astype(jnp.bfloat16)

    pl.loop(0, count, unroll=4)(cut)
    for copy in copies[ready:]:
        copy.wait()

    split = 3 * LANE
    even = jnp.dot(sums[...], table_v[:, :split], preferred_element_type=jnp.float32)
    odd = jnp.dot(diffs[...], table_v[:, split:], preferred_element_type=jnp.float32)
    left = lax.broadcasted_iota(jnp.int32, (1, LANE), 1) < LANE // 2
    mixed_even, mixed_odd = even[:, 2 * LANE :], odd[:, 2 * LANE :]
    real = [even[:, :LANE], odd[:, :LANE], jnp.where(left, mixed_even, mixed_odd)]
    swapped = pltpu.roll(jnp.where(left, mixed_odd, mixed_even), LANE // 2, 1)
    imag = [even[:, LANE : 2 * LANE], odd[:, LANE : 2 * LANE], swapped]
    power = jnp.concatenate([r * r + i * i for r, i in zip(real, imag)], axis=1).astype(jnp.bfloat16)
    smoothed = jnp.dot(power, smooth_v[...], preferred_element_type=jnp.float32)
    factor = lax.rsqrt(smoothed + 1e-05)
    parts = [value * factor[:, i % 3 * LANE : (i % 3 + 1) * LANE] for i, value in enumerate(real + imag)]
    white = jnp.concatenate([part.astype(jnp.bfloat16) for part in parts], axis=1)
    if late:
        at = before_r.shape[0]
        out_r[:at] = before_r[...]
        out_r[at:] = white
    else:
        at = out_r.shape[0]
        out_r[...] = white[:at]
        out_mid[...] = white[at:]
    rows = lax.broadcasted_iota(jnp.int32, (n_src * count, 1), 0)
    cols = lax.broadcasted_iota(jnp.int32, (n_src * count, count * c_dev), 1)
    wanted = jnp.zeros_like(rows)
    for s in range(n_src):
        wanted = jnp.where(rows // count == s, sources_v[s] % c_dev + (rows % count) * c_dev, wanted)
    picker = jnp.where(cols == wanted, 1.0, 0.0).astype(jnp.bfloat16)
    out_s[...] = jnp.dot(picker, white, preferred_element_type=jnp.float32).astype(jnp.bfloat16)
    if late:
        at = before_s.shape[0]
        out_all[:at] = before_s[...]
        out_all[at:] = out_s[...]


def spectra_call(record, offsets, src_idx, tables, first, count, head=None, late=None, after=()):
    c_dev = record.shape[0]
    n_src = src_idx.shape[0]
    vmem = pl.BlockSpec(memory_space=pltpu.VMEM)
    hbm = pl.BlockSpec(memory_space=pltpu.HBM)
    arrays = [offsets, src_idx, record]
    if late is None:
        arrays += tables
    arrays = [pltpu.with_memory_space_constraint(a, pltpu.HBM) for a in arrays]
    specs = [hbm] * len(arrays)
    rows = [head, count - head] if late is None else [count + late[1].shape[0] // c_dev]
    out_shape = [jax.ShapeDtypeStruct((n * c_dev, 2 * NB), jnp.bfloat16) for n in rows]
    out_shape.append(jax.ShapeDtypeStruct((n_src * count, 2 * NB), jnp.bfloat16))
    if late is None:
        out_shape.append(jax.ShapeDtypeStruct((c_dev, W), record.dtype))
        out_shape += [jax.ShapeDtypeStruct(t.shape, t.dtype) for t in tables]
    else:
        halo, middle, sources = late
        arrays += [halo, *tables, middle, sources, *after]
        specs += [vmem] * 6 + [pl.BlockSpec(memory_space=pl.ANY)] * len(after)
        out_shape.append(jax.ShapeDtypeStruct((sources.shape[0] + n_src * count, 2 * NB), jnp.bfloat16))
    return pl.pallas_call(
        functools.partial(spectra_kernel, first, count, late is not None, c_dev, n_src, len(after)),
        out_shape=out_shape,
        in_specs=specs,
        out_specs=[vmem] * len(out_shape),
        scratch_shapes=[
            pltpu.VMEM((count * c_dev, FOLD), jnp.bfloat16),
            pltpu.VMEM((count * c_dev, FOLD), jnp.bfloat16),
            pltpu.VMEM((c_dev, (count + 2) * HOP), jnp.bfloat16),
            pltpu.SMEM(offsets.shape, jnp.int32),
            pltpu.SMEM(src_idx.shape, jnp.int32),
            pltpu.SemaphoreType.DMA((16,)),
        ],
        compiler_params=pltpu.CompilerParams(vmem_limit_bytes=24 << 20),
        cost_estimate=pl.CostEstimate(
            flops=int((1.5 + 0.1 * count) * 0.01e9), bytes_accessed=1 << 20, transcendentals=0
        ),
        name="spectra",
    )(*arrays)


def cross_kernel(runs, outs, counts, n_src, n_win, early, c_dev, scale, *refs):
    groups = []
    for count in counts:
        groups.append(refs[:count])
        refs = refs[count:]
    srcs, recs, befores, done, tables, _ = groups
    outputs, refs = refs[: len(outs)], refs[len(outs) :]
    wide = refs[0]
    span = n_src * n_win
    for k, src in enumerate(srcs):
        rows = slice(k * span, k * span + src.shape[1])
        real = src[0, :, :NB].astype(jnp.float32)
        imag = src[0, :, NB:].astype(jnp.float32)
        wide[rows, :NB] = real
        wide[rows, NB : 2 * NB] = real + imag
        wide[rows, 2 * NB :] = real - imag
    tiles = NB // LANE

    def run(step, first, wave, parts, before, target, offset):
        block = wave * n_src
        local = step // tiles * wave
        lo, hi, top = (
            pl.ds(pl.multiple_of(step % tiles * LANE + i * NB, LANE), LANE) for i in range(3)
        )
        src = wide.at[pl.ds(pl.multiple_of((first + local) * span, 8), wave * span)]

        def place(start, s):
            return pl.ds(pl.multiple_of(((start + local) * n_src + s) * c_dev, c_dev), c_dev)

        sums = [[jnp.zeros((c_dev, LANE), jnp.float32)] * 3 for _ in range(block)]
        for index, base, start, stop in parts:
            for w in range(start, stop):
                row = slice((w - base) * c_dev, (w - base + 1) * c_dev)
                rec_real = recs[index][row, lo].astype(jnp.float32)
                rec_imag = recs[index][row, hi].astype(jnp.float32)
                rec_both = rec_real + rec_imag
                for s in range(block):
                    at = s // n_src * span
                    if w < early:
                        at += s % n_src * early + w
                    else:
                        at += n_src * early + s % n_src * (n_win - early) + w - early
                    row = slice(at, at + 1)
                    both, plus, minus = sums[s]
                    sums[s] = [
                        both + src[row, lo] * rec_both,
                        plus + src[row, hi] * rec_real,
                        minus + src[row, top] * rec_imag,
                    ]
        for s in range(block):
            both, plus, minus = sums[s]
            real, imag = both - minus, both - plus
            if before is not None:
                real += befores[before[0]][place(before[1], s), lo]
                imag += befores[before[0]][place(before[1], s), hi]
            target[place(offset, s), lo] = real.astype(target.dtype)
            target[place(offset, s), hi] = imag.astype(target.dtype)

    lagged = 0
    for first, n_group, parts, before, place in runs:
        if place is None:
            target, offset = refs[1], lagged
            lagged += n_group
        else:
            target, offset = outputs[place[0]], place[1]
        wave = 8 // n_src if n_group * n_src % 8 == 0 and 8 % n_src == 0 else 1
        pl.loop(0, n_group // wave * tiles)(
            functools.partial(
                run, first=first, wave=wave, parts=parts, before=before, target=target, offset=offset
            )
        )

    if lagged:
        lags = jnp.dot(refs[1][...], tables[0][...], preferred_element_type=jnp.float32)
        lags = (lags * scale).astype(jnp.bfloat16)
        unit = n_src * c_dev
        start, done = 0, list(done)
        for out, pieces in zip(outputs, outs):
            at = 0
            for piece in pieces or ():
                if isinstance(piece, str):
                    part = done.pop(0)[...]
                else:
                    part = lags[start * unit : (start + piece) * unit]
                    start += piece
                out[at : at + part.shape[0], :] = part
                at += part.shape[0]


def cross_call(srcs, recs, runs, outs, n_src, n_win, early, c_dev, scale, befores=(), done=(), ltab=None, after=()):
    grid = srcs[0].shape[0]
    unit = n_src * c_dev
    whole = pl.BlockSpec(memory_space=pltpu.VMEM)
    lists = [srcs, recs, befores, done, () if ltab is None else (ltab,), after]
    arrays = [a for some in lists for a in some]
    specs = [whole] * (len(arrays) - len(after)) + [pl.BlockSpec(memory_space=pl.ANY)] * len(after)
    shapes = []
    for out in outs:
        if isinstance(out, int):
            shapes.append(jax.ShapeDtypeStruct((out * unit, 2 * NB), jnp.float32))
        else:
            rows = sum(unit if isinstance(p, str) else p * unit for p in out)
            shapes.append(jax.ShapeDtypeStruct((grid * rows, LAGS), jnp.bfloat16))
    out_specs = [whole] * len(shapes)
    if grid > 1:
        specs[: len(srcs)] = [pl.BlockSpec((1,) + a.shape[1:], lambda g: (g, 0, 0)) for a in srcs]
        out_specs = [pl.BlockSpec((s.shape[0] // grid, s.shape[1]), lambda g: (g, 0)) for s in shapes]
    scratch = [pltpu.VMEM((len(srcs) * n_src * n_win, 3 * NB), jnp.float32)]
    lagged = sum(n for _, n, _, _, place in runs if place is None)
    if lagged:
        scratch.append(pltpu.VMEM((lagged * unit, 2 * NB), jnp.bfloat16))
    pairs = sum(n * n_src * sum(p[3] - p[2] for p in parts) for _, n, parts, _, _ in runs)
    kept = [None if isinstance(out, int) else out for out in outs]
    return pl.pallas_call(
        functools.partial(
            cross_kernel, runs, kept, [len(some) for some in lists], n_src, n_win, early, c_dev, scale
        ),
        grid=() if grid == 1 else (grid,),
        out_shape=shapes,
        in_specs=specs,
        out_specs=out_specs,
        scratch_shapes=scratch,
        compiler_params=pltpu.CompilerParams(vmem_limit_bytes=24 << 20),
        cost_estimate=pl.CostEstimate(
            flops=int((0.4 + grid * pairs * 0.008) * 0.02e9), bytes_accessed=1 << 20, transcendentals=0
        ),
        name="cross",
    )(*arrays)


def join_kernel(*refs):
    *parts, out = refs
    at = 0
    for part in parts:
        out[at : at + part.shape[0]] = part[...]
        at += part.shape[0]


def join_call(*parts):
    rows = sum(part.shape[0] for part in parts)
    vmem = pl.BlockSpec(memory_space=pltpu.VMEM)
    return pl.pallas_call(
        join_kernel,
        out_shape=jax.ShapeDtypeStruct((rows, parts[0].shape[1]), parts[0].dtype),
        in_specs=[vmem] * len(parts),
        out_specs=vmem,
        compiler_params=pltpu.CompilerParams(vmem_limit_bytes=4 << 20),
        cost_estimate=pl.CostEstimate(flops=1 << 20, bytes_accessed=1 << 19, transcendentals=0),
        name="join",
    )(*parts)


def body(record, offsets, src_idx):
    c_dev = record.shape[0]
    n_win = offsets.shape[0]
    n_src = src_idx.shape[0]
    n_tm = lax.axis_size("tm")
    n_fibre = lax.axis_size("fibre")
    n_group = n_fibre // 2
    fibre = lax.axis_index("fibre")
    tm = lax.axis_index("tm")
    head, early = n_win * 3 // 4, n_win * 7 // 8
    scale = 1.0 / math.sqrt(n_win * n_tm * NB)
    tables = [jnp.asarray(t) for t in (half_tables(), taper_table(), smoothing())]
    ltab = jnp.asarray(lag_table())
    direct = n_group == 4 and n_tm == 4

    def trade(array, by):
        return lax.ppermute(array, "fibre", [(i, i ^ by) for i in range(n_fibre)])

    rec_a, middle, src_a, edge, *tables = spectra_call(record, offsets, src_idx, tables, 0, early, head)
    far_a = trade(rec_a, 1)
    if direct:
        by_2a = trade(src_a, 4)
    halo = lax.ppermute(edge, "tm", [(i, i - 1) for i in range(1, n_tm)])
    cross = functools.partial(
        cross_call, n_src=n_src, n_win=n_win, early=early, c_dev=c_dev, scale=scale
    )
    late = (halo, middle, src_a)
    begun = []
    if direct:
        parts = [(0, 0, 0, head), (1, head, head, early)]
        begun = cross([src_a[None]], [rec_a, middle], [(0, 1, parts, None, (0, 0))], [1])
    rec_b, src_b, src = spectra_call(
        record, offsets, src_idx, tables, early, n_win - early, late=late, after=begun
    )
    far_b = trade(rec_b, 1)
    own = [(0, 0, 0, head), (1, head, head, n_win)]
    if direct:
        by_2 = join_call(by_2a, trade(src_b, 4))
        by_1 = trade(src, 2)
        by_3 = trade(by_2, 2)
        srcs = [part[None] for part in (src, by_1, by_2, by_3)]
        mine = functools.partial(cross, recs=[rec_a, rec_b, far_a], ltab=ltab)
        swapped = [(2, 0, 0, head)]
        runs = [
            (0, 1, [(1, head, early, n_win)], (0, 0), None),
            (1, 1, own, None, None),
            (0, 1, swapped, None, (2, 0)),
            (1, 1, swapped, None, (2, 1)),
        ]
        near_0, near_2, sums = mine([srcs[0], srcs[2]], runs=runs, outs=[[1], [1], 2], befores=begun)
        runs = [(0, 1, own, None, None), (0, 1, swapped, None, (1, 0))]
        near_1, sums_1 = mine(srcs[1:2], runs=runs, outs=[[1], 1], after=[sums])
        swapped = [(3, head, head, n_win)]
        runs = [
            (0, 1, swapped, (0, 0), None),
            (1, 1, swapped, (1, 0), None),
            (2, 1, swapped, (0, 1), None),
            (3, 1, [(2, 0, 0, head)] + swapped, None, None),
            (3, 1, own, None, None),
        ]
        far, near = cross(
            srcs, [rec_a, rec_b, far_a, far_b], runs, [[1, 1, 1, 1], ["done"] * 3 + [1]],
            befores=[sums, sums_1], done=[near_0, near_1, near_2], ltab=ltab,
        )
    else:
        ranks = [[2 * j + p for j in range(n_group)] for p in range(2)]
        srcs = [lax.all_gather(src, "fibre", axis=0, axis_index_groups=ranks)]
        runs = [(0, 1, own, None, None)]
        near = cross(srcs, [rec_a, rec_b], runs, [[1]], ltab=ltab)[0]
        far = cross(srcs, [far_a, far_b], runs, [[1]], ltab=ltab)[0]
    near, far = (r.reshape(n_group, n_src, c_dev, LAGS) for r in (near, far))

    def piece(lagged, owner):
        if direct:
            return lax.dynamic_index_in_dim(lagged, (fibre // 2) ^ owner, 0, keepdims=True)
        share = n_group // n_tm
        return lax.dynamic_slice_in_dim(lagged, owner * share, share, 0)

    keep = jnp.stack([piece(r, tm ^ k) for r in (near, far) for k in range(0, n_tm, 2)])
    give = jnp.stack([piece(r, tm ^ k) for r in (near, far) for k in range(1, n_tm, 2)])
    got = lax.ppermute(give, "tm", [(i, i ^ 1) for i in range(n_tm)])
    pairs = keep.astype(jnp.float32) + got.astype(jnp.float32)
    totals = []
    for side in range(2):
        total = None
        for k in range(n_tm // 2):
            mine = pairs[side * (n_tm // 2) + k]
            if side or k:
                routes = [
                    (i * n_tm + t, (i ^ side) * n_tm + (t ^ (2 * k)))
                    for i in range(n_fibre)
                    for t in range(n_tm)
                ]
                mine = lax.ppermute(mine.astype(jnp.bfloat16), ("fibre", "tm"), routes)
                mine = mine.astype(jnp.float32)
            total = mine if total is None else total + mine
        totals.append(total)
    even = fibre % 2 == 0
    near, far = totals
    out = jnp.stack([jnp.where(even, near, far), jnp.where(even, far, near)], axis=1)
    return out.reshape(-1, c_dev, LAGS)


def solution(mesh):
    return jax.shard_map(
        body,
        mesh=mesh,
        in_specs=(P("fibre", "tm"), P("tm"), P("fibre")),
        out_specs=P("tm", "fibre", None),
        check_vma=False,
    )
```

```python
import functools
import math

import jax
import jax.numpy as jnp
import numpy as np
from jax import lax
from jax.experimental import pallas as pl
from jax.experimental.pallas import tpu as pltpu
from jax.sharding import PartitionSpec as P

W = 2048
HOP = 1024
NB = 384
B0 = 20
SMOOTH = 64
LAGS = 256
LANE = 128
CUT = W + LANE
FOLD = W // 2
BINS = np.concatenate(
    [np.arange(0, 256, 2), np.arange(1, 256, 2), np.arange(256, NB, 2), np.arange(257, NB, 2)]
)


def taper_table():
    return (0.5 - 0.5 * np.cos(np.arange(W) * (2.0 * math.pi / W))).astype(np.float32)[None, :]


def half_tables():
    samples = np.arange(FOLD, dtype=np.int64)[:, None]

    def waves(bins):
        turns = (samples * (B0 + bins)[None, :] % W) * (2.0 * math.pi / W)
        return np.cos(turns), -np.sin(turns)

    even_cos, even_sin = waves(np.arange(0, NB, 2))
    odd_cos, odd_sin = waves(np.arange(1, NB, 2))
    cut = LANE
    columns = [
        even_cos[:, :cut], even_sin[:, :cut], even_cos[:, cut:], even_sin[:, cut:],
        odd_cos[:, :cut], odd_sin[:, :cut], odd_sin[:, cut:], odd_cos[:, cut:],
    ]
    return np.concatenate(columns, axis=1).astype(np.float32).astype(jnp.bfloat16)


def smoothing():
    rows = BINS[:, None]
    cols = BINS[None, :]
    first = np.clip(cols - SMOOTH // 2, 0, NB - SMOOTH)
    return np.where((rows >= first) & (rows < first + SMOOTH), 1.0 / SMOOTH, 0.0).astype(jnp.bfloat16)


def lag_table():
    shifts = np.arange(LAGS, dtype=np.int64) - LAGS // 2
    turns = ((B0 + BINS)[:, None] * shifts[None, :] % W) * (2.0 * math.pi / W)
    table = np.concatenate([np.cos(turns), -np.sin(turns)], axis=0)
    return table.astype(np.float32).astype(jnp.bfloat16)


def spectra_kernel(first, count, late, c_dev, n_src, n_after, *refs):
    if late:
        offs, sources, rec, halo, table_v, taper_v, smooth_v, before_r, before_s, *refs = refs
        out_r, out_s, out_all, *refs = refs[n_after:]
        sums, diffs, held, offs_v, sources_v, sems = refs
    else:
        offs, sources, rec, table, taper, smooth, *refs = refs
        out_r, out_mid, out_s, out_edge, table_v, taper_v, smooth_v, *refs = refs
        sums, diffs, held, offs_v, sources_v, sems = refs
    width = (count + 2) * HOP
    copies = []

    def fetch(source, target):
        copy = pltpu.make_async_copy(source, target, sems.at[len(copies)])
        copy.start()
        copies.append(copy)

    fetch(offs, offs_v)
    fetch(sources, sources_v)
    inside = width - (W if late else 0)
    half = 0 if late else (count + 1) // 2
    if late:
        held[:, inside:] = halo[...]
    else:
        fetch(taper, taper_v)
    for start, stop in ((0, (half + 2) * HOP), ((half + 2) * HOP, inside)):
        fetch(rec.at[:, pl.ds(first * HOP + start, stop - start)], held.at[:, pl.ds(start, stop - start)])
    ready = len(copies)
    if not late:
        rows = FOLD // 4
        for at in range(0, FOLD, rows):
            fetch(table.at[pl.ds(at, rows)], table_v.at[pl.ds(at, rows)])
        fetch(smooth, smooth_v)
        fetch(rec.at[:, pl.ds(0, W)], out_edge)
    for copy in copies[: ready - 1]:
        copy.wait()

    lanes = lax.broadcasted_iota(jnp.int32, (c_dev, LANE), 1)

    def cut(slot):
        start = slot * HOP + offs_v[first + slot]
        rest = start % LANE
        keep = lanes < LANE - rest
        shift = (LANE - rest) % LANE
        chunk = held[:, pl.ds(pl.multiple_of(start // LANE * LANE, LANE), CUT)].astype(jnp.float32)
        turned = [pltpu.roll(chunk[:, i * LANE : (i + 1) * LANE], shift, 1) for i in range(CUT // LANE)]
        row = pl.ds(pl.multiple_of(slot * c_dev, c_dev), c_dev)
        tiles = FOLD // LANE
        for i in range(tiles):
            lo = slice(i * LANE, (i + 1) * LANE)
            hi = slice(FOLD + i * LANE, FOLD + (i + 1) * LANE)
            near = jnp.where(keep, turned[i], turned[i + 1]) * taper_v[:, lo]
            far = jnp.where(keep, turned[tiles + i], turned[tiles + i + 1]) * taper_v[:, hi]
            sums[row, lo] = (near + far).astype(jnp.bfloat16)
            diffs[row, lo] = (near - far).astype(jnp.bfloat16)

    for slot in range(half):
        cut(slot)
    copies[ready - 1].wait()
    for slot in range(half, count):
        cut(slot)
    for copy in copies[ready:]:
        copy.wait()

    split = 3 * LANE
    even = jnp.dot(sums[...], table_v[:, :split], preferred_element_type=jnp.float32)
    odd = jnp.dot(diffs[...], table_v[:, split:], preferred_element_type=jnp.float32)
    left = lax.broadcasted_iota(jnp.int32, (1, LANE), 1) < LANE // 2
    mixed_even, mixed_odd = even[:, 2 * LANE :], odd[:, 2 * LANE :]
    real = [even[:, :LANE], odd[:, :LANE], jnp.where(left, mixed_even, mixed_odd)]
    swapped = pltpu.roll(jnp.where(left, mixed_odd, mixed_even), LANE // 2, 1)
    imag = [even[:, LANE : 2 * LANE], odd[:, LANE : 2 * LANE], swapped]
    power = jnp.concatenate([r * r + i * i for r, i in zip(real, imag)], axis=1).astype(jnp.bfloat16)
    smoothed = jnp.dot(power, smooth_v[...], preferred_element_type=jnp.float32)
    factor = lax.rsqrt(smoothed + 1e-05)
    parts = [value * factor[:, i % 3 * LANE : (i % 3 + 1) * LANE] for i, value in enumerate(real + imag)]
    white = jnp.concatenate([part.astype(jnp.bfloat16) for part in parts], axis=1)
    if late:
        at = before_r.shape[0]
        out_r[:at] = before_r[...]
        out_r[at:] = white
    else:
        at = out_r.shape[0]
        out_r[...] = white[:at]
        out_mid[...] = white[at:]
    rows = lax.broadcasted_iota(jnp.int32, (n_src * count, 1), 0)
    cols = lax.broadcasted_iota(jnp.int32, (n_src * count, count * c_dev), 1)
    wanted = jnp.zeros_like(rows)
    for s in range(n_src):
        wanted = jnp.where(rows // count == s, sources_v[s] % c_dev + (rows % count) * c_dev, wanted)
    picker = jnp.where(cols == wanted, 1.0, 0.0).astype(jnp.bfloat16)
    out_s[...] = jnp.dot(picker, white, preferred_element_type=jnp.float32).astype(jnp.bfloat16)
    if late:
        at = before_s.shape[0]
        out_all[:at] = before_s[...]
        out_all[at:] = out_s[...]


def spectra_call(record, offsets, src_idx, tables, first, count, head=None, late=None, after=()):
    c_dev = record.shape[0]
    n_src = src_idx.shape[0]
    vmem = pl.BlockSpec(memory_space=pltpu.VMEM)
    hbm = pl.BlockSpec(memory_space=pltpu.HBM)
    arrays = [offsets, src_idx, record]
    if late is None:
        arrays += tables
    arrays = [pltpu.with_memory_space_constraint(a, pltpu.HBM) for a in arrays]
    specs = [hbm] * len(arrays)
    rows = [head, count - head] if late is None else [count + late[1].shape[0] // c_dev]
    out_shape = [jax.ShapeDtypeStruct((n * c_dev, 2 * NB), jnp.bfloat16) for n in rows]
    out_shape.append(jax.ShapeDtypeStruct((n_src * count, 2 * NB), jnp.bfloat16))
    if late is None:
        out_shape.append(jax.ShapeDtypeStruct((c_dev, W), record.dtype))
        out_shape += [jax.ShapeDtypeStruct(t.shape, t.dtype) for t in tables]
    else:
        halo, middle, sources = late
        arrays += [halo, *tables, middle, sources, *after]
        specs += [vmem] * 6 + [pl.BlockSpec(memory_space=pl.ANY)] * len(after)
        out_shape.append(jax.ShapeDtypeStruct((sources.shape[0] + n_src * count, 2 * NB), jnp.bfloat16))
    return pl.pallas_call(
        functools.partial(spectra_kernel, first, count, late is not None, c_dev, n_src, len(after)),
        out_shape=out_shape,
        in_specs=specs,
        out_specs=[vmem] * len(out_shape),
        scratch_shapes=[
            pltpu.VMEM((count * c_dev, FOLD), jnp.bfloat16),
            pltpu.VMEM((count * c_dev, FOLD), jnp.bfloat16),
            pltpu.VMEM((c_dev, (count + 2) * HOP), jnp.bfloat16),
            pltpu.SMEM(offsets.shape, jnp.int32),
            pltpu.SMEM(src_idx.shape, jnp.int32),
            pltpu.SemaphoreType.DMA((16,)),
        ],
        compiler_params=pltpu.CompilerParams(vmem_limit_bytes=24 << 20),
        cost_estimate=pl.CostEstimate(
            flops=int((1.5 + 0.1 * count) * 0.01e9), bytes_accessed=1 << 20, transcendentals=0
        ),
        name="spectra",
    )(*arrays)


def cross_kernel(runs, outs, counts, n_src, n_win, early, c_dev, scale, *refs):
    groups = []
    for count in counts:
        groups.append(refs[:count])
        refs = refs[count:]
    srcs, recs, befores, done, tables, _ = groups
    outputs, refs = refs[: len(outs)], refs[len(outs) :]
    wide = refs[0]
    span = n_src * n_win
    for k, src in enumerate(srcs):
        rows = slice(k * span, k * span + src.shape[1])
        real = src[0, :, :NB].astype(jnp.float32)
        imag = src[0, :, NB:].astype(jnp.float32)
        wide[rows, :NB] = real
        wide[rows, NB : 2 * NB] = real + imag
        wide[rows, 2 * NB :] = real - imag
    tiles = NB // LANE

    def run(step, first, wave, parts, before, target, offset):
        block = wave * n_src
        local = step // tiles * wave
        lo, hi, top = (
            pl.ds(pl.multiple_of(step % tiles * LANE + i * NB, LANE), LANE) for i in range(3)
        )
        src = wide.at[pl.ds(pl.multiple_of((first + local) * span, 8), wave * span)]

        def place(start, s):
            return pl.ds(pl.multiple_of(((start + local) * n_src + s) * c_dev, c_dev), c_dev)

        sums = [[jnp.zeros((c_dev, LANE), jnp.float32)] * 3 for _ in range(block)]
        for index, base, start, stop in parts:
            for w in range(start, stop):
                row = slice((w - base) * c_dev, (w - base + 1) * c_dev)
                rec_real = recs[index][row, lo].astype(jnp.float32)
                rec_imag = recs[index][row, hi].astype(jnp.float32)
                rec_both = rec_real + rec_imag
                for s in range(block):
                    at = s // n_src * span
                    if w < early:
                        at += s % n_src * early + w
                    else:
                        at += n_src * early + s % n_src * (n_win - early) + w - early
                    row = slice(at, at + 1)
                    both, plus, minus = sums[s]
                    sums[s] = [
                        both + src[row, lo] * rec_both,
                        plus + src[row, hi] * rec_real,
                        minus + src[row, top] * rec_imag,
                    ]
        for s in range(block):
            both, plus, minus = sums[s]
            real, imag = both - minus, both - plus
            if before is not None:
                real += befores[before[0]][place(before[1], s), lo]
                imag += befores[before[0]][place(before[1], s), hi]
            target[place(offset, s), lo] = real.astype(target.dtype)
            target[place(offset, s), hi] = imag.astype(target.dtype)

    lagged = 0
    for first, n_group, parts, before, place in runs:
        if place is None:
            target, offset = refs[1], lagged
            lagged += n_group
        else:
            target, offset = outputs[place[0]], place[1]
        wave = 8 // n_src if n_group * n_src % 8 == 0 and 8 % n_src == 0 else 1
        pl.loop(0, n_group // wave * tiles)(
            functools.partial(
                run, first=first, wave=wave, parts=parts, before=before, target=target, offset=offset
            )
        )

    if lagged:
        lags = jnp.dot(refs[1][...], tables[0][...], preferred_element_type=jnp.float32)
        lags = (lags * scale).astype(jnp.bfloat16)
        unit = n_src * c_dev
        start, done = 0, list(done)
        for out, pieces in zip(outputs, outs):
            at = 0
            for piece in pieces or ():
                if isinstance(piece, str):
                    part = done.pop(0)[...]
                else:
                    part = lags[start * unit : (start + piece) * unit]
                    start += piece
                out[at : at + part.shape[0], :] = part
                at += part.shape[0]


def cross_call(srcs, recs, runs, outs, n_src, n_win, early, c_dev, scale, befores=(), done=(), ltab=None, after=()):
    grid = srcs[0].shape[0]
    unit = n_src * c_dev
    whole = pl.BlockSpec(memory_space=pltpu.VMEM)
    lists = [srcs, recs, befores, done, () if ltab is None else (ltab,), after]
    arrays = [a for some in lists for a in some]
    specs = [whole] * (len(arrays) - len(after)) + [pl.BlockSpec(memory_space=pl.ANY)] * len(after)
    shapes = []
    for out in outs:
        if isinstance(out, int):
            shapes.append(jax.ShapeDtypeStruct((out * unit, 2 * NB), jnp.float32))
        else:
            rows = sum(unit if isinstance(p, str) else p * unit for p in out)
            shapes.append(jax.ShapeDtypeStruct((grid * rows, LAGS), jnp.bfloat16))
    out_specs = [whole] * len(shapes)
    if grid > 1:
        specs[: len(srcs)] = [pl.BlockSpec((1,) + a.shape[1:], lambda g: (g, 0, 0)) for a in srcs]
        out_specs = [pl.BlockSpec((s.shape[0] // grid, s.shape[1]), lambda g: (g, 0)) for s in shapes]
    scratch = [pltpu.VMEM((len(srcs) * n_src * n_win, 3 * NB), jnp.float32)]
    lagged = sum(n for _, n, _, _, place in runs if place is None)
    if lagged:
        scratch.append(pltpu.VMEM((lagged * unit, 2 * NB), jnp.bfloat16))
    pairs = sum(n * n_src * sum(p[3] - p[2] for p in parts) for _, n, parts, _, _ in runs)
    kept = [None if isinstance(out, int) else out for out in outs]
    return pl.pallas_call(
        functools.partial(
            cross_kernel, runs, kept, [len(some) for some in lists], n_src, n_win, early, c_dev, scale
        ),
        grid=() if grid == 1 else (grid,),
        out_shape=shapes,
        in_specs=specs,
        out_specs=out_specs,
        scratch_shapes=scratch,
        compiler_params=pltpu.CompilerParams(vmem_limit_bytes=24 << 20),
        cost_estimate=pl.CostEstimate(
            flops=int((0.4 + grid * pairs * 0.008) * 1.15e9), bytes_accessed=1 << 20, transcendentals=0
        ),
        name="cross",
    )(*arrays)


def join_kernel(*refs):
    *parts, out = refs
    at = 0
    for part in parts:
        out[at : at + part.shape[0]] = part[...]
        at += part.shape[0]


def join_call(*parts):
    rows = sum(part.shape[0] for part in parts)
    vmem = pl.BlockSpec(memory_space=pltpu.VMEM)
    return pl.pallas_call(
        join_kernel,
        out_shape=jax.ShapeDtypeStruct((rows, parts[0].shape[1]), parts[0].dtype),
        in_specs=[vmem] * len(parts),
        out_specs=vmem,
        compiler_params=pltpu.CompilerParams(vmem_limit_bytes=4 << 20),
        cost_estimate=pl.CostEstimate(flops=1 << 20, bytes_accessed=1 << 19, transcendentals=0),
        name="join",
    )(*parts)


def body(record, offsets, src_idx):
    c_dev = record.shape[0]
    n_win = offsets.shape[0]
    n_src = src_idx.shape[0]
    n_tm = lax.axis_size("tm")
    n_fibre = lax.axis_size("fibre")
    n_group = n_fibre // 2
    fibre = lax.axis_index("fibre")
    tm = lax.axis_index("tm")
    head, early = n_win * 3 // 4, n_win * 7 // 8
    scale = 1.0 / math.sqrt(n_win * n_tm * NB)
    tables = [jnp.asarray(t) for t in (half_tables(), taper_table(), smoothing())]
    ltab = jnp.asarray(lag_table())
    direct = n_group == 4 and n_tm == 4

    def trade(array, by):
        return lax.ppermute(array, "fibre", [(i, i ^ by) for i in range(n_fibre)])

    rec_a, middle, src_a, edge, *tables = spectra_call(record, offsets, src_idx, tables, 0, early, head)
    far_a = trade(rec_a, 1)
    if direct:
        by_2a = trade(src_a, 4)
    halo = lax.ppermute(edge, "tm", [(i, i - 1) for i in range(1, n_tm)])
    cross = functools.partial(
        cross_call, n_src=n_src, n_win=n_win, early=early, c_dev=c_dev, scale=scale
    )
    late = (halo, middle, src_a)
    begun = []
    if direct:
        parts = [(0, 0, 0, head), (1, head, head, early)]
        begun = cross([src_a[None]], [rec_a, middle], [(0, 1, parts, None, (0, 0))], [1])
    rec_b, src_b, src = spectra_call(
        record, offsets, src_idx, tables, early, n_win - early, late=late, after=begun
    )
    far_b = trade(rec_b, 1)
    own = [(0, 0, 0, head), (1, head, head, n_win)]
    if direct:
        by_2 = join_call(by_2a, trade(src_b, 4))
        by_1 = trade(src, 2)
        by_3 = trade(by_2, 2)
        srcs = [part[None] for part in (src, by_1, by_2, by_3)]
        mine = functools.partial(cross, recs=[rec_a, rec_b, far_a], ltab=ltab)
        swapped = [(2, 0, 0, head)]
        runs = [
            (0, 1, [(1, head, early, n_win)], (0, 0), None),
            (1, 1, own, None, None),
            (0, 1, swapped, None, (2, 0)),
            (1, 1, swapped, None, (2, 1)),
        ]
        near_0, near_2, sums = mine([srcs[0], srcs[2]], runs=runs, outs=[[1], [1], 2], befores=begun)
        runs = [(0, 1, own, None, None), (0, 1, swapped, None, (1, 0))]
        near_1, sums_1 = mine(srcs[1:2], runs=runs, outs=[[1], 1], after=[sums])
        swapped = [(3, head, head, n_win)]
        runs = [
            (0, 1, swapped, (0, 0), None),
            (1, 1, swapped, (1, 0), None),
            (2, 1, swapped, (0, 1), None),
            (3, 1, [(2, 0, 0, head)] + swapped, None, None),
            (3, 1, own, None, None),
        ]
        far, near = cross(
            srcs, [rec_a, rec_b, far_a, far_b], runs, [[1, 1, 1, 1], ["done"] * 3 + [1]],
            befores=[sums, sums_1], done=[near_0, near_1, near_2], ltab=ltab,
        )
    else:
        ranks = [[2 * j + p for j in range(n_group)] for p in range(2)]
        srcs = [lax.all_gather(src, "fibre", axis=0, axis_index_groups=ranks)]
        runs = [(0, 1, own, None, None)]
        near = cross(srcs, [rec_a, rec_b], runs, [[1]], ltab=ltab)[0]
        far = cross(srcs, [far_a, far_b], runs, [[1]], ltab=ltab)[0]
    near, far = (r.reshape(n_group, n_src, c_dev, LAGS) for r in (near, far))

    def piece(lagged, owner):
        if direct:
            return lax.dynamic_index_in_dim(lagged, (fibre // 2) ^ owner, 0, keepdims=True)
        share = n_group // n_tm
        return lax.dynamic_slice_in_dim(lagged, owner * share, share, 0)

    keep = jnp.stack([piece(r, tm ^ k) for r in (near, far) for k in range(0, n_tm, 2)])
    give = jnp.stack([piece(r, tm ^ k) for r in (near, far) for k in range(1, n_tm, 2)])
    got = lax.ppermute(give, "tm", [(i, i ^ 1) for i in range(n_tm)])
    pairs = keep.astype(jnp.float32) + got.astype(jnp.float32)
    totals = []
    for side in range(2):
        total = None
        for k in range(n_tm // 2):
            mine = pairs[side * (n_tm // 2) + k]
            if side or k:
                routes = [
                    (i * n_tm + t, (i ^ side) * n_tm + (t ^ (2 * k)))
                    for i in range(n_fibre)
                    for t in range(n_tm)
                ]
                mine = lax.ppermute(mine.astype(jnp.bfloat16), ("fibre", "tm"), routes)
                mine = mine.astype(jnp.float32)
            total = mine if total is None else total + mine
        totals.append(total)
    even = fibre % 2 == 0
    near, far = totals
    out = jnp.stack([jnp.where(even, near, far), jnp.where(even, far, near)], axis=1)
    return out.reshape(-1, c_dev, LAGS)


def solution(mesh):
    return jax.shard_map(
        body,
        mesh=mesh,
        in_specs=(P("fibre", "tm"), P("tm"), P("fibre")),
        out_specs=P("tm", "fibre", None),
        check_vma=False,
    )
```

```python
import functools
import math

import jax
import jax.numpy as jnp
import numpy as np
from jax import lax
from jax.experimental import pallas as pl
from jax.experimental.pallas import tpu as pltpu
from jax.sharding import PartitionSpec as P

W = 2048
HOP = 1024
NB = 384
B0 = 20
SMOOTH = 64
LAGS = 256
LANE = 128
CUT = W + LANE
FOLD = W // 2
BINS = np.concatenate(
    [np.arange(0, 256, 2), np.arange(1, 256, 2), np.arange(256, NB, 2), np.arange(257, NB, 2)]
)


def taper_table():
    return (0.5 - 0.5 * np.cos(np.arange(W) * (2.0 * math.pi / W))).astype(np.float32)[None, :]


def half_tables():
    samples = np.arange(FOLD, dtype=np.int64)[:, None]

    def waves(bins):
        turns = (samples * (B0 + bins)[None, :] % W) * (2.0 * math.pi / W)
        return np.cos(turns), -np.sin(turns)

    even_cos, even_sin = waves(np.arange(0, NB, 2))
    odd_cos, odd_sin = waves(np.arange(1, NB, 2))
    cut = LANE
    columns = [
        even_cos[:, :cut], even_sin[:, :cut], even_cos[:, cut:], even_sin[:, cut:],
        odd_cos[:, :cut], odd_sin[:, :cut], odd_sin[:, cut:], odd_cos[:, cut:],
    ]
    return np.concatenate(columns, axis=1).astype(np.float32).astype(jnp.bfloat16)


def smoothing():
    rows = BINS[:, None]
    cols = BINS[None, :]
    first = np.clip(cols - SMOOTH // 2, 0, NB - SMOOTH)
    return np.where((rows >= first) & (rows < first + SMOOTH), 1.0 / SMOOTH, 0.0).astype(jnp.bfloat16)


def lag_table():
    shifts = np.arange(LAGS, dtype=np.int64) - LAGS // 2
    turns = ((B0 + BINS)[:, None] * shifts[None, :] % W) * (2.0 * math.pi / W)
    table = np.concatenate([np.cos(turns), -np.sin(turns)], axis=0)
    return table.astype(np.float32).astype(jnp.bfloat16)


def spectra_kernel(first, count, late, c_dev, n_src, n_after, *refs):
    if late:
        offs, sources, rest, halo, table_v, taper_v, smooth_v, before_r, before_s, *refs = refs
        out_r, out_s, out_all, *refs = refs[n_after:]
        sums, diffs, held, offs_v, sources_v, sems = refs
    else:
        offs, sources, rec, table, taper, smooth, *refs = refs
        out_r, out_mid, out_s, out_edge, out_rest, out_offs, out_sources, *refs = refs
        table_v, taper_v, smooth_v, *refs = refs
        sums, diffs, held, offs_v, sources_v, sems = refs
    width = (count + 2) * HOP
    copies = []

    def fetch(source, target):
        copy = pltpu.make_async_copy(source, target, sems.at[len(copies)])
        copy.start()
        copies.append(copy)

    fetch(offs, offs_v)
    fetch(sources, sources_v)
    inside = width - (W if late else 0)
    half = 0 if late else (count + 1) // 2
    if late:
        held[:, :inside] = rest[...]
        held[:, inside:] = halo[...]
    else:
        fetch(taper, taper_v)
        for start, stop in ((0, (half + 2) * HOP), ((half + 2) * HOP, inside)):
            fetch(rec.at[:, pl.ds(start, stop - start)], held.at[:, pl.ds(start, stop - start)])
    ready = len(copies)
    if not late:
        rows = FOLD // 4
        for at in range(0, FOLD, rows):
            fetch(table.at[pl.ds(at, rows)], table_v.at[pl.ds(at, rows)])
        fetch(smooth, smooth_v)
        fetch(rec.at[:, pl.ds(0, W)], out_edge)
        fetch(rec.at[:, pl.ds(count * HOP, out_rest.shape[1])], out_rest)
        fetch(offs, out_offs)
        fetch(sources, out_sources)
    for copy in copies[: ready - 1]:
        copy.wait()

    lanes = lax.broadcasted_iota(jnp.int32, (c_dev, LANE), 1)

    def cut(slot):
        start = slot * HOP + offs_v[first + slot]
        rest = start % LANE
        keep = lanes < LANE - rest
        shift = (LANE - rest) % LANE
        chunk = held[:, pl.ds(pl.multiple_of(start // LANE * LANE, LANE), CUT)].astype(jnp.float32)
        turned = [pltpu.roll(chunk[:, i * LANE : (i + 1) * LANE], shift, 1) for i in range(CUT // LANE)]
        row = pl.ds(pl.multiple_of(slot * c_dev, c_dev), c_dev)
        tiles = FOLD // LANE
        for i in range(tiles):
            lo = slice(i * LANE, (i + 1) * LANE)
            hi = slice(FOLD + i * LANE, FOLD + (i + 1) * LANE)
            near = jnp.where(keep, turned[i], turned[i + 1]) * taper_v[:, lo]
            far = jnp.where(keep, turned[tiles + i], turned[tiles + i + 1]) * taper_v[:, hi]
            sums[row, lo] = (near + far).astype(jnp.bfloat16)
            diffs[row, lo] = (near - far).astype(jnp.bfloat16)

    for slot in range(half):
        cut(slot)
    copies[ready - 1].wait()
    for slot in range(half, count):
        cut(slot)
    for copy in copies[ready:]:
        copy.wait()

    split = 3 * LANE
    even = jnp.dot(sums[...], table_v[:, :split], preferred_element_type=jnp.float32)
    odd = jnp.dot(diffs[...], table_v[:, split:], preferred_element_type=jnp.float32)
    left = lax.broadcasted_iota(jnp.int32, (1, LANE), 1) < LANE // 2
    mixed_even, mixed_odd = even[:, 2 * LANE :], odd[:, 2 * LANE :]
    real = [even[:, :LANE], odd[:, :LANE], jnp.where(left, mixed_even, mixed_odd)]
    swapped = pltpu.roll(jnp.where(left, mixed_odd, mixed_even), LANE // 2, 1)
    imag = [even[:, LANE : 2 * LANE], odd[:, LANE : 2 * LANE], swapped]
    power = jnp.concatenate([r * r + i * i for r, i in zip(real, imag)], axis=1).astype(jnp.bfloat16)
    smoothed = jnp.dot(power, smooth_v[...], preferred_element_type=jnp.float32)
    factor = lax.rsqrt(smoothed + 1e-05)
    parts = [value * factor[:, i % 3 * LANE : (i % 3 + 1) * LANE] for i, value in enumerate(real + imag)]
    white = jnp.concatenate([part.astype(jnp.bfloat16) for part in parts], axis=1)
    if late:
        at = before_r.shape[0]
        out_r[:at] = before_r[...]
        out_r[at:] = white
    else:
        at = out_r.shape[0]
        out_r[...] = white[:at]
        out_mid[...] = white[at:]
    rows = lax.broadcasted_iota(jnp.int32, (n_src * count, 1), 0)
    cols = lax.broadcasted_iota(jnp.int32, (n_src * count, count * c_dev), 1)
    wanted = jnp.zeros_like(rows)
    for s in range(n_src):
        wanted = jnp.where(rows // count == s, sources_v[s] % c_dev + (rows % count) * c_dev, wanted)
    picker = jnp.where(cols == wanted, 1.0, 0.0).astype(jnp.bfloat16)
    out_s[...] = jnp.dot(picker, white, preferred_element_type=jnp.float32).astype(jnp.bfloat16)
    if late:
        at = before_s.shape[0]
        out_all[:at] = before_s[...]
        out_all[at:] = out_s[...]


def spectra_call(record, offsets, src_idx, tables, first, count, head=None, late=None, after=()):
    c_dev = record.shape[0]
    n_src = src_idx.shape[0]
    vmem = pl.BlockSpec(memory_space=pltpu.VMEM)
    hbm = pl.BlockSpec(memory_space=pltpu.HBM)
    arrays = [offsets, src_idx, record]
    n_rest = record.shape[1] - count * HOP
    if late is None:
        arrays += tables
        arrays = [pltpu.with_memory_space_constraint(a, pltpu.HBM) for a in arrays]
    specs = [hbm if late is None else vmem] * len(arrays)
    rows = [head, count - head] if late is None else [count + late[1].shape[0] // c_dev]
    out_shape = [jax.ShapeDtypeStruct((n * c_dev, 2 * NB), jnp.bfloat16) for n in rows]
    out_shape.append(jax.ShapeDtypeStruct((n_src * count, 2 * NB), jnp.bfloat16))
    if late is None:
        out_shape += [jax.ShapeDtypeStruct((c_dev, n), record.dtype) for n in (W, n_rest)]
        out_shape += [jax.ShapeDtypeStruct(a.shape, a.dtype) for a in (offsets, src_idx)]
        out_shape += [jax.ShapeDtypeStruct(t.shape, t.dtype) for t in tables]
    else:
        halo, middle, sources = late
        arrays += [halo, *tables, middle, sources, *after]
        specs += [vmem] * 6 + [pl.BlockSpec(memory_space=pl.ANY)] * len(after)
        out_shape.append(jax.ShapeDtypeStruct((sources.shape[0] + n_src * count, 2 * NB), jnp.bfloat16))
    return pl.pallas_call(
        functools.partial(spectra_kernel, first, count, late is not None, c_dev, n_src, len(after)),
        out_shape=out_shape,
        in_specs=specs,
        out_specs=[vmem] * len(out_shape),
        scratch_shapes=[
            pltpu.VMEM((count * c_dev, FOLD), jnp.bfloat16),
            pltpu.VMEM((count * c_dev, FOLD), jnp.bfloat16),
            pltpu.VMEM((c_dev, (count + 2) * HOP), jnp.bfloat16),
            pltpu.SMEM(offsets.shape, jnp.int32),
            pltpu.SMEM(src_idx.shape, jnp.int32),
            pltpu.SemaphoreType.DMA((16,)),
        ],
        compiler_params=pltpu.CompilerParams(vmem_limit_bytes=24 << 20),
        cost_estimate=pl.CostEstimate(
            flops=int((1.5 + 0.1 * count) * 0.01e9), bytes_accessed=1 << 20, transcendentals=0
        ),
        name="spectra",
    )(*arrays)


def cross_kernel(runs, outs, counts, n_src, n_win, early, c_dev, scale, *refs):
    groups = []
    for count in counts:
        groups.append(refs[:count])
        refs = refs[count:]
    srcs, recs, befores, done, tables, _ = groups
    outputs, refs = refs[: len(outs)], refs[len(outs) :]
    wide = refs[0]
    span = n_src * n_win
    for k, src in enumerate(srcs):
        rows = slice(k * span, k * span + src.shape[1])
        real = src[0, :, :NB].astype(jnp.float32)
        imag = src[0, :, NB:].astype(jnp.float32)
        wide[rows, :NB] = real
        wide[rows, NB : 2 * NB] = real + imag
        wide[rows, 2 * NB :] = real - imag
    tiles = NB // LANE

    def run(step, first, wave, parts, before, target, offset):
        block = wave * n_src
        local = step // tiles * wave
        lo, hi, top = (
            pl.ds(pl.multiple_of(step % tiles * LANE + i * NB, LANE), LANE) for i in range(3)
        )
        src = wide.at[pl.ds(pl.multiple_of((first + local) * span, 8), wave * span)]

        def place(start, s):
            return pl.ds(pl.multiple_of(((start + local) * n_src + s) * c_dev, c_dev), c_dev)

        sums = [[jnp.zeros((c_dev, LANE), jnp.float32)] * 3 for _ in range(block)]
        for index, base, start, stop in parts:
            for w in range(start, stop):
                row = slice((w - base) * c_dev, (w - base + 1) * c_dev)
                rec_real = recs[index][row, lo].astype(jnp.float32)
                rec_imag = recs[index][row, hi].astype(jnp.float32)
                rec_both = rec_real + rec_imag
                for s in range(block):
                    at = s // n_src * span
                    if w < early:
                        at += s % n_src * early + w
                    else:
                        at += n_src * early + s % n_src * (n_win - early) + w - early
                    row = slice(at, at + 1)
                    both, plus, minus = sums[s]
                    sums[s] = [
                        both + src[row, lo] * rec_both,
                        plus + src[row, hi] * rec_real,
                        minus + src[row, top] * rec_imag,
                    ]
        for s in range(block):
            both, plus, minus = sums[s]
            real, imag = both - minus, both - plus
            if before is not None:
                real += befores[before[0]][place(before[1], s), lo]
                imag += befores[before[0]][place(before[1], s), hi]
            target[place(offset, s), lo] = real.astype(target.dtype)
            target[place(offset, s), hi] = imag.astype(target.dtype)

    lagged = 0
    for first, n_group, parts, before, place in runs:
        if place is None:
            target, offset = refs[1], lagged
            lagged += n_group
        else:
            target, offset = outputs[place[0]], place[1]
        wave = 8 // n_src if n_group * n_src % 8 == 0 and 8 % n_src == 0 else 1
        pl.loop(0, n_group // wave * tiles)(
            functools.partial(
                run, first=first, wave=wave, parts=parts, before=before, target=target, offset=offset
            )
        )

    if lagged:
        lags = jnp.dot(refs[1][...], tables[0][...], preferred_element_type=jnp.float32)
        lags = (lags * scale).astype(jnp.bfloat16)
        unit = n_src * c_dev
        start, done = 0, list(done)
        for out, pieces in zip(outputs, outs):
            at = 0
            for piece in pieces or ():
                if isinstance(piece, str):
                    part = done.pop(0)[...]
                else:
                    part = lags[start * unit : (start + piece) * unit]
                    start += piece
                out[at : at + part.shape[0], :] = part
                at += part.shape[0]


def cross_call(srcs, recs, runs, outs, n_src, n_win, early, c_dev, scale, befores=(), done=(), ltab=None, after=()):
    grid = srcs[0].shape[0]
    unit = n_src * c_dev
    whole = pl.BlockSpec(memory_space=pltpu.VMEM)
    lists = [srcs, recs, befores, done, () if ltab is None else (ltab,), after]
    arrays = [a for some in lists for a in some]
    specs = [whole] * (len(arrays) - len(after)) + [pl.BlockSpec(memory_space=pl.ANY)] * len(after)
    shapes, heights = [], [a.shape[0] for a in done]
    for out in outs:
        if isinstance(out, int):
            shapes.append(jax.ShapeDtypeStruct((out * unit, 2 * NB), jnp.float32))
        else:
            rows = sum(heights.pop(0) if isinstance(p, str) else p * unit for p in out)
            shapes.append(jax.ShapeDtypeStruct((grid * rows, LAGS), jnp.bfloat16))
    out_specs = [whole] * len(shapes)
    if grid > 1:
        specs[: len(srcs)] = [pl.BlockSpec((1,) + a.shape[1:], lambda g: (g, 0, 0)) for a in srcs]
        out_specs = [pl.BlockSpec((s.shape[0] // grid, s.shape[1]), lambda g: (g, 0)) for s in shapes]
    scratch = [pltpu.VMEM((len(srcs) * n_src * n_win, 3 * NB), jnp.float32)]
    lagged = sum(n for _, n, _, _, place in runs if place is None)
    if lagged:
        scratch.append(pltpu.VMEM((lagged * unit, 2 * NB), jnp.bfloat16))
    pairs = sum(n * n_src * sum(p[3] - p[2] for p in parts) for _, n, parts, _, _ in runs)
    kept = [None if isinstance(out, int) else out for out in outs]
    return pl.pallas_call(
        functools.partial(
            cross_kernel, runs, kept, [len(some) for some in lists], n_src, n_win, early, c_dev, scale
        ),
        grid=() if grid == 1 else (grid,),
        out_shape=shapes,
        in_specs=specs,
        out_specs=out_specs,
        scratch_shapes=scratch,
        compiler_params=pltpu.CompilerParams(vmem_limit_bytes=24 << 20),
        cost_estimate=pl.CostEstimate(
            flops=int((0.4 + grid * pairs * 0.008) * 0.02e9), bytes_accessed=1 << 20, transcendentals=0
        ),
        name="cross",
    )(*arrays)


def join_kernel(*refs):
    *parts, out = refs
    at = 0
    for part in parts:
        out[at : at + part.shape[0]] = part[...]
        at += part.shape[0]


def join_call(*parts):
    rows = sum(part.shape[0] for part in parts)
    vmem = pl.BlockSpec(memory_space=pltpu.VMEM)
    return pl.pallas_call(
        join_kernel,
        out_shape=jax.ShapeDtypeStruct((rows, parts[0].shape[1]), parts[0].dtype),
        in_specs=[vmem] * len(parts),
        out_specs=vmem,
        compiler_params=pltpu.CompilerParams(vmem_limit_bytes=4 << 20),
        cost_estimate=pl.CostEstimate(flops=1 << 20, bytes_accessed=1 << 19, transcendentals=0),
        name="join",
    )(*parts)


def body(record, offsets, src_idx):
    c_dev = record.shape[0]
    n_win = offsets.shape[0]
    n_src = src_idx.shape[0]
    n_tm = lax.axis_size("tm")
    n_fibre = lax.axis_size("fibre")
    n_group = n_fibre // 2
    fibre = lax.axis_index("fibre")
    tm = lax.axis_index("tm")
    head, early = n_win * 3 // 4, n_win * 7 // 8
    scale = 1.0 / math.sqrt(n_win * n_tm * NB)
    tables = [jnp.asarray(t) for t in (half_tables(), taper_table(), smoothing())]
    ltab = jnp.asarray(lag_table())
    direct = n_group == 4 and n_tm == 4

    def trade(array, by):
        return lax.ppermute(array, "fibre", [(i, i ^ by) for i in range(n_fibre)])

    rec_a, middle, src_a, edge, rest, offs, sources, *tables = spectra_call(record, offsets, src_idx, tables, 0, early, head)
    far_a = trade(rec_a, 1)
    if direct:
        by_2a = trade(src_a, 4)
    halo = lax.ppermute(edge, "tm", [(i, i - 1) for i in range(1, n_tm)])
    cross = functools.partial(
        cross_call, n_src=n_src, n_win=n_win, early=early, c_dev=c_dev, scale=scale
    )
    late = (halo, middle, src_a)
    begun = []
    if direct:
        parts = [(0, 0, 0, head), (1, head, head, early)]
        begun = cross([src_a[None]], [rec_a, middle], [(0, 1, parts, None, (0, 0))], [1])
    rec_b, src_b, src = spectra_call(
        rest, offs, sources, tables, early, n_win - early, late=late, after=begun
    )
    far_b = trade(rec_b, 1)
    own = [(0, 0, 0, head), (1, head, head, n_win)]
    if direct:
        by_2 = join_call(by_2a, trade(src_b, 4))
        by_1 = trade(src, 2)
        by_3 = trade(by_2, 2)
        srcs = [part[None] for part in (src, by_1, by_2, by_3)]
        mine = functools.partial(cross, recs=[rec_a, rec_b, far_a], ltab=ltab)
        runs = [(0, 1, [(1, head, early, n_win)], (0, 0), None), (1, 1, own, None, None)]
        ours = functools.partial(cross, recs=[rec_a, rec_b], ltab=ltab)
        near_0, near_2 = ours([srcs[0], srcs[2]], runs=runs, outs=[[1], [1]], befores=begun)
        near_1 = ours(srcs[1:2], runs=[(0, 1, own, None, None)], outs=[[1]], after=[near_2])[0]
        swapped = [(2, 0, 0, head)]
        runs = [(0, 2, swapped, None, (0, 0)), (2, 1, swapped, None, (0, 2))]
        sums = mine(srcs[:3], runs=runs, outs=[3], after=[near_1])[0]
        swapped = [(3, head, head, n_win)]
        runs = [(0, 2, swapped, (0, 0), None), (2, 1, swapped, (0, 2), None)]
        theirs = functools.partial(cross, recs=[rec_a, rec_b, far_a, far_b], ltab=ltab)
        far = theirs(srcs[:3], runs=runs, outs=[[1, 1, 1]], befores=[sums])[0]
        runs = [(0, 1, [(2, 0, 0, head)] + swapped, None, None), (0, 1, own, None, None)]
        far, near = theirs(
            srcs[3:], runs=runs, outs=[["done", 1], ["done"] * 3 + [1]], done=[far, near_0, near_1, near_2]
        )
    else:
        ranks = [[2 * j + p for j in range(n_group)] for p in range(2)]
        srcs = [lax.all_gather(src, "fibre", axis=0, axis_index_groups=ranks)]
        runs = [(0, 1, own, None, None)]
        near = cross(srcs, [rec_a, rec_b], runs, [[1]], ltab=ltab)[0]
        far = cross(srcs, [far_a, far_b], runs, [[1]], ltab=ltab)[0]
    near, far = (r.reshape(n_group, n_src, c_dev, LAGS) for r in (near, far))

    def piece(lagged, owner):
        if direct:
            return lax.dynamic_index_in_dim(lagged, (fibre // 2) ^ owner, 0, keepdims=True)
        share = n_group // n_tm
        return lax.dynamic_slice_in_dim(lagged, owner * share, share, 0)

    keep = jnp.stack([piece(r, tm ^ k) for r in (near, far) for k in range(0, n_tm, 2)])
    give = jnp.stack([piece(r, tm ^ k) for r in (near, far) for k in range(1, n_tm, 2)])
    got = lax.ppermute(give, "tm", [(i, i ^ 1) for i in range(n_tm)])
    pairs = keep.astype(jnp.float32) + got.astype(jnp.float32)
    totals = []
    for side in range(2):
        total = None
        for k in range(n_tm // 2):
            mine = pairs[side * (n_tm // 2) + k]
            if side or k:
                routes = [
                    (i * n_tm + t, (i ^ side) * n_tm + (t ^ (2 * k)))
                    for i in range(n_fibre)
                    for t in range(n_tm)
                ]
                mine = lax.ppermute(mine.astype(jnp.bfloat16), ("fibre", "tm"), routes)
                mine = mine.astype(jnp.float32)
            total = mine if total is None else total + mine
        totals.append(total)
    even = fibre % 2 == 0
    near, far = totals
    out = jnp.stack([jnp.where(even, near, far), jnp.where(even, far, near)], axis=1)
    return out.reshape(-1, c_dev, LAGS)


def solution(mesh):
    return jax.shard_map(
        body,
        mesh=mesh,
        in_specs=(P("fibre", "tm"), P("tm"), P("fibre")),
        out_specs=P("tm", "fibre", None),
        check_vma=False,
    )
```

```python
import functools
import math

import jax
import jax.numpy as jnp
import numpy as np
from jax import lax
from jax.experimental import pallas as pl
from jax.experimental.pallas import tpu as pltpu
from jax.sharding import PartitionSpec as P

W = 2048
HOP = 1024
NB = 384
B0 = 20
SMOOTH = 64
LAGS = 256
LANE = 128
CUT = W + LANE
FOLD = W // 2
BINS = np.concatenate(
    [np.arange(0, 256, 2), np.arange(1, 256, 2), np.arange(256, NB, 2), np.arange(257, NB, 2)]
)


def taper_table():
    return (0.5 - 0.5 * np.cos(np.arange(W) * (2.0 * math.pi / W))).astype(np.float32)[None, :]


def half_tables():
    samples = np.arange(FOLD, dtype=np.int64)[:, None]

    def waves(bins):
        turns = (samples * (B0 + bins)[None, :] % W) * (2.0 * math.pi / W)
        return np.cos(turns), -np.sin(turns)

    even_cos, even_sin = waves(np.arange(0, NB, 2))
    odd_cos, odd_sin = waves(np.arange(1, NB, 2))
    cut = LANE
    columns = [
        even_cos[:, :cut], even_sin[:, :cut], even_cos[:, cut:], even_sin[:, cut:],
        odd_cos[:, :cut], odd_sin[:, :cut], odd_sin[:, cut:], odd_cos[:, cut:],
    ]
    return np.concatenate(columns, axis=1).astype(np.float32).astype(jnp.bfloat16)


def smoothing():
    rows = BINS[:, None]
    cols = BINS[None, :]
    first = np.clip(cols - SMOOTH // 2, 0, NB - SMOOTH)
    return np.where((rows >= first) & (rows < first + SMOOTH), 1.0 / SMOOTH, 0.0).astype(jnp.bfloat16)


def lag_table():
    shifts = np.arange(LAGS, dtype=np.int64) - LAGS // 2
    turns = ((B0 + BINS)[:, None] * shifts[None, :] % W) * (2.0 * math.pi / W)
    table = np.concatenate([np.cos(turns), -np.sin(turns)], axis=0)
    return table.astype(np.float32).astype(jnp.bfloat16)


def spectra_kernel(first, count, late, c_dev, n_src, n_after, *refs):
    if late:
        offs, sources, rest, halo, table_v, taper_v, smooth_v, before_r, before_s, *refs = refs
        out_r, out_s, out_all, *refs = refs[n_after:]
        sums, diffs, held, offs_v, sources_v, sems = refs
    else:
        offs, sources, rec, table, taper, smooth, *refs = refs
        out_r, out_mid, out_s, out_edge, out_rest, out_offs, out_sources, *refs = refs
        table_v, taper_v, smooth_v, *refs = refs
        sums, diffs, held, offs_v, sources_v, sems = refs
    width = (count + 2) * HOP
    copies = []

    def fetch(source, target):
        copy = pltpu.make_async_copy(source, target, sems.at[len(copies)])
        copy.start()
        copies.append(copy)

    fetch(offs, offs_v)
    fetch(sources, sources_v)
    inside = width - (W if late else 0)
    half = 0 if late else (count + 1) // 2
    if late:
        held[:, :inside] = rest[...]
        held[:, inside:] = halo[...]
    else:
        for start, stop in ((0, (half + 2) * HOP), ((half + 2) * HOP, inside)):
            fetch(rec.at[:, pl.ds(start, stop - start)], held.at[:, pl.ds(start, stop - start)])
            if not start:
                fetch(taper, taper_v)
    ready = len(copies)
    if not late:
        rows = FOLD // 4
        for at in range(0, FOLD, rows):
            fetch(table.at[pl.ds(at, rows)], table_v.at[pl.ds(at, rows)])
        fetch(smooth, smooth_v)
        fetch(rec.at[:, pl.ds(0, W)], out_edge)
        fetch(rec.at[:, pl.ds(count * HOP, out_rest.shape[1])], out_rest)
        fetch(offs, out_offs)
        fetch(sources, out_sources)
    for copy in copies[: ready - 1]:
        copy.wait()

    lanes = lax.broadcasted_iota(jnp.int32, (c_dev, LANE), 1)

    def cut(slot):
        start = slot * HOP + offs_v[first + slot]
        rest = start % LANE
        keep = lanes < LANE - rest
        shift = (LANE - rest) % LANE
        chunk = held[:, pl.ds(pl.multiple_of(start // LANE * LANE, LANE), CUT)].astype(jnp.float32)
        turned = [pltpu.roll(chunk[:, i * LANE : (i + 1) * LANE], shift, 1) for i in range(CUT // LANE)]
        row = pl.ds(pl.multiple_of(slot * c_dev, c_dev), c_dev)
        tiles = FOLD // LANE
        for i in range(tiles):
            lo = slice(i * LANE, (i + 1) * LANE)
            hi = slice(FOLD + i * LANE, FOLD + (i + 1) * LANE)
            near = jnp.where(keep, turned[i], turned[i + 1]) * taper_v[:, lo]
            far = jnp.where(keep, turned[tiles + i], turned[tiles + i + 1]) * taper_v[:, hi]
            sums[row, lo] = (near + far).astype(jnp.bfloat16)
            diffs[row, lo] = (near - far).astype(jnp.bfloat16)

    for slot in range(half):
        cut(slot)
    copies[ready - 1].wait()
    for slot in range(half, count):
        cut(slot)
    for copy in copies[ready:]:
        copy.wait()

    split = 3 * LANE
    even = jnp.dot(sums[...], table_v[:, :split], preferred_element_type=jnp.float32)
    odd = jnp.dot(diffs[...], table_v[:, split:], preferred_element_type=jnp.float32)
    left = lax.broadcasted_iota(jnp.int32, (1, LANE), 1) < LANE // 2
    mixed_even, mixed_odd = even[:, 2 * LANE :], odd[:, 2 * LANE :]
    real = [even[:, :LANE], odd[:, :LANE], jnp.where(left, mixed_even, mixed_odd)]
    swapped = pltpu.roll(jnp.where(left, mixed_odd, mixed_even), LANE // 2, 1)
    imag = [even[:, LANE : 2 * LANE], odd[:, LANE : 2 * LANE], swapped]
    power = jnp.concatenate([r * r + i * i for r, i in zip(real, imag)], axis=1).astype(jnp.bfloat16)
    smoothed = jnp.dot(power, smooth_v[...], preferred_element_type=jnp.float32)
    factor = lax.rsqrt(smoothed + 1e-05)
    parts = [value * factor[:, i % 3 * LANE : (i % 3 + 1) * LANE] for i, value in enumerate(real + imag)]
    white = jnp.concatenate([part.astype(jnp.bfloat16) for part in parts], axis=1)
    if late:
        at = before_r.shape[0]
        out_r[:at] = before_r[...]
        out_r[at:] = white
    else:
        at = out_r.shape[0]
        out_r[...] = white[:at]
        out_mid[...] = white[at:]
    rows = lax.broadcasted_iota(jnp.int32, (n_src * count, 1), 0)
    cols = lax.broadcasted_iota(jnp.int32, (n_src * count, count * c_dev), 1)
    wanted = jnp.zeros_like(rows)
    for s in range(n_src):
        wanted = jnp.where(rows // count == s, sources_v[s] % c_dev + (rows % count) * c_dev, wanted)
    picker = jnp.where(cols == wanted, 1.0, 0.0).astype(jnp.bfloat16)
    out_s[...] = jnp.dot(picker, white, preferred_element_type=jnp.float32).astype(jnp.bfloat16)
    if late:
        at = before_s.shape[0]
        out_all[:at] = before_s[...]
        out_all[at:] = out_s[...]


def spectra_call(record, offsets, src_idx, tables, first, count, head=None, late=None, after=()):
    c_dev = record.shape[0]
    n_src = src_idx.shape[0]
    vmem = pl.BlockSpec(memory_space=pltpu.VMEM)
    hbm = pl.BlockSpec(memory_space=pltpu.HBM)
    arrays = [offsets, src_idx, record]
    n_rest = record.shape[1] - count * HOP
    if late is None:
        arrays += tables
        arrays = [pltpu.with_memory_space_constraint(a, pltpu.HBM) for a in arrays]
    specs = [hbm if late is None else vmem] * len(arrays)
    rows = [head, count - head] if late is None else [count + late[1].shape[0] // c_dev]
    out_shape = [jax.ShapeDtypeStruct((n * c_dev, 2 * NB), jnp.bfloat16) for n in rows]
    out_shape.append(jax.ShapeDtypeStruct((n_src * count, 2 * NB), jnp.bfloat16))
    if late is None:
        out_shape += [jax.ShapeDtypeStruct((c_dev, n), record.dtype) for n in (W, n_rest)]
        out_shape += [jax.ShapeDtypeStruct(a.shape, a.dtype) for a in (offsets, src_idx)]
        out_shape += [jax.ShapeDtypeStruct(t.shape, t.dtype) for t in tables]
    else:
        halo, middle, sources = late
        arrays += [halo, *tables, middle, sources, *after]
        specs += [vmem] * 6 + [pl.BlockSpec(memory_space=pl.ANY)] * len(after)
        out_shape.append(jax.ShapeDtypeStruct((sources.shape[0] + n_src * count, 2 * NB), jnp.bfloat16))
    return pl.pallas_call(
        functools.partial(spectra_kernel, first, count, late is not None, c_dev, n_src, len(after)),
        out_shape=out_shape,
        in_specs=specs,
        out_specs=[vmem] * len(out_shape),
        scratch_shapes=[
            pltpu.VMEM((count * c_dev, FOLD), jnp.bfloat16),
            pltpu.VMEM((count * c_dev, FOLD), jnp.bfloat16),
            pltpu.VMEM((c_dev, (count + 2) * HOP), jnp.bfloat16),
            pltpu.SMEM(offsets.shape, jnp.int32),
            pltpu.SMEM(src_idx.shape, jnp.int32),
            pltpu.SemaphoreType.DMA((16,)),
        ],
        compiler_params=pltpu.CompilerParams(vmem_limit_bytes=24 << 20),
        cost_estimate=pl.CostEstimate(
            flops=int((1.5 + 0.1 * count) * 0.01e9), bytes_accessed=1 << 20, transcendentals=0
        ),
        name="spectra",
    )(*arrays)


def cross_kernel(runs, outs, counts, n_src, n_win, early, c_dev, scale, *refs):
    groups = []
    for count in counts:
        groups.append(refs[:count])
        refs = refs[count:]
    srcs, recs, befores, done, tables, _ = groups
    outputs, refs = refs[: len(outs)], refs[len(outs) :]
    wide = refs[0]
    span = n_src * n_win
    for k, src in enumerate(srcs):
        rows = slice(k * span, k * span + src.shape[1])
        real = src[0, :, :NB].astype(jnp.float32)
        imag = src[0, :, NB:].astype(jnp.float32)
        wide[rows, :NB] = real
        wide[rows, NB : 2 * NB] = real + imag
        wide[rows, 2 * NB :] = real - imag
    tiles = NB // LANE

    def run(step, first, wave, parts, before, target, offset):
        block = wave * n_src
        local = step // tiles * wave
        lo, hi, top = (
            pl.ds(pl.multiple_of(step % tiles * LANE + i * NB, LANE), LANE) for i in range(3)
        )
        src = wide.at[pl.ds(pl.multiple_of((first + local) * span, 8), wave * span)]

        def place(start, s):
            return pl.ds(pl.multiple_of(((start + local) * n_src + s) * c_dev, c_dev), c_dev)

        sums = [[jnp.zeros((c_dev, LANE), jnp.float32)] * 3 for _ in range(block)]
        for index, base, start, stop in parts:
            for w in range(start, stop):
                row = slice((w - base) * c_dev, (w - base + 1) * c_dev)
                rec_real = recs[index][row, lo].astype(jnp.float32)
                rec_imag = recs[index][row, hi].astype(jnp.float32)
                rec_both = rec_real + rec_imag
                for s in range(block):
                    at = s // n_src * span
                    if w < early:
                        at += s % n_src * early + w
                    else:
                        at += n_src * early + s % n_src * (n_win - early) + w - early
                    row = slice(at, at + 1)
                    both, plus, minus = sums[s]
                    sums[s] = [
                        both + src[row, lo] * rec_both,
                        plus + src[row, hi] * rec_real,
                        minus + src[row, top] * rec_imag,
                    ]
        for s in range(block):
            both, plus, minus = sums[s]
            real, imag = both - minus, both - plus
            if before is not None:
                real += befores[before[0]][place(before[1], s), lo]
                imag += befores[before[0]][place(before[1], s), hi]
            target[place(offset, s), lo] = real.astype(target.dtype)
            target[place(offset, s), hi] = imag.astype(target.dtype)

    lagged = 0
    for first, n_group, parts, before, place in runs:
        if place is None:
            target, offset = refs[1], lagged
            lagged += n_group
        else:
            target, offset = outputs[place[0]], place[1]
        wave = 8 // n_src if n_group * n_src % 8 == 0 and 8 % n_src == 0 else 1
        pl.loop(0, n_group // wave * tiles)(
            functools.partial(
                run, first=first, wave=wave, parts=parts, before=before, target=target, offset=offset
            )
        )

    if lagged:
        lags = jnp.dot(refs[1][...], tables[0][...], preferred_element_type=jnp.float32)
        lags = (lags * scale).astype(jnp.bfloat16)
        unit = n_src * c_dev
        start, done = 0, list(done)
        for out, pieces in zip(outputs, outs):
            at = 0
            for piece in pieces or ():
                if isinstance(piece, str):
                    part = done.pop(0)[...]
                else:
                    part = lags[start * unit : (start + piece) * unit]
                    start += piece
                out[at : at + part.shape[0], :] = part
                at += part.shape[0]


def cross_call(srcs, recs, runs, outs, n_src, n_win, early, c_dev, scale, befores=(), done=(), ltab=None, after=()):
    grid = srcs[0].shape[0]
    unit = n_src * c_dev
    whole = pl.BlockSpec(memory_space=pltpu.VMEM)
    lists = [srcs, recs, befores, done, () if ltab is None else (ltab,), after]
    arrays = [a for some in lists for a in some]
    specs = [whole] * (len(arrays) - len(after)) + [pl.BlockSpec(memory_space=pl.ANY)] * len(after)
    shapes, heights = [], [a.shape[0] for a in done]
    for out in outs:
        if isinstance(out, int):
            shapes.append(jax.ShapeDtypeStruct((out * unit, 2 * NB), jnp.float32))
        else:
            rows = sum(heights.pop(0) if isinstance(p, str) else p * unit for p in out)
            shapes.append(jax.ShapeDtypeStruct((grid * rows, LAGS), jnp.bfloat16))
    out_specs = [whole] * len(shapes)
    if grid > 1:
        specs[: len(srcs)] = [pl.BlockSpec((1,) + a.shape[1:], lambda g: (g, 0, 0)) for a in srcs]
        out_specs = [pl.BlockSpec((s.shape[0] // grid, s.shape[1]), lambda g: (g, 0)) for s in shapes]
    scratch = [pltpu.VMEM((len(srcs) * n_src * n_win, 3 * NB), jnp.float32)]
    lagged = sum(n for _, n, _, _, place in runs if place is None)
    if lagged:
        scratch.append(pltpu.VMEM((lagged * unit, 2 * NB), jnp.bfloat16))
    pairs = sum(n * n_src * sum(p[3] - p[2] for p in parts) for _, n, parts, _, _ in runs)
    kept = [None if isinstance(out, int) else out for out in outs]
    return pl.pallas_call(
        functools.partial(
            cross_kernel, runs, kept, [len(some) for some in lists], n_src, n_win, early, c_dev, scale
        ),
        grid=() if grid == 1 else (grid,),
        out_shape=shapes,
        in_specs=specs,
        out_specs=out_specs,
        scratch_shapes=scratch,
        compiler_params=pltpu.CompilerParams(vmem_limit_bytes=24 << 20),
        cost_estimate=pl.CostEstimate(
            flops=int((0.4 + grid * pairs * 0.008) * 0.02e9), bytes_accessed=1 << 20, transcendentals=0
        ),
        name="cross",
    )(*arrays)


def join_kernel(*refs):
    *parts, out = refs
    at = 0
    for part in parts:
        out[at : at + part.shape[0]] = part[...]
        at += part.shape[0]


def join_call(*parts):
    rows = sum(part.shape[0] for part in parts)
    vmem = pl.BlockSpec(memory_space=pltpu.VMEM)
    return pl.pallas_call(
        join_kernel,
        out_shape=jax.ShapeDtypeStruct((rows, parts[0].shape[1]), parts[0].dtype),
        in_specs=[vmem] * len(parts),
        out_specs=vmem,
        compiler_params=pltpu.CompilerParams(vmem_limit_bytes=4 << 20),
        cost_estimate=pl.CostEstimate(flops=1 << 20, bytes_accessed=1 << 19, transcendentals=0),
        name="join",
    )(*parts)


def body(record, offsets, src_idx):
    c_dev = record.shape[0]
    n_win = offsets.shape[0]
    n_src = src_idx.shape[0]
    n_tm = lax.axis_size("tm")
    n_fibre = lax.axis_size("fibre")
    n_group = n_fibre // 2
    fibre = lax.axis_index("fibre")
    tm = lax.axis_index("tm")
    head, early = n_win * 3 // 4, n_win * 7 // 8
    scale = 1.0 / math.sqrt(n_win * n_tm * NB)
    tables = [jnp.asarray(t) for t in (half_tables(), taper_table(), smoothing())]
    ltab = jnp.asarray(lag_table())
    direct = n_group == 4 and n_tm == 4

    def trade(array, by):
        return lax.ppermute(array, "fibre", [(i, i ^ by) for i in range(n_fibre)])

    rec_a, middle, src_a, edge, rest, offs, sources, *tables = spectra_call(record, offsets, src_idx, tables, 0, early, head)
    far_a = trade(rec_a, 1)
    if direct:
        by_2a = trade(src_a, 4)
    halo = lax.ppermute(edge, "tm", [(i, i - 1) for i in range(1, n_tm)])
    cross = functools.partial(
        cross_call, n_src=n_src, n_win=n_win, early=early, c_dev=c_dev, scale=scale
    )
    late = (halo, middle, src_a)
    begun = []
    if direct:
        parts = [(0, 0, 0, head), (1, head, head, early)]
        begun = cross([src_a[None]], [rec_a, middle], [(0, 1, parts, None, (0, 0))], [1])
    rec_b, src_b, src = spectra_call(
        rest, offs, sources, tables, early, n_win - early, late=late, after=begun
    )
    far_b = trade(rec_b, 1)
    own = [(0, 0, 0, head), (1, head, head, n_win)]
    if direct:
        by_2 = join_call(by_2a, trade(src_b, 4))
        by_1 = trade(src, 2)
        by_3 = trade(by_2, 2)
        srcs = [part[None] for part in (src, by_1, by_2, by_3)]
        mine = functools.partial(cross, recs=[rec_a, rec_b, far_a], ltab=ltab)
        runs = [(0, 1, [(1, head, early, n_win)], (0, 0), None), (1, 1, own, None, None)]
        ours = functools.partial(cross, recs=[rec_a, rec_b], ltab=ltab)
        near_0, near_2 = ours([srcs[0], srcs[2]], runs=runs, outs=[[1], [1]], befores=begun)
        near_1 = ours(srcs[1:2], runs=[(0, 1, own, None, None)], outs=[[1]], after=[near_2])[0]
        swapped = [(2, 0, 0, head)]
        runs = [(0, 2, swapped, None, (0, 0)), (2, 1, swapped, None, (0, 2))]
        sums = mine(srcs[:3], runs=runs, outs=[3], after=[near_1])[0]
        swapped = [(3, head, head, n_win)]
        runs = [(0, 2, swapped, (0, 0), None), (2, 1, swapped, (0, 2), None)]
        theirs = functools.partial(cross, recs=[rec_a, rec_b, far_a, far_b], ltab=ltab)
        far = theirs(srcs[:3], runs=runs, outs=[[1, 1, 1]], befores=[sums])[0]
        runs = [(0, 1, [(2, 0, 0, head)] + swapped, None, None), (0, 1, own, None, None)]
        far, near = theirs(
            srcs[3:], runs=runs, outs=[["done", 1], ["done"] * 3 + [1]], done=[far, near_0, near_1, near_2]
        )
    else:
        ranks = [[2 * j + p for j in range(n_group)] for p in range(2)]
        srcs = [lax.all_gather(src, "fibre", axis=0, axis_index_groups=ranks)]
        runs = [(0, 1, own, None, None)]
        near = cross(srcs, [rec_a, rec_b], runs, [[1]], ltab=ltab)[0]
        far = cross(srcs, [far_a, far_b], runs, [[1]], ltab=ltab)[0]
    near, far = (r.reshape(n_group, n_src, c_dev, LAGS) for r in (near, far))

    def piece(lagged, owner):
        if direct:
            return lax.dynamic_index_in_dim(lagged, (fibre // 2) ^ owner, 0, keepdims=True)
        share = n_group // n_tm
        return lax.dynamic_slice_in_dim(lagged, owner * share, share, 0)

    keep = jnp.stack([piece(r, tm ^ k) for r in (near, far) for k in range(0, n_tm, 2)])
    give = jnp.stack([piece(r, tm ^ k) for r in (near, far) for k in range(1, n_tm, 2)])
    got = lax.ppermute(give, "tm", [(i, i ^ 1) for i in range(n_tm)])
    pairs = keep.astype(jnp.float32) + got.astype(jnp.float32)
    totals = []
    for side in range(2):
        total = None
        for k in range(n_tm // 2):
            mine = pairs[side * (n_tm // 2) + k]
            if side or k:
                routes = [
                    (i * n_tm + t, (i ^ side) * n_tm + (t ^ (2 * k)))
                    for i in range(n_fibre)
                    for t in range(n_tm)
                ]
                mine = lax.ppermute(mine.astype(jnp.bfloat16), ("fibre", "tm"), routes)
                mine = mine.astype(jnp.float32)
            total = mine if total is None else total + mine
        totals.append(total)
    even = fibre % 2 == 0
    near, far = totals
    out = jnp.stack([jnp.where(even, near, far), jnp.where(even, far, near)], axis=1)
    return out.reshape(-1, c_dev, LAGS)


def solution(mesh):
    return jax.shard_map(
        body,
        mesh=mesh,
        in_specs=(P("fibre", "tm"), P("tm"), P("fibre")),
        out_specs=P("tm", "fibre", None),
        check_vma=False,
    )
```
